32 devices in a mesh: dp: 4 (over y, core), seq: 8 (over z, x).
Axes of the slice: x: 2, y: 2, z: 4, core: 2. Of those that a mesh axis runs over, the one named last changes fastest.
Arguments:
- stream_one: bfloat16 [8, 1024, 1024], P('dp', 'seq'), may hold values from -6 to 6
- stream_two: bfloat16 [8, 1024, 1024], P('dp', 'seq'), may hold values from -6 to 6
- slot_place: int32 [8, 4, 1024], P('dp', None, 'seq'), may hold values from 0 to 1535, as said below
- bucket_ids: int32 [8, 4, 1024], P('dp', None, 'seq'), may hold values from 0 to 23, as said below
- grad_one: bfloat16 [8, 1024, 1024], P('dp', 'seq'), may hold values from -6 to 6
- grad_two: bfloat16 [8, 1024, 1024], P('dp', 'seq'), may hold values from -6 to 6
- norm1_gain: bfloat16 [1024], P(('dp', 'seq')), may hold values from 0.5 to 1.5
- norm1_bias: bfloat16 [1024], P(('dp', 'seq')), may hold values from -1 to 1
- w_query_key: bfloat16 [1024, 1024], P(('dp', 'seq')), may hold values from -3 to 3
- w_value: bfloat16 [1024, 1024], P(('dp', 'seq')), may hold values from -0.1875 to 0.1875
- w_output: bfloat16 [1024, 1024], P(('dp', 'seq')), may hold values from -1.5 to 1.5
- norm2_gain: bfloat16 [1024], P(('dp', 'seq')), may hold values from 0.5 to 1.5
- norm2_bias: bfloat16 [1024], P(('dp', 'seq')), may hold values from -1 to 1
- w_inner: bfloat16 [1024, 4096], P(('dp', 'seq')), may hold values from -0.1875 to 0.1875
- inner_bias: bfloat16 [4096], P(('dp', 'seq')), may hold values from -3 to 3
- w_outer: bfloat16 [4096, 1024], P(('dp', 'seq')), may hold values from -0.1875 to 0.1875
- outer_bias: bfloat16 [1024], P(('dp', 'seq')), may hold values from -3 to 3
Outputs:
- out_one: float32 [8, 1024, 1024], P('dp', 'seq')
- out_two: float32 [8, 1024, 1024], P('dp', 'seq')
- back_one: float32 [8, 1024, 1024], P('dp', 'seq')
- back_two: float32 [8, 1024, 1024], P('dp', 'seq')
- grad_norm1_gain: float32 [1024], P(('dp', 'seq'))
- grad_norm1_bias: float32 [1024], P(('dp', 'seq'))
- grad_query_key: float32 [1024, 1024], P(('dp', 'seq'))
- grad_value: float32 [1024, 1024], P(('dp', 'seq'))
- grad_output: float32 [1024, 1024], P(('dp', 'seq'))
- grad_norm2_gain: float32 [1024], P(('dp', 'seq'))
- grad_norm2_bias: float32 [1024], P(('dp', 'seq'))
- grad_inner: float32 [1024, 4096], P(('dp', 'seq'))
- grad_inner_bias: float32 [4096], P(('dp', 'seq'))
- grad_outer: float32 [4096, 1024], P(('dp', 'seq'))
- grad_outer_bias: float32 [1024], P(('dp', 'seq'))
The draws below stay inside these ranges and needn't reach their ends.
Inputs may be any that keep to these rules, and one draw needn't show every extreme that they name: `slot_place`: within a sequence and round, the places of the 1024 tokens are distinct. Of the tokens k * 128 to (k + 1) * 128 - 1 of a sequence, at most 32 have places in any one block m * 192 to (m + 1) * 192 - 1 of a round, and some reach 32. `bucket_ids`: along a round's order of places, bucket ids never fall; a bucket takes whole spans of 64 places, its unused places being empty.
All inputs are finite; a program needn't handle non-finite values.
Results may differ from the reference program's by a relative error of at most 0.015.
Values may be sent and summed in bfloat16 or wider, within the bound.
No kernel may reach another device: no remote copies, remote signals or barrier semaphores. Data moves between devices by JAX's collectives and lax.ppermute only.
A program may use at most 320 MiB of HBM per device.

```python
import jax
import jax.numpy as jnp
from jax import lax

D = 1024
HEADS = 8
HEAD_DIM = 128
FF = 4096
SPAN = 64
ROUNDS = 4
SEQ_TOK = 128
LENGTH = 1024
SEQUENCES = 8
CAP = 32
N_SEQ = 8


def layout_round(key):
    groups = N_SEQ // 2
    offset_key, source_key, arrive_key, fill_key, join_key = jax.random.split(key, 5)
    offsets = jax.random.permutation(offset_key, N_SEQ)[:groups]
    order = jax.vmap(lambda sub: jax.random.permutation(sub, SEQ_TOK))(jax.random.split(source_key, N_SEQ))
    entry = jnp.argsort(order, axis=1).astype(jnp.int32)
    group = entry // CAP
    target = (jnp.arange(N_SEQ, dtype=jnp.int32)[:, None] + offsets[group]) % N_SEQ
    arrival = jax.vmap(lambda sub: jax.random.permutation(sub, SEQ_TOK))(jax.random.split(arrive_key, N_SEQ))
    live = arrival[target, entry]
    first_fill = jax.random.randint(fill_key, (N_SEQ,), SPAN // 4, 3 * SPAN // 4 + 1)
    fill_here = first_fill[target]
    local = jnp.where(live < fill_here, live, jnp.where(live < SPAN, live - fill_here + SPAN, live + SPAN))
    place = target * (3 * SPAN) + local
    joins = jax.random.randint(join_key, (N_SEQ,), 0, 2).at[0].set(0)
    fresh = jnp.ones((N_SEQ, 3), jnp.int32).at[:, 0].set(1 - joins).reshape(-1)
    span_index = jnp.arange(3 * N_SEQ, dtype=jnp.int32)
    numbers = lax.cummax(jnp.where(fresh > 0, span_index, 0), axis=0).reshape(N_SEQ, 3)
    bucket = numbers[target, local // SPAN]
    return (place.reshape(-1).astype(jnp.int32), bucket.reshape(-1).astype(jnp.int32))


def layout(key):
    keys = jax.random.split(key, SEQUENCES * ROUNDS)
    place, bucket = jax.vmap(layout_round)(keys)
    return (place.reshape(SEQUENCES, ROUNDS, LENGTH), bucket.reshape(SEQUENCES, ROUNDS, LENGTH))


def draw_slot_place(key, part):
    return layout(key)[0]


def draw_bucket_ids(key, part):
    return layout(key)[1]


def levels(key, dims, pieces, low, high):
    level, own = 1.0, jax.random.fold_in(key, 6)
    for dim, shards_of in pieces:
        steps = jnp.exp(jax.random.uniform(jax.random.fold_in(own, dim), (shards_of,), jnp.float32, low / len(pieces), high / len(pieces)))
        level = level * jnp.repeat(steps, dims[dim] // shards_of).reshape([-1 if axis == dim else 1 for axis in range(len(dims))])
    return level


def gaussian(key, shape, deviation, limit, pieces=(), held_as=jnp.bfloat16):
    array = deviation * jax.random.normal(key, shape, jnp.float32)
    if pieces:
        array = array * levels(key, shape, pieces, -0.22, 0.18)
    return jnp.clip(array, -limit, limit).astype(held_as)


def setup_inputs(seed: int = 0) -> dict:
    key_of = jax.random.split(jax.random.key(seed), 18)
    return {
        "stream_one": gaussian(key_of[0], (SEQUENCES, LENGTH, D), 1.0, 6.0, ((0, 4), (1, 8))),
        "stream_two": gaussian(key_of[1], (SEQUENCES, LENGTH, D), 1.0, 6.0, ((0, 4), (1, 8))),
        "slot_place": draw_slot_place(jax.random.fold_in(key_of[17], 71), 0),
        "bucket_ids": draw_bucket_ids(jax.random.fold_in(key_of[17], 71), 0),
        "grad_one": gaussian(key_of[4], (SEQUENCES, LENGTH, D), 1.0, 6.0, ((0, 4), (1, 8))),
        "grad_two": gaussian(key_of[5], (SEQUENCES, LENGTH, D), 1.0, 6.0, ((0, 4), (1, 8))),
        "norm1_gain": jnp.clip(1.0 + 0.1 * jax.random.normal(key_of[6], (D,), jnp.float32), 0.5, 1.5).astype(jnp.bfloat16),
        "norm1_bias": gaussian(key_of[7], (D,), 0.2, 1.0, ((0, 32),)),
        "w_query_key": gaussian(key_of[8], (D, D), (max(D // 256, 1)) ** -0.5, 3.0, ((0, 32),)),
        "w_value": gaussian(key_of[9], (D, D), D ** -0.5, 0.1875, ((0, 32),)),
        "w_output": gaussian(key_of[10], (D, D), (max(D // 64, 1)) ** -0.5, 1.5, ((0, 32),)),
        "norm2_gain": jnp.clip(1.0 + 0.1 * jax.random.normal(key_of[11], (D,), jnp.float32), 0.5, 1.5).astype(jnp.bfloat16),
        "norm2_bias": gaussian(key_of[12], (D,), 0.2, 1.0, ((0, 32),)),
        "w_inner": gaussian(key_of[13], (D, FF), D ** -0.5, 0.1875, ((0, 32),)),
        "inner_bias": gaussian(key_of[14], (FF,), 0.5, 3.0, ((0, 32),)),
        "w_outer": gaussian(key_of[15], (FF, D), (FF // 4) ** -0.5, 0.1875, ((0, 32),)),
        "outer_bias": gaussian(key_of[16], (D,), 0.5, 3.0, ((0, 32),)),
    }


@jax.custom_vjp
def low(v):
    return lax.optimization_barrier(v.astype(jnp.bfloat16)).astype(jnp.float32)

@jax.custom_vjp
def low_back(v):
    return v

def low_keep(v):
    return (low(v), None)

def low_pass(kept, grad):
    return (grad,)

def back_keep(v):
    return (v, None)

def back_low(kept, grad):
    return (low(grad),)
low.defvjp(low_keep, low_pass)
low_back.defvjp(back_keep, back_low)

def matmul(left, right):
    return jnp.dot(left, right, precision=lax.Precision.HIGHEST, preferred_element_type=jnp.float32)

def layer_norm(value, gain, bias):
    row_mean = lax.optimization_barrier(jnp.mean(value, -1, keepdims=True))
    centred = value - row_mean
    variance = lax.optimization_barrier(jnp.mean(centred * centred, -1, keepdims=True))
    return centred * lax.rsqrt(variance + 1e-05) * gain + bias

def round_attention(qkv_round, places, buckets):
    slot_count = 3 * LENGTH // 2
    block_count = slot_count // SPAN
    filled = jnp.zeros((slot_count, 2 * D), jnp.float32).at[places].set(qkv_round)
    tags = jnp.zeros((slot_count,), jnp.int32).at[places].set(buckets + 1)
    query_heads = filled[:, :D].reshape(slot_count, HEADS, HEAD_DIM)
    value_heads = filled[:, D:].reshape(slot_count, HEADS, HEAD_DIM)
    unit = query_heads * lax.rsqrt(lax.optimization_barrier(jnp.mean(query_heads * query_heads, -1, keepdims=True)) + 1e-06)
    unit = low(unit)
    query_blocks = query_heads.reshape(block_count, SPAN, HEADS, HEAD_DIM)
    key_blocks = unit.reshape(block_count, SPAN, HEADS, HEAD_DIM)
    value_blocks = value_heads.reshape(block_count, SPAN, HEADS, HEAD_DIM)
    tag_blocks = tags.reshape(block_count, SPAN)
    key_window = jnp.concatenate([jnp.concatenate([jnp.zeros_like(key_blocks[:1]), key_blocks[:-1]], 0), key_blocks], 1)
    value_window = jnp.concatenate([jnp.concatenate([jnp.zeros_like(value_blocks[:1]), value_blocks[:-1]], 0), value_blocks], 1)
    tag_window = jnp.concatenate([jnp.concatenate([jnp.zeros_like(tag_blocks[:1]), tag_blocks[:-1]], 0), tag_blocks], 1)
    scores = jnp.einsum('cqhd,ckhd->chqk', query_blocks, key_window, precision=lax.Precision.HIGHEST) / HEAD_DIM
    scores = low_back(scores)
    allowed = (tag_window[:, None, None, :] > 0) & (tag_blocks[:, None, :, None] == tag_window[:, None, None, :])
    scores = jnp.where(allowed, scores, -1000000000.0)
    own_place = jnp.arange(2 * SPAN)[None, :] == jnp.arange(SPAN)[:, None] + SPAN
    scores = jnp.where(own_place, scores - 100000.0, scores)
    row_max = lax.optimization_barrier(jnp.max(scores, -1, keepdims=True))
    exponent = jnp.exp(scores - row_max)
    row_sum = lax.optimization_barrier(jnp.sum(exponent, -1, keepdims=True))
    probability = low(exponent / row_sum)
    result = jnp.einsum('chqk,ckhd->cqhd', probability, value_window, precision=lax.Precision.HIGHEST)
    result = low_back(low(result.reshape(slot_count, D)))
    spread = (row_max + jnp.log(row_sum))[..., 0]
    spread = jnp.transpose(spread, (0, 2, 1)).reshape(slot_count, HEADS)
    return (result[places], spread[places])

def sequence_forward(params, first, second, places, buckets):
    gain_one, bias_one, w_qk, w_val, w_out, gain_two, bias_two, w_in, b_in, w_up, b_up = params
    hidden = low(layer_norm(second, gain_one, bias_one))
    projected = low_back(jnp.concatenate([matmul(hidden, w_qk), matmul(hidden, w_val)], 1))
    results = []
    spreads = []
    for round_idx in range(ROUNDS):
        result, spread = jax.checkpoint(round_attention)(low(low_back(projected)), places[round_idx], buckets[round_idx])
        results.append(result)
        spreads.append(spread)
    results = jnp.stack(results, 0)
    spreads = jnp.stack(spreads, 0)
    mix_weights = jax.nn.softmax(spreads, axis=0)
    mixed = lax.optimization_barrier(jnp.sum(mix_weights[..., None] * results.reshape(ROUNDS, LENGTH, HEADS, HEAD_DIM), 0)).reshape(LENGTH, D)
    attended = low_back(matmul(low(mixed), w_out))
    out_one = first + attended
    normed_two = low(layer_norm(out_one, gain_two, bias_two))
    pre_act = low_back(matmul(normed_two, w_in) + b_in)
    activated = low(jax.nn.gelu(pre_act))
    out_two = second + matmul(activated, w_up) + b_up
    return (out_one, out_two)

def reference(stream_one, stream_two, slot_place, bucket_ids, grad_one, grad_two, norm1_gain, norm1_bias, w_query_key, w_value, w_output, norm2_gain, norm2_bias, w_inner, inner_bias, w_outer, outer_bias):
    params = tuple((item.astype(jnp.float32) for item in (norm1_gain, norm1_bias, w_query_key, w_value, w_output, norm2_gain, norm2_bias, w_inner, inner_bias, w_outer, outer_bias)))

    def step(totals, items):
        first, second, places, buckets, cot_one, cot_two = items

        def forward(weights, first_in, second_in):
            return sequence_forward(weights, first_in, second_in, places, buckets)
        outputs, pullback = jax.vjp(forward, params, first.astype(jnp.float32), second.astype(jnp.float32))
        d_params, d_first, d_second = pullback((cot_one.astype(jnp.float32), cot_two.astype(jnp.float32)))
        totals = jax.tree.map(lambda total_grad, new_grad: total_grad + new_grad, totals, d_params)
        return (totals, (outputs[0], outputs[1], d_first, d_second))
    zero_grads = jax.tree.map(jnp.zeros_like, params)
    totals, stacked = lax.scan(step, zero_grads, (stream_one, stream_two, slot_place, bucket_ids, grad_one, grad_two))
    return (stacked[0], stacked[1], stacked[2], stacked[3], totals[0], totals[1], totals[2], totals[3], totals[4], totals[5], totals[6], totals[7], totals[8], totals[9], totals[10])
```

```python
import functools

import jax
import jax.numpy as jnp
from jax import lax
from jax.experimental import pallas as pl
from jax.experimental.pallas import tpu as pltpu
from jax.sharding import Mesh, PartitionSpec as P

HEADS = 8
HEAD_DIM = 128
SPAN = 64
GROUP = 3 * SPAN
WINDOW = GROUP + SPAN
F32 = jnp.float32
BF16 = jnp.bfloat16
CORE_SWAP = [(0, 1), (1, 0)]


def matmul(left, right):
    return jnp.dot(left, right, preferred_element_type=F32)


def matmul_left(left, right):
    return lax.dot_general(left, right, (((0,), (0,)), ((), ())), preferred_element_type=F32)


def matmul_right(left, right):
    return lax.dot_general(left, right, (((1,), (1,)), ((), ())), preferred_element_type=F32)


def norm_parts(value, gain, bias):
    row_mean = jnp.mean(value, -1, keepdims=True)
    centred = value - row_mean
    inv_scale = lax.rsqrt(jnp.mean(centred * centred, -1, keepdims=True) + 1e-05)
    normal = centred * inv_scale
    return (normal * gain + bias, normal, inv_scale)


def norm_back(cotangent, normal, inv_scale, gain):
    d_normal = cotangent * gain
    d_input = inv_scale * (
        d_normal
        - jnp.mean(d_normal, -1, keepdims=True)
        - normal * jnp.mean(d_normal * normal, -1, keepdims=True)
    )
    return (d_input, jnp.sum(cotangent * normal, 0), jnp.sum(cotangent, 0))


def swap(block):
    return lax.ppermute(block, "core", CORE_SWAP)


def pick(block, position, axis):
    return lax.dynamic_index_in_dim(block, position, axis, keepdims=False)


def exchange(block, axis, bit):
    size = lax.axis_size(axis)
    return lax.ppermute(block, axis, [(i, i ^ bit) for i in range(size)])


def half_steps(axes):
    steps = []
    for axis in axes:
        bit = lax.axis_size(axis) // 2
        while bit:
            steps.append((axis, bit))
            bit //= 2
    return steps


def gather_steps(block, axes):
    out = block[None]
    for axis, bit in reversed(half_steps(axes)):
        other = exchange(out, axis, bit)
        upper = (lax.axis_index(axis) // bit) % 2 == 1
        out = jnp.where(upper, jnp.concatenate([other, out], 0), jnp.concatenate([out, other], 0))
    return out


def scatter_steps(total, axes, sent_as):
    for axis, bit in half_steps(axes):
        half = total.reshape((2, total.shape[0] // 2) + total.shape[1:])
        mine = (lax.axis_index(axis) // bit) % 2
        sent = exchange(pick(half, 1 - mine, 0).astype(sent_as), axis, bit)
        total = pick(half, mine, 0) + sent.astype(F32)
    return total[0]


def all_to_all(block):
    return lax.all_to_all(block, "seq", split_axis=0, concat_axis=0, tiled=True)


def group_routes(count):
    size = lax.axis_size("seq")
    return [
        [(i, i // count * count + (i % count + step) % count) for i in range(size)]
        for step in range(1, count)
    ]


def group_sum(value, count):
    total = value
    for route in group_routes(count):
        total = total + lax.ppermute(value, "seq", route)
    return total


def group_max(value, count):
    total = value
    for route in group_routes(count):
        total = jnp.maximum(total, lax.ppermute(value, "seq", route))
    return total


def span_bias():
    query = jnp.arange(GROUP)[:, None]
    key = jnp.arange(WINDOW)[None, :]
    reach = key // SPAN - query // SPAN
    bias = jnp.where((reach == 0) | (reach == 1), 0.0, -1e9)
    return jnp.where(key == query + SPAN, -1e5, bias).astype(F32)


def split_three(value):
    high = value.astype(BF16).astype(F32)
    rest = value - high
    middle = rest.astype(BF16).astype(F32)
    return high, middle, rest - middle


def in_lanes(columns, rows):
    lane = lax.broadcasted_iota(jnp.int32, (rows, 128), 1)
    out = jnp.zeros((rows, 128), F32)
    for k, column in enumerate(columns):
        out = jnp.where(lane == k, column, out)
    return out


def one_hot_rows(place_row, base, rows, tokens):
    slot = lax.broadcasted_iota(jnp.int32, (rows, tokens), 0) + base
    return jnp.where(slot == place_row, 1.0, 0.0).astype(BF16)


def one_hot_columns(place_column, rows, slots):
    slot = lax.broadcasted_iota(jnp.int32, (rows, slots), 1)
    return jnp.where(slot == place_column, 1.0, 0.0).astype(BF16)


def tile_rows(tokens):
    if tokens <= 1024:
        return 3 * tokens // 2 // 2, tokens // 2
    return GROUP, 128


def head_scores(query, keys, bias, same):
    raw = matmul_right(query, keys) * (1.0 / HEAD_DIM)
    return jnp.where(same, raw + bias, -1e9)


def forward_kernel(
    heads, qv_ref, row_ref, column_ref, key_tag_ref, query_tag_ref, bias_ref,
    out_ref, spread_ref, placed_ref, slot_spread_ref, result_ref
):
    tokens = qv_ref.shape[0]
    slots = placed_ref.shape[1] - SPAN
    width = heads * HEAD_DIM
    place_rows, token_rows = tile_rows(tokens)
    placed_ref[0, 0:SPAN] = jnp.zeros((SPAN, 3 * width), BF16)

    def place(step, carry):
        base = pl.multiple_of(step * place_rows, place_rows)
        hot = one_hot_rows(row_ref[0], base, place_rows, tokens)
        rows = matmul(hot, qv_ref[...])
        where = pl.ds(pl.multiple_of(base + SPAN, SPAN), place_rows)
        placed_ref[0, where, 0 : 2 * width] = rows.astype(BF16)
        for head in range(heads):
            query = rows[:, head * HEAD_DIM : (head + 1) * HEAD_DIM]
            scale = lax.rsqrt(jnp.mean(query * query, -1, keepdims=True) + 1e-06)
            first = 2 * width + head * HEAD_DIM
            placed_ref[0, where, first : first + HEAD_DIM] = (query * scale).astype(BF16)
        return carry

    lax.fori_loop(0, slots // place_rows, place, 0)

    def attend(group, carry):
        base = pl.multiple_of(group * GROUP, GROUP)
        own = pl.ds(pl.multiple_of(base + SPAN, SPAN), GROUP)
        window = pl.ds(base, WINDOW)
        same = query_tag_ref[0, pl.ds(base, GROUP), :] == key_tag_ref[0, group]
        bias = bias_ref[...]
        spreads = []
        for head in range(heads):
            lanes = slice(head * HEAD_DIM, (head + 1) * HEAD_DIM)
            query = placed_ref[0, own, lanes]
            keys = placed_ref[0, window, 2 * width + head * HEAD_DIM : 2 * width + (head + 1) * HEAD_DIM]
            values = placed_ref[0, window, width + head * HEAD_DIM : width + (head + 1) * HEAD_DIM]
            scores = head_scores(query, keys, bias, same)
            row_max = jnp.max(scores, -1, keepdims=True)
            exponent = jnp.exp(scores - row_max)
            row_sum = jnp.sum(exponent, -1, keepdims=True)
            probability = (exponent * (1.0 / row_sum)).astype(BF16)
            result_ref[pl.ds(base, GROUP), lanes] = matmul(probability, values).astype(BF16)
            spreads.append(row_max + jnp.log(row_sum))
        query_tag = query_tag_ref[0, pl.ds(base, GROUP), :]
        slot_spread_ref[0, pl.ds(base, GROUP), :] = in_lanes(spreads + [query_tag], GROUP)
        pieces = [split_three(spread) for spread in spreads]
        packed = in_lanes([piece[k] for k in range(3) for piece in pieces], GROUP)
        result_ref[pl.ds(base, GROUP), width : width + 128] = packed.astype(BF16)
        return carry

    lax.fori_loop(0, slots // GROUP, attend, 0)

    def read_back(step, carry):
        where = pl.ds(pl.multiple_of(step * token_rows, token_rows), token_rows)
        hot = one_hot_columns(column_ref[0, where, :], token_rows, slots)
        rows = matmul(hot, result_ref[...])
        out_ref[0, where, :] = rows[:, :width].astype(BF16)
        packed = rows[:, width:]
        spread_ref[0, where, :] = (
            packed[:, 0:heads] + packed[:, heads : 2 * heads] + packed[:, 2 * heads : 3 * heads]
        )
        return carry

    lax.fori_loop(0, tokens // token_rows, read_back, 0)


def backward_kernel(
    heads, grad_ref, placed_ref, slot_spread_ref, row_ref, column_ref, key_tag_ref,
    bias_ref, total_ref, slot_grad_ref, d_query_ref, d_key_ref, d_value_ref, d_place_ref
):
    tokens = grad_ref.shape[1]
    slots = placed_ref.shape[1] - SPAN
    width = heads * HEAD_DIM
    place_rows, token_rows = tile_rows(tokens)

    @pl.when(pl.program_id(0) == 0)
    def _():
        total_ref[...] = jnp.zeros(total_ref.shape, F32)

    d_key_ref[...] = jnp.zeros(d_key_ref.shape, F32)
    d_value_ref[...] = jnp.zeros(d_value_ref.shape, F32)

    def place(step, carry):
        base = pl.multiple_of(step * place_rows, place_rows)
        hot = one_hot_rows(row_ref[0], base, place_rows, tokens)
        slot_grad_ref[pl.ds(base, place_rows), :] = matmul(hot, grad_ref[0]).astype(BF16)
        return carry

    lax.fori_loop(0, slots // place_rows, place, 0)

    def attend(group, carry):
        base = pl.multiple_of(group * GROUP, GROUP)
        here = pl.ds(base, GROUP)
        own = pl.ds(pl.multiple_of(base + SPAN, SPAN), GROUP)
        window = pl.ds(base, WINDOW)
        same = slot_spread_ref[0, here, heads : heads + 1] == key_tag_ref[0, group]
        bias = bias_ref[...]
        packed = slot_grad_ref[here, width : width + 128].astype(F32)
        for head in range(heads):
            lanes = slice(head * HEAD_DIM, (head + 1) * HEAD_DIM)
            query = placed_ref[0, own, lanes]
            keys = placed_ref[0, window, 2 * width + head * HEAD_DIM : 2 * width + (head + 1) * HEAD_DIM]
            values = placed_ref[0, window, width + head * HEAD_DIM : width + (head + 1) * HEAD_DIM]
            d_out = slot_grad_ref[here, lanes]
            d_spread = (
                packed[:, head : head + 1]
                + packed[:, heads + head : heads + head + 1]
                + packed[:, 2 * heads + head : 2 * heads + head + 1]
            )
            scores = head_scores(query, keys, bias, same)
            probability = jnp.exp(scores - slot_spread_ref[0, here, head : head + 1])
            d_probs = matmul_right(d_out, values)
            row_dot = jnp.sum(probability * d_probs, -1, keepdims=True)
            d_scores = (probability * (d_probs + (d_spread - row_dot))).astype(BF16)
            d_query_ref[here, lanes] = matmul(d_scores, keys) * (1.0 / HEAD_DIM)
            d_key_ref[window, lanes] += matmul_left(d_scores, query)
            d_value_ref[window, lanes] += matmul_left(probability.astype(BF16), d_out)
        return carry

    lax.fori_loop(0, slots // GROUP, attend, 0)

    def finish(group, carry):
        base = pl.multiple_of(group * GROUP, GROUP)
        here = pl.ds(base, GROUP)
        own = pl.ds(pl.multiple_of(base + SPAN, SPAN), GROUP)
        for head in range(heads):
            lanes = slice(head * HEAD_DIM, (head + 1) * HEAD_DIM)
            query = placed_ref[0, own, lanes].astype(F32)
            d_unit = d_key_ref[own, lanes] * (1.0 / HEAD_DIM)
            scale = lax.rsqrt(jnp.mean(query * query, -1, keepdims=True) + 1e-06)
            inner = jnp.mean(d_unit * query, -1, keepdims=True)
            d_query = d_query_ref[here, lanes] + scale * d_unit - query * (scale * scale * scale * inner)
            d_place_ref[here, lanes] = d_query.astype(BF16)
        d_place_ref[here, width : 2 * width] = d_value_ref[own, :].astype(BF16)
        return carry

    lax.fori_loop(0, slots // GROUP, finish, 0)

    def read_back(step, carry):
        where = pl.ds(pl.multiple_of(step * token_rows, token_rows), token_rows)
        hot = one_hot_columns(column_ref[0, where, :], token_rows, slots)
        total_ref[where, :] += matmul(hot, d_place_ref[...])
        return carry

    lax.fori_loop(0, tokens // token_rows, read_back, 0)


def per_round(shape, buffers):
    rest = (0,) * (len(shape) - 1)
    return pl.BlockSpec((1,) + shape[1:], lambda r: (r,) + rest, pipeline_mode=pl.Buffered(buffers))


def whole(shape):
    return pl.BlockSpec(shape, lambda r: (0,) * len(shape), pipeline_mode=pl.Buffered(1))


def attention_forward(qv, places, tags):
    row, column, key_tag, query_tag = places[0], places[1], tags[0], tags[1]
    rounds, _, tokens = row.shape
    slots = query_tag.shape[1]
    width = qv.shape[1] // 2
    heads = width // HEAD_DIM
    buffers = min(2, rounds)
    bias = span_bias()
    outs = [
        jax.ShapeDtypeStruct((rounds, tokens, width), BF16),
        jax.ShapeDtypeStruct((rounds, tokens, heads), F32),
        jax.ShapeDtypeStruct((rounds, slots + SPAN, 3 * width), BF16),
        jax.ShapeDtypeStruct((rounds, slots, 128), F32),
    ]
    flops = rounds * slots * (2 * tokens * (3 * width + 128) + 4 * width * WINDOW)
    return pl.pallas_call(
        functools.partial(forward_kernel, heads),
        grid=(rounds,),
        in_specs=[whole(qv.shape)]
        + [per_round(x.shape, buffers) for x in (row, column, key_tag, query_tag)]
        + [whole(bias.shape)],
        out_specs=[per_round(x.shape, buffers) for x in outs],
        out_shape=outs,
        scratch_shapes=[pltpu.VMEM((slots, width + 128), BF16)],
        compiler_params=pltpu.CompilerParams(vmem_limit_bytes=56 * 1024 * 1024),
        cost_estimate=pl.CostEstimate(flops=flops, bytes_accessed=20 << 20, transcendentals=0),
    )(qv, row, column, key_tag, query_tag, bias)


def attention_backward(grads, placed, slot_spread, places, tags):
    row, column, key_tag = places[0], places[1], tags
    rounds, _, tokens = row.shape
    slots = placed.shape[1] - SPAN
    width = placed.shape[2] // 3
    heads = width // HEAD_DIM
    buffers = min(2, rounds)
    bias = span_bias()
    flops = rounds * slots * (2 * tokens * (3 * width + 128) + 10 * width * WINDOW)
    return pl.pallas_call(
        functools.partial(backward_kernel, heads),
        grid=(rounds,),
        in_specs=[
            per_round(x.shape, buffers)
            for x in (grads, placed, slot_spread, row, column, key_tag)
        ]
        + [whole(bias.shape)],
        out_specs=whole((tokens, 2 * width)),
        out_shape=jax.ShapeDtypeStruct((tokens, 2 * width), F32),
        scratch_shapes=[
            pltpu.VMEM((slots, width + 128), BF16),
            pltpu.VMEM((slots, width), F32),
            pltpu.VMEM((slots + SPAN, width), F32),
            pltpu.VMEM((slots + SPAN, width), F32),
            pltpu.VMEM((slots, 2 * width), BF16),
        ],
        compiler_params=pltpu.CompilerParams(vmem_limit_bytes=56 * 1024 * 1024),
        cost_estimate=pl.CostEstimate(flops=flops, bytes_accessed=20 << 20, transcendentals=0),
    )(grads, placed, slot_spread, row, column, key_tag, bias)


def local(
    stream_one,
    stream_two,
    slot_place,
    bucket_ids,
    grad_one,
    grad_two,
    norm1_gain,
    norm1_bias,
    w_query_key,
    w_value,
    w_output,
    norm2_gain,
    norm2_bias,
    w_inner,
    inner_bias,
    w_outer,
    outer_bias,
):
    chips, devices = lax.axis_size("chip"), lax.axis_size("seq")
    batch, tok, features = stream_one.shape
    rounds = slot_place.shape[1]
    sequences = 2 * batch
    tokens = devices * tok
    slots = 3 * tokens // 2
    own_rows = batch * tok
    rows = sequences * tok
    width = features // (2 * chips)
    heads = width // HEAD_DIM
    hidden_units = w_inner.shape[1]
    units = sequences * chips
    sharing = devices // units
    own_rounds = rounds // sharing
    shard = w_query_key.shape[0]
    core = lax.axis_index("core")
    place = ("chip", "seq")
    every = ("chip", "core", "seq")

    def by_core(own, other):
        return jnp.where(core == 0, jnp.stack([own, other]), jnp.stack([other, own]))

    small = jnp.stack([norm1_gain, norm1_bias, norm2_gain, norm2_bias, outer_bias])
    small = jnp.swapaxes(gather_steps(small, every), 0, 1).reshape(5, features).astype(F32)
    gain_one, bias_one, gain_two, bias_two, full_outer_bias = [small[k] for k in range(5)]
    half_inner_bias = gather_steps(inner_bias, place).reshape(-1).astype(F32)

    def column_halves(weight, outer):
        split = weight.reshape(weight.shape[0], outer, 2, -1)
        return pick(split, core, 2), pick(split, 1 - core, 2)

    key_own, key_other = column_halves(w_query_key, chips)
    value_own, value_other = column_halves(w_value, chips)
    joined_own = jnp.concatenate([key_own, value_own], 2).reshape(shard, -1)
    joined_other = jnp.concatenate([key_other, value_other], 2).reshape(shard, -1)
    joined = gather_steps(by_core(joined_own, swap(joined_other)), place)
    joined = jnp.swapaxes(joined.reshape(chips, devices, 2, shard, -1), 1, 2).reshape(features, -1)

    inner_own, inner_other = column_halves(w_inner, chips)
    inner_both = by_core(inner_own.reshape(shard, -1), swap(inner_other.reshape(shard, -1)))
    full_inner = lax.all_gather(inner_both, place, axis=0, tiled=False)
    full_inner = jnp.swapaxes(
        full_inner.reshape(chips, devices, 2, shard, -1), 1, 2
    ).reshape(features, -1)
    full_output = lax.all_gather(w_output, place, axis=0, tiled=True)
    full_outer = lax.all_gather(w_outer, place, axis=0, tiled=True)

    meta = jnp.stack([slot_place, bucket_ids + 1], 1)
    meta = jnp.concatenate([meta, swap(meta)], 0)
    meta = meta.reshape(sequences, 1, 2, sharing, own_rounds, tok)
    meta = jnp.swapaxes(jnp.broadcast_to(meta, (sequences, chips) + meta.shape[2:]), 2, 3)
    meta = all_to_all(meta.reshape(devices, 2, own_rounds, tok))
    meta = jnp.moveaxis(meta, 0, 2).reshape(2, own_rounds, tokens)
    token_place, token_tag = meta[0], meta[1]
    found = token_place[:, :, None] == jnp.arange(slots)[None, None, :]
    slot_tag = jnp.sum(jnp.where(found, token_tag[:, :, None], 0), 1).astype(F32)
    before = jnp.concatenate([jnp.zeros((own_rounds, SPAN), F32), slot_tag], 1)
    key_tag = jnp.stack(
        [before[:, first : first + WINDOW] for first in range(0, slots, GROUP)], 1
    )[:, :, None, :]
    places = (token_place[:, None, :], token_place[:, :, None])
    tags = (key_tag, slot_tag[:, :, None])

    stream_a = stream_one.astype(F32).reshape(own_rows, features)
    stream_b = stream_two.astype(F32).reshape(own_rows, features)
    normed_one, unit_one, scale_one = norm_parts(stream_b, gain_one, bias_one)
    hidden = normed_one.astype(BF16)
    hidden = jnp.concatenate([hidden, swap(hidden)], 0)
    projected = matmul(hidden, joined).astype(BF16)

    def to_attention(value):
        value = jnp.swapaxes(value.reshape(sequences, tok, chips, -1), 1, 2)
        value = jnp.broadcast_to(value[:, :, None], value.shape[:2] + (sharing,) + value.shape[2:])
        return all_to_all(value.reshape(devices, tok, -1)).reshape(tokens, -1)

    def from_attention(value):
        value = all_to_all(value.reshape(devices, tok, -1))
        value = value.reshape(sequences, chips, sharing, tok, -1)[:, :, 0]
        return jnp.swapaxes(value, 1, 2).reshape(rows, -1)

    round_heads, round_spread, placed, slot_spread = attention_forward(
        to_attention(projected), places, tags
    )
    top = group_max(jnp.max(round_spread, 0), sharing)
    weight = jnp.exp(round_spread - top)
    mix_weights = weight / group_sum(jnp.sum(weight, 0), sharing)
    round_heads = round_heads.reshape(own_rounds, tokens, heads, HEAD_DIM)
    mixed = group_sum(jnp.sum(mix_weights[..., None] * round_heads, 0), sharing)
    mixed = from_attention(mixed.reshape(tokens, width).astype(BF16))

    def core_sum(value):
        return value[:own_rows] + swap(value[own_rows:])

    out_one = stream_a + core_sum(matmul(mixed, full_output))
    normed_two, unit_two, scale_two = norm_parts(out_one, gain_two, bias_two)
    inner_low = normed_two.astype(BF16)
    inner_low = jnp.concatenate([inner_low, swap(inner_low)], 0)
    pre_act = matmul(inner_low, full_inner) + half_inner_bias
    activated, gelu_pull = jax.vjp(jax.nn.gelu, pre_act)
    act_low = activated.astype(BF16)
    out_two = stream_b + core_sum(matmul(act_low, full_outer)) + full_outer_bias

    cot_own = grad_two.reshape(own_rows, features)
    cot_two = jnp.concatenate([cot_own, swap(cot_own)], 0)
    grad_outer = matmul_left(act_low, cot_two)
    d_act = matmul_right(cot_two, full_outer)
    d_pre = gelu_pull(d_act)[0].astype(BF16)
    grad_inner = matmul_left(inner_low, d_pre)
    d_normed_two = core_sum(matmul_right(d_pre, full_inner))
    d_from_two, grad_gain_two, grad_bias_two = norm_back(
        d_normed_two, unit_two, scale_two, gain_two
    )
    back_one = grad_one.astype(F32).reshape(own_rows, features) + d_from_two
    grad_outer = lax.psum_scatter(grad_outer.astype(BF16), place, scatter_dimension=0, tiled=True)
    grad_inner = jnp.swapaxes(
        grad_inner.astype(BF16).reshape(chips, 2, devices, shard, -1), 1, 2
    ).reshape(chips * devices, 2 * shard, -1)
    grad_inner = lax.psum_scatter(grad_inner, place, scatter_dimension=0, tiled=True)
    grad_inner = grad_inner.reshape(2, shard, -1).astype(F32)
    grad_inner_bias = scatter_steps(
        jnp.sum(d_pre.astype(F32), 0).reshape(chips * devices, -1), place, F32
    )

    def join_columns(pieces, outer):
        own, other = pick(pieces, core, 0), swap(pick(pieces, 1 - core, 0))
        both = by_core(own.reshape(shard, outer, -1), other.reshape(shard, outer, -1))
        return jnp.moveaxis(both, 0, 2)

    grad_inner = join_columns(grad_inner, chips).reshape(shard, hidden_units)

    d_attended = back_one.astype(BF16)
    d_attended = jnp.concatenate([d_attended, swap(d_attended)], 0)
    grad_output = matmul_left(mixed, d_attended).astype(BF16)
    grad_output = lax.psum_scatter(grad_output, place, scatter_dimension=0, tiled=True)
    d_mixed = to_attention(matmul_right(d_attended, full_output).astype(BF16))
    d_mixed = d_mixed.reshape(1, tokens, heads, HEAD_DIM).astype(F32)
    head_dot = jnp.sum(d_mixed * round_heads, -1)
    all_dot = group_sum(jnp.sum(mix_weights * head_dot, 0), sharing)
    d_spread = mix_weights * (head_dot - all_dot)
    d_round = (mix_weights[..., None] * d_mixed).astype(BF16).reshape(own_rounds, tokens, width)
    pieces = [piece.astype(BF16) for piece in split_three(d_spread)]
    blank = jnp.zeros((own_rounds, tokens, 128 - 3 * heads), BF16)
    grads = jnp.concatenate([d_round] + pieces + [blank], 2)
    d_total = attention_backward(grads, placed, slot_spread, places, tags[0])
    d_projected = from_attention(group_sum(d_total, sharing).astype(BF16))

    d_hidden = core_sum(matmul_right(d_projected, joined))
    d_from_one, grad_gain_one, grad_bias_one = norm_back(d_hidden, unit_one, scale_one, gain_one)
    back_two = cot_own.astype(F32) + d_from_one
    grad_joined = matmul_left(hidden, d_projected)
    grad_joined = jnp.swapaxes(
        grad_joined.reshape(chips, 2, devices, shard, -1), 1, 2
    ).reshape(chips * devices, 2 * shard, -1)
    grad_joined = scatter_steps(grad_joined, place, BF16).reshape(2, shard, -1)
    grad_joined = join_columns(grad_joined, chips).reshape(shard, chips, 2, 2, width)
    grad_query_key = grad_joined[:, :, :, 0].reshape(shard, features)
    grad_value = grad_joined[:, :, :, 1].reshape(shard, features)
    small_grads = jnp.stack(
        [grad_gain_one, grad_bias_one, grad_gain_two, grad_bias_two, jnp.sum(cot_own.astype(F32), 0)]
    )
    small_grads = jnp.swapaxes(small_grads.reshape(5, 2 * chips * devices, shard), 0, 1)
    small_grads = scatter_steps(small_grads, every, F32)
    out_shape = (batch, tok, features)
    return (
        out_one.reshape(out_shape),
        out_two.reshape(out_shape),
        back_one.reshape(out_shape),
        back_two.reshape(out_shape),
        small_grads[0],
        small_grads[1],
        grad_query_key,
        grad_value,
        grad_output.astype(F32),
        small_grads[2],
        small_grads[3],
        grad_inner,
        grad_inner_bias,
        grad_outer.astype(F32),
        small_grads[4],
    )


def solution(mesh):
    split = Mesh(
        mesh.devices.reshape(mesh.shape["dp"] // 2, 2, mesh.shape["seq"]), ("chip", "core", "seq")
    )
    dp = ("chip", "core")
    every = ("chip", "core", "seq")
    stream, meta, vector, matrix = (
        P(dp, "seq", None), P(dp, None, "seq"), P(every), P(every, None)
    )
    return jax.shard_map(
        local,
        mesh=split,
        in_specs=(
            stream, stream, meta, meta, stream, stream,
            vector, vector, matrix, matrix, matrix, vector, vector, matrix, vector, matrix, vector,
        ),
        out_specs=(
            stream, stream, stream, stream,
            vector, vector, matrix, matrix, matrix, vector, vector, matrix, vector, matrix, vector,
        ),
        check_vma=False,
    )
```

```python
import functools

import jax
import jax.numpy as jnp
from jax import lax
from jax.experimental import pallas as pl
from jax.experimental.pallas import tpu as pltpu
from jax.sharding import Mesh, PartitionSpec as P

HEADS = 8
HEAD_DIM = 128
SPAN = 64
PAIR = 2 * SPAN
WINDOW = PAIR + SPAN
FORWARD_PAIRS = 4
BACKWARD_PAIRS = 4
F32 = jnp.float32
BF16 = jnp.bfloat16
CORE_SWAP = [(0, 1), (1, 0)]


def matmul(left, right):
    return jnp.dot(left, right, preferred_element_type=F32)


def matmul_left(left, right):
    return lax.dot_general(left, right, (((0,), (0,)), ((), ())), preferred_element_type=F32)


def matmul_right(left, right):
    return lax.dot_general(left, right, (((1,), (1,)), ((), ())), preferred_element_type=F32)


def norm_parts(value, gain, bias):
    row_mean = jnp.mean(value, -1, keepdims=True)
    centred = value - row_mean
    inv_scale = lax.rsqrt(jnp.mean(centred * centred, -1, keepdims=True) + 1e-05)
    normal = centred * inv_scale
    return (normal * gain + bias, normal, inv_scale)


def norm_back(cotangent, normal, inv_scale, gain):
    d_normal = cotangent * gain
    d_input = inv_scale * (
        d_normal
        - jnp.mean(d_normal, -1, keepdims=True)
        - normal * jnp.mean(d_normal * normal, -1, keepdims=True)
    )
    return (d_input, jnp.sum(cotangent * normal, 0), jnp.sum(cotangent, 0))


def swap(block):
    return lax.ppermute(block, "core", CORE_SWAP)


def pick(block, position, axis):
    return lax.dynamic_index_in_dim(block, position, axis, keepdims=False)


def exchange(block, axis, bit):
    size = lax.axis_size(axis)
    return lax.ppermute(block, axis, [(i, i ^ bit) for i in range(size)])


def half_steps(axis):
    steps = []
    bit = lax.axis_size(axis) // 2
    while bit:
        steps.append((axis, bit))
        bit //= 2
    return steps


def side(axis, bit):
    return (lax.axis_index(axis) // bit) % 2


def ordered(own, other, axis, bit):
    upper = side(axis, bit) == 1
    return jnp.where(upper, jnp.stack([other, own]), jnp.stack([own, other]))


class Gather:
    def __init__(self, block):
        self.dims = half_steps("chip") + [None] + half_steps("seq")
        self.tail = list(block.shape[1:])
        self.sizes = [2 if dim is None else 1 for dim in self.dims] + self.tail
        self.starts = [0 if dim is None else side(*dim) for dim in self.dims] + [0] * len(self.tail)
        buffer = jnp.zeros([2] * len(self.dims) + self.tail, block.dtype)
        self.held = lax.dynamic_update_slice(buffer, block.reshape(self.sizes), self.starts)

    def step(self, step):
        dim = self.dims.index(step)
        piece = exchange(lax.dynamic_slice(self.held, self.starts, self.sizes), *step)
        opposite = list(self.starts)
        opposite[dim] = 1 - self.starts[dim]
        self.held = lax.dynamic_update_slice(self.held, piece, opposite)
        self.starts[dim], self.sizes[dim] = 0, 2


class Stack:
    def __init__(self, block):
        self.held = block

    def step(self, step):
        self.held = ordered(self.held, exchange(self.held, *step), *step)


class Scatter:
    def __init__(self, total):
        self.dims = half_steps("chip") + [None] + half_steps("seq")
        self.held = total.reshape([2] * len(self.dims) + list(total.shape[3:]))

    def step(self, step):
        dim = self.dims.index(step)
        mine = side(*step)
        sent = exchange(pick(self.held, 1 - mine, dim).astype(BF16), *step)
        self.held = pick(self.held, mine, dim) + sent.astype(F32)
        self.dims.pop(dim)


class Halve:
    def __init__(self, total):
        self.held = total

    def step(self, step):
        half = self.held.reshape((2, self.held.shape[0] // 2) + self.held.shape[1:])
        mine = side(*step)
        self.held = pick(half, mine, 0) + exchange(pick(half, 1 - mine, 0), *step)


def together(chains):
    for chain, held in zip(chains, lax.optimization_barrier([chain.held for chain in chains])):
        chain.held = held


def all_to_all(block):
    return lax.all_to_all(block, "seq", split_axis=0, concat_axis=0, tiled=True)


def group_routes(count):
    size = lax.axis_size("seq")
    return [
        [(i, i // count * count + (i % count + step) % count) for i in range(size)]
        for step in range(1, count)
    ]


def group_sum(value, count):
    total = value
    for route in group_routes(count):
        total = total + lax.ppermute(value, "seq", route)
    return total


def group_max(value, count):
    total = value
    for route in group_routes(count):
        total = jnp.maximum(total, lax.ppermute(value, "seq", route))
    return total


def own_bias():
    own = jnp.arange(WINDOW)[:, None] == jnp.arange(PAIR)[None, :] + SPAN
    return jnp.where(own, -1e5, 0.0).astype(F32)


def pair_rows():
    return (jnp.arange(HEAD_DIM)[:, None] == jnp.arange(PAIR)[None, :] // SPAN).astype(BF16)


def flipped(value):
    return jnp.transpose(value.astype(F32)).astype(BF16)


def split_three(value):
    high = value.astype(BF16).astype(F32)
    rest = value - high
    middle = rest.astype(BF16).astype(F32)
    return high, middle, rest - middle


def in_lanes(columns, rows):
    lane = lax.broadcasted_iota(jnp.int32, (rows, 128), 1)
    out = jnp.zeros((rows, 128), F32)
    for k, column in enumerate(columns):
        out = jnp.where(lane == k, column, out)
    return out


def stacked_rows(rows):
    blank = jnp.zeros((128 - len(rows), 128), F32)
    return jnp.transpose(jnp.concatenate(rows + [blank], 0))


def pack_three(value, count):
    high, middle, low = split_three(value)
    return (high + pltpu.roll(middle, count, 1) + pltpu.roll(low, 2 * count, 1)).astype(BF16)


def sum_three(packed, count):
    return packed + pltpu.roll(packed, 128 - count, 1) + pltpu.roll(packed, 128 - 2 * count, 1)


def one_hot_rows(place_row, base, rows, tokens):
    slot = lax.broadcasted_iota(jnp.int32, (rows, tokens), 0) + base
    return jnp.where(slot == place_row, 1.0, 0.0).astype(BF16)


def one_hot_columns(place_column, rows, slots):
    slot = lax.broadcasted_iota(jnp.int32, (rows, slots), 1)
    return jnp.where(slot == place_column, 1.0, 0.0).astype(BF16)


def tile_rows(tokens):
    if tokens <= 1024:
        return 3 * tokens // 4, tokens // 2
    return 3 * SPAN, 128


def at_once(pairs, most):
    return most if pairs % most == 0 else 1


def aligned(start, rows):
    return pl.ds(pl.multiple_of(start, SPAN), rows)


def forward_kernel(
    heads, mixing, qv_ref, row_ref, column_ref, key_bias_ref, own_bias_ref, pair_row_ref,
    out_ref, spread_ref, mixed_ref, placed_ref, slot_spread_ref, result_ref
):
    this_round, rounds = pl.program_id(0), out_ref.shape[0]
    tokens = qv_ref.shape[0]
    slots = placed_ref.shape[1] - SPAN
    width = heads * HEAD_DIM
    place_rows, token_rows = tile_rows(tokens)
    placed_ref[0, 0:SPAN] = jnp.zeros((SPAN, 3 * width), BF16)

    def place(step, carry):
        base = pl.multiple_of(step * place_rows, place_rows)
        hot = one_hot_rows(row_ref[0], base, place_rows, tokens)
        rows = matmul(hot, qv_ref[...])
        where = pl.ds(pl.multiple_of(base + SPAN, SPAN), place_rows)
        placed_ref[0, where, 0 : 2 * width] = rows.astype(BF16)
        for head in range(heads):
            query = rows[:, head * HEAD_DIM : (head + 1) * HEAD_DIM]
            scale = lax.rsqrt(jnp.mean(query * query, -1, keepdims=True) + 1e-06)
            first = 2 * width + head * HEAD_DIM
            placed_ref[0, where, first : first + HEAD_DIM] = (query * (scale * (1.0 / HEAD_DIM))).astype(BF16)
        return carry

    lax.fori_loop(0, slots // place_rows, place, 0)

    pairs = slots // PAIR
    batch = at_once(pairs, FORWARD_PAIRS)
    lanes_of = [slice(head * HEAD_DIM, (head + 1) * HEAD_DIM) for head in range(heads)]

    def attend(step, carry):
        chains = [(step * batch + part, head) for part in range(batch) for head in range(heads)]
        bias, pair_row = own_bias_ref[...], pair_row_ref[...]
        scores = []
        for pair, head in chains:
            query = placed_ref[0, aligned(pair * PAIR + SPAN, PAIR), lanes_of[head]]
            keys = placed_ref[0, aligned(pair * PAIR, WINDOW), 2 * width + head * HEAD_DIM : 2 * width + (head + 1) * HEAD_DIM]
            left = jnp.concatenate([keys, key_bias_ref[0, pair]], 1)
            right = jnp.concatenate([flipped(query), pair_row], 0)
            scores.append(matmul(left, right) + bias)
        tops = [jnp.max(score, 0, keepdims=True) for score in scores]
        exponents = [jnp.exp(score - top) for score, top in zip(scores, tops)]
        sums = [jnp.sum(exponent, 0, keepdims=True) for exponent in exponents]
        spreads = [top + jnp.log(total) for top, total in zip(tops, sums)]
        for (pair, head), exponent, total in zip(chains, exponents, sums):
            values = placed_ref[0, aligned(pair * PAIR, WINDOW), width + head * HEAD_DIM : width + (head + 1) * HEAD_DIM]
            probability = jnp.transpose(exponent * (1.0 / total)).astype(BF16)
            result_ref[aligned(pair * PAIR, PAIR), lanes_of[head]] = matmul(probability, values).astype(BF16)
        for part in range(batch):
            pair, rows = step * batch + part, spreads[part * heads : (part + 1) * heads]
            slot_spread_ref[0, pair] = jnp.concatenate(rows + [jnp.zeros((8 - heads, 128), F32)], 0)
            terms = [split_three(row) for row in rows]
            packed = stacked_rows([term[k] for k in range(3) for term in terms])
            result_ref[aligned(pair * PAIR, PAIR), width : width + 128] = packed.astype(BF16)
        return carry

    lax.fori_loop(0, pairs // batch, attend, 0)

    def read_back(step, carry):
        where = pl.ds(pl.multiple_of(step * token_rows, token_rows), token_rows)
        hot = one_hot_columns(column_ref[0, where, :], token_rows, slots)
        rows = matmul(hot, result_ref[...])
        out_ref[this_round, where, :] = rows[:, :width].astype(BF16)
        spread_ref[this_round, where, :] = sum_three(rows[:, width:], heads)
        return carry

    lax.fori_loop(0, tokens // token_rows, read_back, 0)

    if mixing:

        @pl.when(this_round == rounds - 1)
        def _():
            def mix(step, carry):
                where = pl.ds(pl.multiple_of(step * 128, 128), 128)
                spreads = [spread_ref[r, where, :] for r in range(rounds)]
                top = functools.reduce(jnp.maximum, spreads)
                weights = [jnp.exp(spread - top) for spread in spreads]
                share = 1.0 / functools.reduce(jnp.add, weights)
                weights = [weight * share for weight in weights]
                for r in range(rounds):
                    spread_ref[r, where, :] = weights[r]
                for head in range(heads):
                    lanes = slice(head * HEAD_DIM, (head + 1) * HEAD_DIM)
                    total = functools.reduce(
                        jnp.add,
                        [
                            weights[r][:, head : head + 1] * out_ref[r, where, lanes].astype(F32)
                            for r in range(rounds)
                        ],
                    )
                    mixed_ref[where, lanes] = total.astype(BF16)
                return carry

            lax.fori_loop(0, tokens // 128, mix, 0)


def backward_kernel(
    heads, mixing, d_mixed_ref, out_ref, weight_ref, dot_ref, placed_ref, slot_spread_ref, row_ref,
    column_ref, key_bias_ref, own_bias_ref, pair_row_ref, total_ref, d_spread_ref, token_grad_ref, slot_grad_ref,
    d_place_ref, sum_ref
):
    if not mixing:
        sum_ref = total_ref
    this_round, rounds = pl.program_id(0), out_ref.shape[0]
    tokens = d_mixed_ref.shape[0]
    slots = placed_ref.shape[1] - SPAN
    width = heads * HEAD_DIM
    place_rows, token_rows = tile_rows(tokens)
    head_lanes = [slice(head * HEAD_DIM, (head + 1) * HEAD_DIM) for head in range(heads)]

    @pl.when(this_round == 0)
    def _():
        sum_ref[...] = jnp.zeros(sum_ref.shape, F32)

        def dots(step, carry):
            where = pl.ds(pl.multiple_of(step * 128, 128), 128)
            inner = []
            for r in range(rounds):
                columns = [
                    jnp.sum(
                        d_mixed_ref[where, lanes].astype(F32) * out_ref[r, where, lanes].astype(F32),
                        -1,
                        keepdims=True,
                    )
                    for lanes in head_lanes
                ]
                inner.append(in_lanes(columns, 128))
            if mixing:
                every = functools.reduce(
                    jnp.add, [weight_ref[r, where, :] * inner[r] for r in range(rounds)]
                )
            else:
                every = dot_ref[where, :]
            for r in range(rounds):
                d_spread_ref[r, where, :] = weight_ref[r, where, :] * (inner[r] - every)
            return carry

        lax.fori_loop(0, tokens // 128, dots, 0)


    def weigh(step, carry):
        where = pl.ds(pl.multiple_of(step * 128, 128), 128)
        for head, lanes in enumerate(head_lanes):
            share = weight_ref[this_round, where, head : head + 1]
            token_grad_ref[where, lanes] = (share * d_mixed_ref[where, lanes].astype(F32)).astype(BF16)
        token_grad_ref[where, width : width + 128] = pack_three(
            d_spread_ref[this_round, where, :], heads
        )
        return carry

    lax.fori_loop(0, tokens // 128, weigh, 0)

    def place(step, carry):
        base = pl.multiple_of(step * place_rows, place_rows)
        hot = one_hot_rows(row_ref[0], base, place_rows, tokens)
        slot_grad_ref[pl.ds(base, place_rows), :] = matmul(
            hot, token_grad_ref[...]
        ).astype(BF16)
        return carry

    lax.fori_loop(0, slots // place_rows, place, 0)

    pairs = slots // PAIR
    batch = at_once(pairs, BACKWARD_PAIRS)

    def finish(start, rows, head, d_query, d_unit, d_value):
        here = aligned(start + SPAN, rows)
        query = placed_ref[0, here, head_lanes[head]].astype(F32)
        scale = lax.rsqrt(jnp.mean(query * query, -1, keepdims=True) + 1e-06)
        inner = jnp.mean(d_unit * query, -1, keepdims=True)
        factor = scale * (1.0 / HEAD_DIM)
        d_query = d_query + factor * d_unit - query * (factor * scale * scale * inner)
        d_place_ref[here, head_lanes[head]] = d_query.astype(BF16)
        d_place_ref[here, width + head * HEAD_DIM : width + (head + 1) * HEAD_DIM] = d_value.astype(BF16)

    def attend(step, carry):
        chains = [(step * batch + part, head) for part in range(batch) for head in range(heads)]
        bias, pair_row = own_bias_ref[...], pair_row_ref[...]
        d_spread_rows = []
        for part in range(batch):
            packed = slot_grad_ref[aligned((step * batch + part) * PAIR, PAIR), width : width + 128]
            rows = jnp.transpose(packed.astype(F32))
            d_spread_rows += [
                rows[head : head + 1]
                + rows[heads + head : heads + head + 1]
                + rows[2 * heads + head : 2 * heads + head + 1]
                for head in range(heads)
            ]
        scores, d_probs = [], []
        for pair, head in chains:
            query = placed_ref[0, aligned(pair * PAIR + SPAN, PAIR), head_lanes[head]]
            keys = placed_ref[0, aligned(pair * PAIR, WINDOW), 2 * width + head * HEAD_DIM : 2 * width + (head + 1) * HEAD_DIM]
            values = placed_ref[0, aligned(pair * PAIR, WINDOW), width + head * HEAD_DIM : width + (head + 1) * HEAD_DIM]
            left = jnp.concatenate([keys, key_bias_ref[0, pair]], 1)
            right = jnp.concatenate([flipped(query), pair_row], 0)
            scores.append(matmul(left, right) + bias)
            d_out = slot_grad_ref[aligned(pair * PAIR, PAIR), head_lanes[head]]
            d_probs.append(matmul(values, flipped(d_out)))
        probs = [
            jnp.exp(score - slot_spread_ref[0, pair, head : head + 1, :])
            for (pair, head), score in zip(chains, scores)
        ]
        dots = [jnp.sum(p * d, 0, keepdims=True) for p, d in zip(probs, d_probs)]
        d_scores = [
            p * (d + (row - dot)) for p, d, row, dot in zip(probs, d_probs, d_spread_rows, dots)
        ]
        last = list(carry)
        for (pair, head), p, d in zip(chains, probs, d_scores):
            query = placed_ref[0, aligned(pair * PAIR + SPAN, PAIR), head_lanes[head]]
            keys = placed_ref[0, aligned(pair * PAIR, WINDOW), 2 * width + head * HEAD_DIM : 2 * width + (head + 1) * HEAD_DIM]
            d_out = slot_grad_ref[aligned(pair * PAIR, PAIR), head_lanes[head]]
            d_query = matmul(jnp.transpose(d).astype(BF16), keys)
            d_keys = matmul(d.astype(BF16), query)
            d_values = matmul(p.astype(BF16), d_out)
            last_query, last_key, last_value = last[head]

            before = pair * PAIR - SPAN
            finish(before, SPAN, head, last_query, last_key + d_keys[:SPAN], last_value + d_values[:SPAN])
            finish(pair * PAIR, SPAN, head, d_query[:SPAN], d_keys[SPAN:PAIR], d_values[SPAN:PAIR])
            last[head] = (d_query[SPAN:], d_keys[PAIR:], d_values[PAIR:])
        return tuple(last)

    blank = jnp.zeros((SPAN, HEAD_DIM), F32)
    carry = lax.fori_loop(
        0, pairs // batch, attend, tuple((blank, blank, blank) for _ in range(heads))
    )
    for head in range(heads):
        finish(slots - SPAN, SPAN, head, *carry[head])

    def read_back(step, carry):
        where = pl.ds(pl.multiple_of(step * token_rows, token_rows), token_rows)
        hot = one_hot_columns(column_ref[0, where, :], token_rows, slots)
        sum_ref[where, :] += matmul(hot, d_place_ref[SPAN:, :])
        return carry

    lax.fori_loop(0, tokens // token_rows, read_back, 0)

    if mixing:

        @pl.when(this_round == rounds - 1)
        def _():
            total_ref[...] = sum_ref[...].astype(BF16)


def per_round(shape, buffers):
    rest = (0,) * (len(shape) - 1)
    return pl.BlockSpec((1,) + shape[1:], lambda r: (r,) + rest, pipeline_mode=pl.Buffered(buffers))


def whole(shape):
    return pl.BlockSpec(shape, lambda r: (0,) * len(shape), pipeline_mode=pl.Buffered(1))


def attention_forward(qv, places, key_bias, mixing):
    row, column = places
    rounds, _, tokens = row.shape
    slots = key_bias.shape[1] * PAIR
    width = qv.shape[1] // 2
    heads = width // HEAD_DIM
    buffers = min(2, rounds)
    bias, pair_row = own_bias(), pair_rows()
    kept = [
        jax.ShapeDtypeStruct((rounds, tokens, width), BF16),
        jax.ShapeDtypeStruct((rounds, tokens, 128), F32),
        jax.ShapeDtypeStruct((tokens if mixing else 8, width), BF16),
    ]
    outs = [
        jax.ShapeDtypeStruct((rounds, slots + SPAN, 3 * width), BF16),
        jax.ShapeDtypeStruct((rounds, slots // PAIR, 8, PAIR), F32),
    ]
    flops = rounds * slots * (2 * tokens * (3 * width + 128) + 4 * width * WINDOW)
    return pl.pallas_call(
        functools.partial(forward_kernel, heads, mixing),
        grid=(rounds,),
        in_specs=[whole(qv.shape)]
        + [per_round(x.shape, buffers) for x in (row, column, key_bias)]
        + [whole(bias.shape), whole(pair_row.shape)],
        out_specs=[whole(x.shape) for x in kept] + [per_round(x.shape, buffers) for x in outs],
        out_shape=kept + outs,
        scratch_shapes=[pltpu.VMEM((slots, width + 128), BF16)],
        compiler_params=pltpu.CompilerParams(vmem_limit_bytes=56 * 1024 * 1024),
        cost_estimate=pl.CostEstimate(flops=flops, bytes_accessed=20 << 20, transcendentals=0),
    )(qv, row, column, key_bias, bias, pair_row)


def attention_backward(d_mixed, round_out, weights, all_dot, placed, slot_spread, places, key_bias):
    row, column = places
    rounds, _, tokens = row.shape
    slots = placed.shape[1] - SPAN
    width = placed.shape[2] // 3
    heads = width // HEAD_DIM
    buffers = min(2, rounds)
    bias, pair_row = own_bias(), pair_rows()
    mixing = all_dot is None
    if mixing:
        all_dot = jnp.zeros((8, 128), F32)
    flops = rounds * slots * (2 * tokens * (3 * width + 128) + 10 * width * WINDOW)
    return pl.pallas_call(
        functools.partial(backward_kernel, heads, mixing),
        grid=(rounds,),
        in_specs=[whole(x.shape) for x in (d_mixed, round_out, weights, all_dot)]
        + [per_round(x.shape, buffers) for x in (placed, slot_spread, row, column, key_bias)]
        + [whole(bias.shape), whole(pair_row.shape)],
        out_specs=whole((tokens, 2 * width)),
        out_shape=jax.ShapeDtypeStruct((tokens, 2 * width), BF16 if mixing else F32),
        scratch_shapes=[
            pltpu.VMEM((rounds, tokens, 128), F32),
            pltpu.VMEM((tokens, width + 128), BF16),
            pltpu.VMEM((slots, width + 128), BF16),
            pltpu.VMEM((slots + SPAN, 2 * width), BF16),
            pltpu.VMEM((tokens if mixing else 8, 2 * width), F32),
        ],
        compiler_params=pltpu.CompilerParams(vmem_limit_bytes=60 * 1024 * 1024),
        cost_estimate=pl.CostEstimate(flops=flops, bytes_accessed=20 << 20, transcendentals=0),
    )(d_mixed, round_out, weights, all_dot, placed, slot_spread, row, column, key_bias, bias, pair_row)


def local(
    stream_one,
    stream_two,
    slot_place,
    bucket_ids,
    grad_one,
    grad_two,
    norm1_gain,
    norm1_bias,
    w_query_key,
    w_value,
    w_output,
    norm2_gain,
    norm2_bias,
    w_inner,
    inner_bias,
    w_outer,
    outer_bias,
):
    chips, devices = lax.axis_size("chip"), lax.axis_size("seq")
    batch, tok, features = stream_one.shape
    rounds = slot_place.shape[1]
    sequences = 2 * batch
    tokens = devices * tok
    slots = 3 * tokens // 2
    own_rows = batch * tok
    width = features // (2 * chips)
    heads = width // HEAD_DIM
    hidden_units = w_inner.shape[1]
    quarter = hidden_units // (2 * chips)
    units = sequences * chips
    sharing = devices // units
    mixing = sharing == 1
    own_rounds = rounds // sharing
    shard = w_query_key.shape[0]
    core, chip = lax.axis_index("core"), lax.axis_index("chip")

    def by_core(own, other):
        return jnp.where(core == 0, jnp.stack([own, other]), jnp.stack([other, own]))

    def flip(block):
        return exchange(block, "chip", 1)

    def both_chips(block):
        return ordered(block, flip(block), "chip", 1) if chips == 2 else block[None]

    def trade_quarters(pieces):
        if chips == 2:
            kept, sent = pick(pieces, chip, 0), pick(pieces, 1 - chip, 0)
            pieces = ordered(kept, flip(sent), "chip", 1)
        return jnp.swapaxes(by_core(pick(pieces, core, 1), swap(pick(pieces, 1 - core, 1))), 0, 1)

    seq_steps, chip_steps = half_steps("seq"), half_steps("chip")
    mid_steps = seq_steps[1:-1]
    gather_orders = [
        seq_steps[:1] + seq_steps[-1:] + mid_steps + chip_steps,
        chip_steps + seq_steps[:1] + seq_steps[-1:] + mid_steps,
    ]
    scatter_orders = [
        chip_steps + seq_steps[-1:] + mid_steps + seq_steps[:1],
        mid_steps + chip_steps + seq_steps[-1:] + seq_steps[:1],
    ]

    base = 64
    meta = jnp.stack([slot_place // base, slot_place % base, bucket_ids + 1], 1).astype(BF16)
    small = [norm1_gain, norm1_bias, norm2_gain, norm2_bias, outer_bias]
    small = jnp.concatenate([jnp.concatenate(small), inner_bias, meta.reshape(-1)])

    key_split = w_query_key.reshape(shard, chips, 2, width)
    value_split = w_value.reshape(shard, chips, 2, width)
    joined_split = jnp.concatenate([key_split, value_split], 3)
    joined_own, joined_sent = pick(joined_split, core, 2), pick(joined_split, 1 - core, 2)
    streams, joined_got, small_other = lax.optimization_barrier(
        (stream_two.reshape(own_rows, features), swap(joined_sent), swap(small))
    )
    joined_both = by_core(joined_own, joined_got)
    chains = [Gather(joined_both[:, :, pair]) for pair in range(chips)]
    small = Stack(by_core(small, small_other))
    small_steps = mid_steps + seq_steps[:1] + seq_steps[-1:]
    for k in range(len(seq_steps) + len(chip_steps)):
        for pair, chain in enumerate(chains):
            chain.step(gather_orders[pair % 2][k])
        if k < len(small_steps):
            small.step(small_steps[k])
            together(chains + [small])
            if k == len(small_steps) - 1:
                split = small.held.reshape([2] * len(small_steps) + list(small.held.shape[-2:]))
                taken = small_steps[::-1]
                split = jnp.transpose(
                    split,
                    [taken.index(step) for step in seq_steps] + [split.ndim - 2, split.ndim - 1],
                ).reshape(devices, 2, -1)
                vectors = Stack(jnp.swapaxes(split[:, :, : 5 * shard], 0, 1))
                cut = 5 * shard + inner_bias.shape[0]
                quarter_bias = pick(split[:, :, 5 * shard : cut], core, 1).reshape(-1).astype(F32)
                meta = split[:, :, cut:].reshape(devices, 2, batch, 3, rounds, tok)
                for step in chip_steps:
                    vectors.step(step)
    joined = [chain.held.reshape(features, 2 * width) for chain in chains]
    vectors = jnp.moveaxis(vectors.held.reshape(-1, 5, shard), 1, 0).reshape(5, features).astype(F32)
    gain_one, bias_one, gain_two, bias_two, full_outer_bias = [vectors[k] for k in range(5)]

    inner_pieces = jnp.moveaxis(w_inner.reshape(shard, chips, 2, quarter), 0, 2)
    inner_pieces = trade_quarters(inner_pieces).reshape(-1, features)
    output_pieces = both_chips(w_output).reshape(-1, features)
    bundle = jnp.concatenate([w_outer, inner_pieces, output_pieces], 0)
    bundle, *joined = lax.optimization_barrier([bundle] + joined)
    cuts = [w_outer.shape[0], w_outer.shape[0] + inner_pieces.shape[0]]
    gathered = lax.all_gather(bundle, "seq", axis=0, tiled=False)
    full_outer = gathered[:, : cuts[0]].reshape(quarter, features)
    full_inner = gathered[:, cuts[0] : cuts[1]].reshape(devices, 2 * chips, shard, quarter)
    full_inner = jnp.swapaxes(full_inner, 0, 1).reshape(features, quarter)
    full_output = gathered[:, cuts[1] :].reshape(devices, chips, shard, features)
    full_output = jnp.swapaxes(full_output, 0, 1).reshape(chips * width, features)

    unit = lax.axis_index("seq") // sharing
    sequence = unit // chips
    owner = jnp.where(sequence < batch, core, 1 - core)
    meta = lax.dynamic_slice(
        meta,
        (0, owner, sequence % batch, 0, lax.axis_index("seq") % sharing * own_rounds, 0),
        (devices, 1, 1, 3, own_rounds, tok),
    )
    meta = jnp.moveaxis(meta.reshape(devices, 3, own_rounds, tok), 0, 2)
    meta = meta.reshape(3, own_rounds, tokens).astype(jnp.int32)
    token_place, token_tag = meta[0] * base + meta[1], meta[2]
    found = token_place[:, :, None] == jnp.arange(slots)[None, None, :]
    slot_tag = jnp.sum(jnp.where(found, token_tag[:, :, None], 0), 1)
    slot_tag = jnp.pad(slot_tag.reshape(own_rounds, slots // SPAN, SPAN), ((0, 0), (1, 0), (0, 0)))
    span_tag = jnp.max(slot_tag, 2, keepdims=True)
    first, second, third = slot_tag[:, :-2:2], slot_tag[:, 1:-1:2], slot_tag[:, 2::2]
    unmet = jnp.full(first.shape, False)
    met = jnp.stack(
        [
            jnp.concatenate([first == span_tag[:, 1:-1:2], second == span_tag[:, 1:-1:2], unmet], 2),
            jnp.concatenate([unmet, second == span_tag[:, 2::2], third == span_tag[:, 2::2]], 2),
        ],
        3,
    )
    key_bias = jnp.where(met, 0.0, -1e9).astype(BF16)
    key_bias = jnp.pad(key_bias, ((0, 0), (0, 0), (0, 0), (0, HEAD_DIM - 2)))
    places = (token_place[:, None, :], token_place[:, :, None])

    def near(value):
        return jnp.concatenate([value, swap(value)], 0)

    def far(value):
        return near(flip(value))

    def everywhere(value):
        return jnp.concatenate([near(value), far(value)], 0) if chips == 2 else near(value)

    stream_a = stream_one.astype(F32).reshape(own_rows, features)
    stream_b = streams.astype(F32)
    normed_one, unit_one, scale_one = norm_parts(near(streams).astype(F32), gain_one, bias_one)
    hidden = normed_one.astype(BF16)
    unit_one, scale_one = unit_one[:own_rows], scale_one[:own_rows]
    projected = [matmul(hidden, weight).astype(BF16) for weight in joined]

    def to_attention(pairs):
        value = jnp.stack([pair.reshape(sequences, tok, -1) for pair in pairs], 1)
        value = jnp.broadcast_to(value[:, :, None], value.shape[:2] + (sharing,) + value.shape[2:])
        return all_to_all(value.reshape(devices, tok, -1)).reshape(tokens, -1)

    def from_attention(value):
        value = all_to_all(value.reshape(devices, tok, -1))
        value = value.reshape(sequences, chips, sharing, tok, -1)
        return [value[:, pair, 0].reshape(sequences * tok, -1) for pair in range(chips)]

    round_out, weights, mixed, placed, slot_spread = attention_forward(
        to_attention(projected), places, key_bias, mixing
    )
    if not mixing:
        top = group_max(jnp.max(weights, 0), sharing)
        weights = jnp.exp(weights - top)
        weights = weights / group_sum(jnp.sum(weights, 0), sharing)
        by_head = round_out.reshape(own_rounds, tokens, heads, HEAD_DIM)
        mixed = group_sum(jnp.sum(weights[:, :, :heads, None] * by_head, 0), sharing)
        mixed = mixed.reshape(tokens, width).astype(BF16)
    mixed = jnp.concatenate(from_attention(mixed), 1)

    def core_sum(value):
        return value[:own_rows] + swap(value[own_rows:])

    out_one = stream_a + core_sum(matmul(mixed, full_output))
    normed_two, unit_two, scale_two = norm_parts(out_one, gain_two, bias_two)
    inner_low = normed_two.astype(BF16)
    cot_own = grad_two.reshape(own_rows, features)

    def feed_forward(value, cotangent):
        pre_act = matmul(value, full_inner) + quarter_bias
        activated, gelu_pull = jax.vjp(jax.nn.gelu, pre_act)
        act_low = activated.astype(BF16)
        d_act = matmul_right(cotangent, full_outer)
        d_pre = gelu_pull(d_act)[0].astype(BF16)
        return act_low, d_pre, matmul(act_low, full_outer), matmul_right(d_pre, full_inner)

    parts = [(near(inner_low), near(cot_own))]
    if chips == 2:
        parts.append((far(inner_low), far(cot_own)))
    done = [feed_forward(*part) for part in parts]
    rows_in, rows_cot = [jnp.concatenate([part[k] for part in parts], 0) for k in range(2)]
    act_low, d_pre = [jnp.concatenate([part[k] for part in done], 0) for k in range(2)]

    def quarter_sum(values):
        total = core_sum(values[0])
        if chips == 2:
            total = total + flip(core_sum(values[1]).astype(BF16)).astype(F32)
        return total

    d_normed_two = quarter_sum([part[3] for part in done])
    d_from_two, grad_gain_two, grad_bias_two = norm_back(
        d_normed_two, unit_two, scale_two, gain_two
    )
    back_one = grad_one.astype(F32).reshape(own_rows, features) + d_from_two
    out_two = stream_b + quarter_sum([part[2] for part in done]) + full_outer_bias

    d_attended = near(back_one.astype(BF16))
    d_mixed = matmul_right(d_attended, full_output).astype(BF16)
    d_mixed = to_attention([d_mixed[:, p * width : (p + 1) * width] for p in range(chips)])

    grad_outer = matmul_left(act_low, rows_cot).astype(BF16)
    grad_inner = matmul_left(rows_in, d_pre).astype(BF16)
    grad_output = matmul_left(mixed, d_attended).astype(BF16)
    grad_inner = jnp.swapaxes(grad_inner.reshape(2 * chips, devices, shard, quarter), 0, 1)
    grad_output = jnp.swapaxes(grad_output.reshape(chips, devices, shard, features), 0, 1)
    summed = jnp.concatenate(
        [
            grad_outer.reshape(devices, -1, features),
            grad_inner.reshape(devices, -1, features),
            grad_output.reshape(devices, -1, features),
        ],
        1,
    )
    summed, d_mixed = lax.optimization_barrier((summed, d_mixed))
    summed = lax.psum_scatter(summed, "seq", scatter_dimension=0, tiled=True)[0]
    quarter_bias_grad = jnp.sum(d_pre.astype(F32), 0).reshape(devices, -1)

    all_dot = None
    if not mixing:
        inner = d_mixed.reshape(1, tokens, heads, HEAD_DIM).astype(F32) * by_head
        inner = jnp.sum(weights[:, :, :heads] * jnp.sum(inner, -1), 0)
        all_dot = jnp.pad(group_sum(inner, sharing), ((0, 0), (0, 128 - heads)))
    d_total = attention_backward(
        d_mixed, round_out, weights, all_dot, placed, slot_spread, places, key_bias
    )
    if not mixing:
        d_total = group_sum(d_total, sharing).astype(BF16)
    d_projected = from_attention(d_total)

    chains = []
    for pair in range(chips):
        grad = matmul_left(hidden, d_projected[pair])
        chains.append(Scatter(grad.reshape(chips, 2, devices, shard, 2 * width)))
    orders = list(zip(*[scatter_orders[pair % 2] for pair in range(chips)]))
    for chain, step in zip(chains, orders[0]):
        chain.step(step)
    d_hidden = core_sum(
        functools.reduce(jnp.add, [matmul_right(d, w) for d, w in zip(d_projected, joined)])
    )
    d_from_one, grad_gain_one, grad_bias_one = norm_back(d_hidden, unit_one, scale_one, gain_one)
    back_two = cot_own.astype(F32) + d_from_one
    small_grads = jnp.stack(
        [grad_gain_one, grad_bias_one, grad_gain_two, grad_bias_two, jnp.sum(cot_own.astype(F32), 0)]
    )
    small_grads = jnp.swapaxes(small_grads.reshape(5, 2 * chips * devices, shard), 0, 1)
    small_grads = Halve(small_grads.reshape(-1, 5 * shard))
    small_steps = chip_steps + [("core", 1)] + seq_steps
    reduced = Stack(summed)
    for k in range(max(len(orders) - 1, len(small_steps))):
        together(chains + [small_grads] + [reduced] * (k == 0))
        if k + 1 < len(orders):
            for chain, step in zip(chains, orders[k + 1]):
                chain.step(step)
        elif k + 1 == len(orders):
            grad_joined = jnp.stack([chain.held for chain in chains], 1)
            grad_joined = by_core(pick(grad_joined, core, 0), swap(pick(grad_joined, 1 - core, 0)))
        if small_steps[k][0] == "seq" and small_grads.held.shape[1] == 5 * shard:
            small_grads.held = jnp.concatenate([small_grads.held, quarter_bias_grad], 1)
        small_grads.step(small_steps[k])
    summed = reduced.held
    grad_outer = summed[: cuts[0]].astype(F32)
    grad_inner = trade_quarters(summed[cuts[0] : cuts[1]].reshape(chips, 2, shard, quarter))
    grad_inner = jnp.moveaxis(grad_inner, 2, 0).reshape(shard, hidden_units).astype(F32)
    grad_output = summed[cuts[1] :].reshape(chips, shard, features)
    if chips == 2:
        other = flip(pick(grad_output, 1 - chip, 0)).astype(F32)
        grad_output = pick(grad_output, chip, 0).astype(F32) + other
    else:
        grad_output = grad_output[0].astype(F32)
    small_grads, grad_inner_bias = (
        small_grads.held[0, : 5 * shard].reshape(5, shard), small_grads.held[0, 5 * shard :]
    )
    grad_joined = grad_joined.reshape(2, chips, shard, 2, width)
    grad_joined = jnp.transpose(grad_joined, (3, 2, 1, 0, 4)).reshape(2, shard, features)
    out_shape = (batch, tok, features)
    return (
        out_one.reshape(out_shape),
        out_two.reshape(out_shape),
        back_one.reshape(out_shape),
        back_two.reshape(out_shape),
        small_grads[0],
        small_grads[1],
        grad_joined[0],
        grad_joined[1],
        grad_output,
        small_grads[2],
        small_grads[3],
        grad_inner,
        grad_inner_bias,
        grad_outer,
        small_grads[4],
    )


def solution(mesh):
    split = Mesh(
        mesh.devices.reshape(mesh.shape["dp"] // 2, 2, mesh.shape["seq"]), ("chip", "core", "seq")
    )
    dp = ("chip", "core")
    every = ("chip", "core", "seq")
    stream, meta, vector, matrix = (
        P(dp, "seq", None), P(dp, None, "seq"), P(every), P(every, None)
    )
    return jax.shard_map(
        local,
        mesh=split,
        in_specs=(
            stream, stream, meta, meta, stream, stream,
            vector, vector, matrix, matrix, matrix, vector, vector, matrix, vector, matrix, vector,
        ),
        out_specs=(
            stream, stream, stream, stream,
            vector, vector, matrix, matrix, matrix, vector, vector, matrix, vector, matrix, vector,
        ),
        check_vma=False,
    )
```

```python
import functools

import jax
import jax.numpy as jnp
from jax import lax
from jax.experimental import pallas as pl
from jax.experimental.pallas import tpu as pltpu
from jax.sharding import Mesh, PartitionSpec as P

HEADS = 8
HEAD_DIM = 128
SPAN = 64
PAIR = 2 * SPAN
WINDOW = PAIR + SPAN
FORWARD_PAIRS = 12
BACKWARD_PAIRS = 12
HEADS_AT_CALL = 2
TIE = 0
F32 = jnp.float32
BF16 = jnp.bfloat16
CORE_SWAP = [(0, 1), (1, 0)]


def matmul(left, right):
    return jnp.dot(left, right, preferred_element_type=F32)


def matmul_left(left, right):
    return lax.dot_general(left, right, (((0,), (0,)), ((), ())), preferred_element_type=F32)


def matmul_right(left, right):
    return lax.dot_general(left, right, (((1,), (1,)), ((), ())), preferred_element_type=F32)


def norm_parts(value, gain, bias):
    row_mean = jnp.mean(value, -1, keepdims=True)
    centred = value - row_mean
    inv_scale = lax.rsqrt(jnp.mean(centred * centred, -1, keepdims=True) + 1e-05)
    normal = centred * inv_scale
    return (normal * gain + bias, normal, inv_scale)


def norm_back(cotangent, normal, inv_scale, gain):
    d_normal = cotangent * gain
    d_input = inv_scale * (
        d_normal
        - jnp.mean(d_normal, -1, keepdims=True)
        - normal * jnp.mean(d_normal * normal, -1, keepdims=True)
    )
    return (d_input, jnp.sum(cotangent * normal, 0), jnp.sum(cotangent, 0))


def swap(block):
    return lax.ppermute(block, "core", CORE_SWAP)


def pick(block, position, axis):
    return lax.dynamic_index_in_dim(block, position, axis, keepdims=False)


def exchange(block, axis, bit):
    size = lax.axis_size(axis)
    return lax.ppermute(block, axis, [(i, i ^ bit) for i in range(size)])


def half_steps(axis):
    steps = []
    bit = lax.axis_size(axis) // 2
    while bit:
        steps.append((axis, bit))
        bit //= 2
    return steps


def side(axis, bit):
    return (lax.axis_index(axis) // bit) % 2


def ordered(own, other, axis, bit):
    upper = side(axis, bit) == 1
    return jnp.where(upper, jnp.stack([other, own]), jnp.stack([own, other]))


class Gather:
    def __init__(self, block):
        self.dims = half_steps("chip") + [None] + half_steps("seq")
        self.tail = list(block.shape[1:])
        self.sizes = [2 if dim is None else 1 for dim in self.dims] + self.tail
        self.starts = [0 if dim is None else side(*dim) for dim in self.dims] + [0] * len(self.tail)
        buffer = jnp.zeros([2] * len(self.dims) + self.tail, block.dtype)
        self.held = lax.dynamic_update_slice(buffer, block.reshape(self.sizes), self.starts)

    def step(self, step):
        dim = self.dims.index(step)
        piece = exchange(lax.dynamic_slice(self.held, self.starts, self.sizes), *step)
        opposite = list(self.starts)
        opposite[dim] = 1 - self.starts[dim]
        self.held = lax.dynamic_update_slice(self.held, piece, opposite)
        self.starts[dim], self.sizes[dim] = 0, 2


class Held:
    def __init__(self, held):
        self.held = held


class Scatter:
    def __init__(self, total, whole_core=True):
        self.dims = half_steps("chip") + [None] * whole_core + half_steps("seq")
        shape = total.shape[3:] if whole_core else (-1,) + total.shape[1:]
        self.held = total.reshape([2] * len(self.dims) + list(shape))

    def step(self, step):
        dim = self.dims.index(step)
        mine = side(*step)
        sent = exchange(pick(self.held, 1 - mine, dim).astype(BF16), *step)
        self.held = pick(self.held, mine, dim) + sent.astype(F32)
        self.dims.pop(dim)


class Halve:
    def __init__(self, total, sent_as):
        self.held, self.sent_as = total, sent_as

    def step(self, step):
        half = self.held.reshape((2, self.held.shape[0] // 2) + self.held.shape[1:])
        mine = side(*step)
        sent = exchange(pick(half, 1 - mine, 0).astype(self.sent_as), *step)
        self.held = pick(half, mine, 0) + sent.astype(F32)


def together(chains):
    for chain, held in zip(chains, lax.optimization_barrier([chain.held for chain in chains])):
        chain.held = held


def all_to_all(block):
    return lax.all_to_all(block, "seq", split_axis=0, concat_axis=0, tiled=True)


def group_routes(count):
    size = lax.axis_size("seq")
    return [
        [(i, i // count * count + (i % count + step) % count) for i in range(size)]
        for step in range(1, count)
    ]


def group_sum(value, count):
    total = value
    for route in group_routes(count):
        total = total + lax.ppermute(value, "seq", route)
    return total


def group_max(value, count):
    total = value
    for route in group_routes(count):
        total = jnp.maximum(total, lax.ppermute(value, "seq", route))
    return total


def own_bias():
    own = jnp.arange(WINDOW)[:, None] == jnp.arange(PAIR)[None, :] + SPAN
    return jnp.where(own, -1e5, 0.0).astype(F32)


def pair_rows():
    return (jnp.arange(HEAD_DIM)[:, None] == jnp.arange(PAIR)[None, :] // SPAN).astype(BF16)


def flipped(value):
    return jnp.transpose(value.astype(F32)).astype(BF16)


def split_three(value):
    high = value.astype(BF16).astype(F32)
    rest = value - high
    middle = rest.astype(BF16).astype(F32)
    return high, middle, rest - middle


def in_lanes(columns, rows):
    lane = lax.broadcasted_iota(jnp.int32, (rows, 128), 1)
    out = jnp.zeros((rows, 128), F32)
    for k, column in enumerate(columns):
        out = jnp.where(lane == k, column, out)
    return out


def stacked_rows(rows):
    blank = jnp.zeros((128 - len(rows), 128), F32)
    return jnp.transpose(jnp.concatenate(rows + [blank], 0))


def pack_three(value, count):
    high, middle, low = split_three(value)
    return (high + pltpu.roll(middle, count, 1) + pltpu.roll(low, 2 * count, 1)).astype(BF16)


def sum_three(packed, count):
    return packed + pltpu.roll(packed, 128 - count, 1) + pltpu.roll(packed, 128 - 2 * count, 1)


def one_hot_rows(place_row, base, rows, tokens):
    slot = lax.broadcasted_iota(jnp.int32, (rows, tokens), 0) + base
    return jnp.where(slot == place_row, 1.0, 0.0).astype(BF16)


def one_hot_columns(place_column, rows, slots):
    slot = lax.broadcasted_iota(jnp.int32, (rows, slots), 1)
    return jnp.where(slot == place_column, 1.0, 0.0).astype(BF16)


def tile_rows(tokens):
    if tokens <= 1024:
        return 3 * tokens // 4, tokens // 2
    return 3 * SPAN, 128


def at_once(pairs, most):
    return most if pairs % most == 0 else 1


def aligned(start, rows):
    return pl.ds(pl.multiple_of(start, SPAN), rows)


def forward_kernel(
    heads, mixing, qv_ref, row_ref, column_ref, key_bias_ref, own_bias_ref, pair_row_ref,
    out_ref, spread_ref, mixed_ref, placed_ref, slot_spread_ref, result_ref
):
    this_round, rounds = pl.program_id(0), out_ref.shape[0]
    tokens = qv_ref.shape[0]
    slots = placed_ref.shape[1] - SPAN
    width = heads * HEAD_DIM
    place_rows, token_rows = tile_rows(tokens)
    placed_ref[0, 0:SPAN] = jnp.zeros((SPAN, 3 * width), BF16)

    def place(step, carry):
        base = pl.multiple_of(step * place_rows, place_rows)
        hot = one_hot_rows(row_ref[0], base, place_rows, tokens)
        rows = matmul(hot, qv_ref[...])
        where = pl.ds(pl.multiple_of(base + SPAN, SPAN), place_rows)
        placed_ref[0, where, 0 : 2 * width] = rows.astype(BF16)
        for head in range(heads):
            query = rows[:, head * HEAD_DIM : (head + 1) * HEAD_DIM]
            scale = lax.rsqrt(jnp.mean(query * query, -1, keepdims=True) + 1e-06)
            first = 2 * width + head * HEAD_DIM
            placed_ref[0, where, first : first + HEAD_DIM] = (query * (scale * (1.0 / HEAD_DIM))).astype(BF16)
        return carry

    lax.fori_loop(0, slots // place_rows, place, 0, unroll=2)

    pairs = slots // PAIR
    batch = at_once(pairs, FORWARD_PAIRS)
    lanes_of = [slice(head * HEAD_DIM, (head + 1) * HEAD_DIM) for head in range(heads)]

    def attend(step, carry):
        chains = [(step * batch + part, head) for part in range(batch) for head in range(heads)]
        bias, pair_row = own_bias_ref[...], pair_row_ref[...]
        scores = []
        for pair, head in chains:
            query = placed_ref[0, aligned(pair * PAIR + SPAN, PAIR), lanes_of[head]]
            keys = placed_ref[0, aligned(pair * PAIR, WINDOW), 2 * width + head * HEAD_DIM : 2 * width + (head + 1) * HEAD_DIM]
            left = jnp.concatenate([keys, key_bias_ref[0, pair]], 1)
            right = jnp.concatenate([flipped(query), pair_row], 0)
            scores.append(matmul(left, right) + bias)
        tops = [jnp.max(score, 0, keepdims=True) for score in scores]
        exponents = [jnp.exp(score - top) for score, top in zip(scores, tops)]
        sums = [jnp.sum(exponent, 0, keepdims=True) for exponent in exponents]
        spreads = [top + jnp.log(total) for top, total in zip(tops, sums)]
        for (pair, head), exponent, total in zip(chains, exponents, sums):
            values = placed_ref[0, aligned(pair * PAIR, WINDOW), width + head * HEAD_DIM : width + (head + 1) * HEAD_DIM]
            probability = jnp.transpose(exponent * (1.0 / total)).astype(BF16)
            result_ref[aligned(pair * PAIR, PAIR), lanes_of[head]] = matmul(probability, values).astype(BF16)
        for part in range(batch):
            pair, rows = step * batch + part, spreads[part * heads : (part + 1) * heads]
            slot_spread_ref[0, pair] = jnp.concatenate(rows + [jnp.zeros((8 - heads, 128), F32)], 0)
            terms = [split_three(row) for row in rows]
            packed = stacked_rows([term[k] for k in range(3) for term in terms])
            result_ref[aligned(pair * PAIR, PAIR), width : width + 128] = packed.astype(BF16)
        return carry

    lax.fori_loop(0, pairs // batch, attend, 0)

    def read_back(step, carry):
        where = pl.ds(pl.multiple_of(step * token_rows, token_rows), token_rows)
        hot = one_hot_columns(column_ref[0, where, :], token_rows, slots)
        rows = matmul(hot, result_ref[...])
        out_ref[this_round, where, :] = rows[:, :width].astype(BF16)
        spread_ref[this_round, where, :] = sum_three(rows[:, width:], heads)
        return carry

    lax.fori_loop(0, tokens // token_rows, read_back, 0, unroll=2)

    if mixing:

        @pl.when(this_round == rounds - 1)
        def _():
            def mix(step, carry):
                where = pl.ds(pl.multiple_of(step * 128, 128), 128)
                spreads = [spread_ref[r, where, :] for r in range(rounds)]
                top = functools.reduce(jnp.maximum, spreads)
                weights = [jnp.exp(spread - top) for spread in spreads]
                share = 1.0 / functools.reduce(jnp.add, weights)
                weights = [weight * share for weight in weights]
                for r in range(rounds):
                    spread_ref[r, where, :] = weights[r]
                for head in range(heads):
                    lanes = slice(head * HEAD_DIM, (head + 1) * HEAD_DIM)
                    total = functools.reduce(
                        jnp.add,
                        [
                            weights[r][:, head : head + 1] * out_ref[r, where, lanes].astype(F32)
                            for r in range(rounds)
                        ],
                    )
                    mixed_ref[where, lanes] = total.astype(BF16)
                return carry

            lax.fori_loop(0, tokens // 128, mix, 0, unroll=4)


def backward_kernel(
    heads, mixing, d_mixed_ref, out_ref, weight_ref, dot_ref, placed_ref, slot_spread_ref, row_ref,
    column_ref, key_bias_ref, own_bias_ref, pair_row_ref, total_ref, d_spread_ref, token_grad_ref, slot_grad_ref,
    d_place_ref, sum_ref
):
    if not mixing:
        sum_ref = total_ref
    this_round, rounds = pl.program_id(0), out_ref.shape[0]
    tokens = d_mixed_ref.shape[0]
    slots = placed_ref.shape[1] - SPAN
    width = heads * HEAD_DIM
    place_rows, token_rows = tile_rows(tokens)
    head_lanes = [slice(head * HEAD_DIM, (head + 1) * HEAD_DIM) for head in range(heads)]

    @pl.when(this_round == 0)
    def _():
        sum_ref[...] = jnp.zeros(sum_ref.shape, F32)

        def dots(step, carry):
            where = pl.ds(pl.multiple_of(step * 128, 128), 128)
            inner = []
            for r in range(rounds):
                columns = [
                    jnp.sum(
                        d_mixed_ref[where, lanes].astype(F32) * out_ref[r, where, lanes].astype(F32),
                        -1,
                        keepdims=True,
                    )
                    for lanes in head_lanes
                ]
                inner.append(in_lanes(columns, 128))
            if mixing:
                every = functools.reduce(
                    jnp.add, [weight_ref[r, where, :] * inner[r] for r in range(rounds)]
                )
            else:
                every = dot_ref[where, :]
            for r in range(rounds):
                d_spread_ref[r, where, :] = weight_ref[r, where, :] * (inner[r] - every)
            return carry

        lax.fori_loop(0, tokens // 128, dots, 0, unroll=4)


    def weigh(step, carry):
        where = pl.ds(pl.multiple_of(step * 128, 128), 128)
        for head, lanes in enumerate(head_lanes):
            share = weight_ref[this_round, where, head : head + 1]
            token_grad_ref[where, lanes] = (share * d_mixed_ref[where, lanes].astype(F32)).astype(BF16)
        token_grad_ref[where, width : width + 128] = pack_three(
            d_spread_ref[this_round, where, :], heads
        )
        return carry

    lax.fori_loop(0, tokens // 128, weigh, 0, unroll=4)

    def place(step, carry):
        base = pl.multiple_of(step * place_rows, place_rows)
        hot = one_hot_rows(row_ref[0], base, place_rows, tokens)
        slot_grad_ref[pl.ds(base, place_rows), :] = matmul(
            hot, token_grad_ref[...]
        ).astype(BF16)
        return carry

    lax.fori_loop(0, slots // place_rows, place, 0, unroll=2)

    pairs = slots // PAIR
    batch = at_once(pairs, BACKWARD_PAIRS)

    def finish(start, rows, head, d_query, d_unit, d_value):
        here = aligned(start + SPAN, rows)
        query = placed_ref[0, here, head_lanes[head]].astype(F32)
        scale = lax.rsqrt(jnp.mean(query * query, -1, keepdims=True) + 1e-06)
        inner = jnp.mean(d_unit * query, -1, keepdims=True)
        factor = scale * (1.0 / HEAD_DIM)
        d_query = d_query + factor * d_unit - query * (factor * scale * scale * inner)
        d_place_ref[here, head_lanes[head]] = d_query.astype(BF16)
        d_place_ref[here, width + head * HEAD_DIM : width + (head + 1) * HEAD_DIM] = d_value.astype(BF16)

    def attend(step, carry):
        chains = [(step * batch + part, head) for part in range(batch) for head in range(heads)]
        bias, pair_row = own_bias_ref[...], pair_row_ref[...]
        d_spread_rows = []
        for part in range(batch):
            packed = slot_grad_ref[aligned((step * batch + part) * PAIR, PAIR), width : width + 128]
            rows = jnp.transpose(packed.astype(F32))
            d_spread_rows += [
                rows[head : head + 1]
                + rows[heads + head : heads + head + 1]
                + rows[2 * heads + head : 2 * heads + head + 1]
                for head in range(heads)
            ]
        scores, d_probs = [], []
        for pair, head in chains:
            query = placed_ref[0, aligned(pair * PAIR + SPAN, PAIR), head_lanes[head]]
            keys = placed_ref[0, aligned(pair * PAIR, WINDOW), 2 * width + head * HEAD_DIM : 2 * width + (head + 1) * HEAD_DIM]
            values = placed_ref[0, aligned(pair * PAIR, WINDOW), width + head * HEAD_DIM : width + (head + 1) * HEAD_DIM]
            left = jnp.concatenate([keys, key_bias_ref[0, pair]], 1)
            right = jnp.concatenate([flipped(query), pair_row], 0)
            scores.append(matmul(left, right) + bias)
            d_out = slot_grad_ref[aligned(pair * PAIR, PAIR), head_lanes[head]]
            d_probs.append(matmul(values, flipped(d_out)))
        probs = [
            jnp.exp(score - slot_spread_ref[0, pair, head : head + 1, :])
            for (pair, head), score in zip(chains, scores)
        ]
        dots = [jnp.sum(p * d, 0, keepdims=True) for p, d in zip(probs, d_probs)]
        d_scores = [
            p * (d + (row - dot)) for p, d, row, dot in zip(probs, d_probs, d_spread_rows, dots)
        ]
        last = list(carry)
        for (pair, head), p, d in zip(chains, probs, d_scores):
            query = placed_ref[0, aligned(pair * PAIR + SPAN, PAIR), head_lanes[head]]
            keys = placed_ref[0, aligned(pair * PAIR, WINDOW), 2 * width + head * HEAD_DIM : 2 * width + (head + 1) * HEAD_DIM]
            d_out = slot_grad_ref[aligned(pair * PAIR, PAIR), head_lanes[head]]
            d_query = matmul(jnp.transpose(d).astype(BF16), keys)
            d_keys = matmul(d.astype(BF16), query)
            d_values = matmul(p.astype(BF16), d_out)
            last_query, last_key, last_value = last[head]

            before = pair * PAIR - SPAN
            finish(before, SPAN, head, last_query, last_key + d_keys[:SPAN], last_value + d_values[:SPAN])
            finish(pair * PAIR, SPAN, head, d_query[:SPAN], d_keys[SPAN:PAIR], d_values[SPAN:PAIR])
            last[head] = (d_query[SPAN:], d_keys[PAIR:], d_values[PAIR:])
        return tuple(last)

    blank = jnp.zeros((SPAN, HEAD_DIM), F32)
    carry = lax.fori_loop(
        0, pairs // batch, attend, tuple((blank, blank, blank) for _ in range(heads))
    )
    for head in range(heads):
        finish(slots - SPAN, SPAN, head, *carry[head])

    def read_back(step, carry):
        where = pl.ds(pl.multiple_of(step * token_rows, token_rows), token_rows)
        hot = one_hot_columns(column_ref[0, where, :], token_rows, slots)
        sum_ref[where, :] += matmul(hot, d_place_ref[SPAN:, :])
        return carry

    lax.fori_loop(0, tokens // token_rows, read_back, 0, unroll=2)

    if mixing:

        @pl.when(this_round == rounds - 1)
        def _():
            total_ref[...] = sum_ref[...].astype(BF16)


def per_round(shape, buffers):
    rest = (0,) * (len(shape) - 1)
    return pl.BlockSpec((1,) + shape[1:], lambda r: (r,) + rest, pipeline_mode=pl.Buffered(buffers))


def whole(shape):
    return pl.BlockSpec(shape, lambda r: (0,) * len(shape), pipeline_mode=pl.Buffered(1))


def attention_forward(qv, places, key_bias, mixing):
    row, column = places
    rounds, _, tokens = row.shape
    slots = key_bias.shape[1] * PAIR
    width = qv.shape[1] // 2
    heads = width // HEAD_DIM
    buffers = min(2, rounds)
    bias, pair_row = own_bias(), pair_rows()
    kept = [
        jax.ShapeDtypeStruct((rounds, tokens, width), BF16),
        jax.ShapeDtypeStruct((rounds, tokens, 128), F32),
        jax.ShapeDtypeStruct((tokens if mixing else 8, width), BF16),
    ]
    outs = [
        jax.ShapeDtypeStruct((rounds, slots + SPAN, 3 * width), BF16),
        jax.ShapeDtypeStruct((rounds, slots // PAIR, 8, PAIR), F32),
    ]
    flops = rounds * slots * (2 * tokens * (3 * width + 128) + 4 * width * WINDOW)
    return pl.pallas_call(
        functools.partial(forward_kernel, heads, mixing),
        grid=(rounds,),
        in_specs=[whole(qv.shape)]
        + [per_round(x.shape, buffers) for x in (row, column, key_bias)]
        + [whole(bias.shape), whole(pair_row.shape)],
        out_specs=[whole(x.shape) for x in kept] + [per_round(x.shape, buffers) for x in outs],
        out_shape=kept + outs,
        scratch_shapes=[pltpu.VMEM((slots, width + 128), BF16)],
        compiler_params=pltpu.CompilerParams(vmem_limit_bytes=56 * 1024 * 1024),
        cost_estimate=pl.CostEstimate(flops=flops, bytes_accessed=20 << 20, transcendentals=0),
    )(qv, row, column, key_bias, bias, pair_row)


def attention_backward(d_mixed, round_out, weights, all_dot, placed, slot_spread, places, key_bias):
    row, column = places
    rounds, _, tokens = row.shape
    slots = placed.shape[1] - SPAN
    width = placed.shape[2] // 3
    heads = width // HEAD_DIM
    buffers = min(2, rounds)
    bias, pair_row = own_bias(), pair_rows()
    mixing = all_dot is None
    if mixing:
        all_dot = jnp.zeros((8, 128), F32)
    flops = rounds * slots * (2 * tokens * (3 * width + 128) + 10 * width * WINDOW)
    return pl.pallas_call(
        functools.partial(backward_kernel, heads, mixing),
        grid=(rounds,),
        in_specs=[whole(x.shape) for x in (d_mixed, round_out, weights, all_dot)]
        + [per_round(x.shape, buffers) for x in (placed, slot_spread, row, column, key_bias)]
        + [whole(bias.shape), whole(pair_row.shape)],
        out_specs=whole((tokens, 2 * width)),
        out_shape=jax.ShapeDtypeStruct((tokens, 2 * width), BF16 if mixing else F32),
        scratch_shapes=[
            pltpu.VMEM((rounds, tokens, 128), F32),
            pltpu.VMEM((tokens, width + 128), BF16),
            pltpu.VMEM((slots, width + 128), BF16),
            pltpu.VMEM((slots + SPAN, 2 * width), BF16),
            pltpu.VMEM((tokens if mixing else 8, 2 * width), F32),
        ],
        compiler_params=pltpu.CompilerParams(vmem_limit_bytes=60 * 1024 * 1024),
        cost_estimate=pl.CostEstimate(flops=flops, bytes_accessed=20 << 20, transcendentals=0),
    )(d_mixed, round_out, weights, all_dot, placed, slot_spread, row, column, key_bias, bias, pair_row)


def local(
    stream_one,
    stream_two,
    slot_place,
    bucket_ids,
    grad_one,
    grad_two,
    norm1_gain,
    norm1_bias,
    w_query_key,
    w_value,
    w_output,
    norm2_gain,
    norm2_bias,
    w_inner,
    inner_bias,
    w_outer,
    outer_bias,
):
    chips, devices = lax.axis_size("chip"), lax.axis_size("seq")
    batch, tok, features = stream_one.shape
    rounds = slot_place.shape[1]
    sequences = 2 * batch
    tokens = devices * tok
    slots = 3 * tokens // 2
    own_rows = batch * tok
    width = features // (2 * chips)
    heads = width // HEAD_DIM
    at_call = min(heads, HEADS_AT_CALL)
    hidden_units = w_inner.shape[1]
    quarter = hidden_units // (2 * chips)
    units = sequences * chips
    sharing = devices // units
    mixing = sharing == 1
    own_rounds = rounds // sharing
    shard = w_query_key.shape[0]
    core, chip = lax.axis_index("core"), lax.axis_index("chip")

    def by_core(own, other):
        return jnp.where(core == 0, jnp.stack([own, other]), jnp.stack([other, own]))

    def flip(block):
        return exchange(block, "chip", 1)

    def both_chips(block):
        return ordered(block, flip(block), "chip", 1) if chips == 2 else block[None]

    def trade_quarters(pieces):
        if chips == 2:
            kept, sent = pick(pieces, chip, 0), pick(pieces, 1 - chip, 0)
            pieces = ordered(kept, flip(sent), "chip", 1)
        return jnp.swapaxes(by_core(pick(pieces, core, 1), swap(pick(pieces, 1 - core, 1))), 0, 1)

    seq_steps, chip_steps = half_steps("seq"), half_steps("chip")
    mid_steps = seq_steps[1:-1]
    gather_orders = [
        seq_steps[:1] + seq_steps[-1:] + mid_steps + chip_steps,
        chip_steps + seq_steps[:1] + seq_steps[-1:] + mid_steps,
    ]
    scatter_orders = [
        chip_steps + seq_steps[-1:] + mid_steps + seq_steps[:1],
        mid_steps + chip_steps + seq_steps[-1:] + seq_steps[:1],
    ]

    base = 64
    meta = jnp.stack([slot_place // base, slot_place % base, bucket_ids + 1], 1).astype(BF16)
    vectors = jnp.stack([norm1_gain, norm1_bias, norm2_gain, norm2_bias, outer_bias])
    small_rows = [meta.reshape(-1, tok)] + [
        jnp.pad(part, ((0, 0), (0, tok - part.shape[1]))) for part in (vectors, inner_bias[None])
    ]
    taken = [part.shape[0] for part in small_rows]
    fold = 2 * width // tok
    extra = 8 * (-(-sum(taken) // (8 * fold)))
    small = jnp.concatenate(
        small_rows + [jnp.zeros((extra * fold - sum(taken), tok), BF16)], 0
    )
    small = jnp.concatenate([small[k * extra : (k + 1) * extra] for k in range(fold)], 1)

    key_split = w_query_key.reshape(shard, chips, 2, heads, HEAD_DIM)
    value_split = w_value.reshape(shard, chips, 2, heads, HEAD_DIM)

    def pair_blocks(which):
        keys, values = pick(key_split, which, 2), pick(value_split, which, 2)
        blocks = [
            jnp.concatenate(
                [
                    part[:, pair, head]
                    for first in range(0, heads, at_call)
                    for part in (keys, values)
                    for head in range(first, first + at_call)
                ],
                1,
            )
            for pair in range(chips)
        ]
        return [jnp.concatenate([blocks[0], small], 0)] + blocks[1:]

    sent = jnp.concatenate(pair_blocks(1 - core), 0)
    streams, got = lax.optimization_barrier((stream_two.reshape(own_rows, features), swap(sent)))
    got = [got[: shard + extra]] + [
        got[extra + pair * shard : extra + (pair + 1) * shard] for pair in range(1, chips)
    ]
    chains = [Gather(by_core(own, other)) for own, other in zip(pair_blocks(core), got)]
    for k in range(len(seq_steps) + len(chip_steps)):
        for pair, chain in enumerate(chains):
            chain.step(gather_orders[pair % 2][k])
        together(chains)
    small = chains[0].held.reshape(-1, shard + extra, 2 * width)[:, shard:]
    small = jnp.concatenate([small[:, :, k * tok : (k + 1) * tok] for k in range(fold)], 1)
    joined = [chains[0].held.reshape(-1, shard + extra, 2 * width)[:, :shard]]
    joined = [part.reshape(features, 2 * width) for part in joined + [c.held for c in chains[1:]]]
    cuts = [taken[0], taken[0] + taken[1]]
    vectors = jnp.moveaxis(small[:, cuts[0] : cuts[1], :shard], 1, 0).reshape(taken[1], features)
    vectors = vectors.astype(F32)
    gain_one, bias_one, gain_two, bias_two, full_outer_bias = [vectors[k] for k in range(5)]
    by_place = small.reshape(chips, 2, devices, -1, tok)
    quarter_bias = lax.dynamic_slice(
        by_place, (chip, core, 0, cuts[1], 0), (1, 1, devices, 1, inner_bias.shape[0])
    )
    quarter_bias = quarter_bias.reshape(-1).astype(F32)
    meta = pick(by_place, chip, 0)[:, :, : cuts[0]]
    meta = jnp.swapaxes(meta, 0, 1).reshape(devices, 2, batch, 3, rounds, tok)

    inner_pieces = jnp.moveaxis(w_inner.reshape(shard, chips, 2, quarter), 0, 2)
    inner_pieces = trade_quarters(inner_pieces).reshape(-1, features)
    output_pieces = both_chips(w_output).reshape(-1, features)
    bundle = jnp.concatenate([w_outer, inner_pieces, output_pieces], 0)
    bundle, *joined = lax.optimization_barrier([bundle] + joined)
    grad_rows = w_outer.shape[0]
    cuts = [grad_rows, grad_rows + inner_pieces.shape[0]]
    gathered = lax.all_gather(bundle, "seq", axis=0, tiled=False)
    full_outer = gathered[:, : cuts[0]].reshape(quarter, features)
    full_inner = gathered[:, cuts[0] : cuts[1]].reshape(devices, 2 * chips, shard, quarter)
    full_inner = jnp.swapaxes(full_inner, 0, 1).reshape(features, quarter)
    full_output = gathered[:, cuts[1] :].reshape(devices, chips, shard, features)
    full_output = jnp.swapaxes(full_output, 0, 1).reshape(chips * width, features)

    unit = lax.axis_index("seq") // sharing
    sequence = unit // chips
    owner = jnp.where(sequence < batch, core, 1 - core)
    meta = lax.dynamic_slice(
        meta,
        (0, owner, sequence % batch, 0, lax.axis_index("seq") % sharing * own_rounds, 0),
        (devices, 1, 1, 3, own_rounds, tok),
    )
    meta = jnp.moveaxis(meta.reshape(devices, 3, own_rounds, tok), 0, 2)
    meta = meta.reshape(3, own_rounds, tokens).astype(jnp.int32)
    token_place, token_tag = meta[0] * base + meta[1], meta[2]
    found = token_place[:, :, None] == jnp.arange(slots)[None, None, :]
    slot_tag = jnp.sum(jnp.where(found, token_tag[:, :, None], 0), 1)
    slot_tag = jnp.pad(slot_tag.reshape(own_rounds, slots // SPAN, SPAN), ((0, 0), (1, 0), (0, 0)))
    span_tag = jnp.max(slot_tag, 2, keepdims=True)
    first, second, third = slot_tag[:, :-2:2], slot_tag[:, 1:-1:2], slot_tag[:, 2::2]
    unmet = jnp.full(first.shape, False)
    met = jnp.stack(
        [
            jnp.concatenate([first == span_tag[:, 1:-1:2], second == span_tag[:, 1:-1:2], unmet], 2),
            jnp.concatenate([unmet, second == span_tag[:, 2::2], third == span_tag[:, 2::2]], 2),
        ],
        3,
    )
    key_bias = jnp.where(met, 0.0, -1e9).astype(BF16)
    key_bias = jnp.pad(key_bias, ((0, 0), (0, 0), (0, 0), (0, HEAD_DIM - 2)))
    places = (token_place[:, None, :], token_place[:, :, None])

    def near(value):
        return jnp.concatenate([value, swap(value)], 0)

    def far(value):
        return near(flip(value))

    def everywhere(value):
        return jnp.concatenate([near(value), far(value)], 0) if chips == 2 else near(value)

    stream_a = stream_one.astype(F32).reshape(own_rows, features)
    stream_b = streams.astype(F32)
    normed_one, unit_one, scale_one = norm_parts(near(streams).astype(F32), gain_one, bias_one)
    hidden = normed_one.astype(BF16)
    unit_one, scale_one = unit_one[:own_rows], scale_one[:own_rows]
    projected = [matmul(hidden, weight).astype(BF16) for weight in joined]

    def to_attention(pairs):
        value = jnp.stack([pair.reshape(sequences, tok, -1) for pair in pairs], 1)
        value = jnp.broadcast_to(value[:, :, None], value.shape[:2] + (sharing,) + value.shape[2:])
        return all_to_all(value.reshape(devices, tok, -1)).reshape(tokens, -1)

    def from_attention(value):
        value = all_to_all(value.reshape(devices, tok, -1))
        value = value.reshape(sequences, chips, sharing, tok, -1)
        return [value[:, pair, 0].reshape(sequences * tok, -1) for pair in range(chips)]

    def by_heads(pairs, size):
        arrived = []
        for call in range(heads // at_call):
            parts = [pair[:, call * size : (call + 1) * size] for pair in pairs]
            if arrived:
                parts, arrived[-1] = lax.optimization_barrier((parts, arrived[-1]))
            arrived.append(to_attention(parts))
        return arrived

    def join_heads(parts):
        return [jnp.concatenate([part[pair] for part in parts], 1) for pair in range(chips)]

    kept, mixed = [], []
    for qv in by_heads(projected, 2 * at_call * HEAD_DIM):
        round_out, weights, head_mixed, placed, slot_spread = attention_forward(
            qv, places, key_bias, mixing
        )
        if not mixing:
            top = group_max(jnp.max(weights, 0), sharing)
            weights = jnp.exp(weights - top)
            weights = weights / group_sum(jnp.sum(weights, 0), sharing)
            by_head = round_out.reshape(own_rounds, tokens, at_call, HEAD_DIM)
            head_mixed = group_sum(jnp.sum(weights[:, :, :at_call, None] * by_head, 0), sharing)
            head_mixed = head_mixed.reshape(tokens, -1).astype(BF16)
        kept.append((round_out, weights, placed, slot_spread))
        mixed.append(from_attention(head_mixed))
    mixed = jnp.concatenate(join_heads(mixed), 1)
    cot_own = grad_two.reshape(own_rows, features)
    parts_cot = [near(cot_own)] + ([far(cot_own)] if chips == 2 else [])
    mixed, parts_cot = lax.optimization_barrier((mixed, parts_cot))

    def core_sum(value):
        return value[:own_rows] + swap(value[own_rows:])

    out_one = stream_a + core_sum(matmul(mixed, full_output))
    normed_two, unit_two, scale_two = norm_parts(out_one, gain_two, bias_two)
    inner_low = normed_two.astype(BF16)

    def feed_forward(value, cotangent):
        pre_act = matmul(value, full_inner) + quarter_bias
        activated, gelu_pull = jax.vjp(jax.nn.gelu, pre_act)
        act_low = activated.astype(BF16)
        d_act = matmul_right(cotangent, full_outer)
        d_pre = gelu_pull(d_act)[0].astype(BF16)
        return act_low, d_pre, matmul(act_low, full_outer), matmul_right(d_pre, full_inner)

    parts = [(near(inner_low), parts_cot[0])]
    done = [feed_forward(*parts[0])]
    if chips == 2:
        crossed, done[0] = lax.optimization_barrier((flip(inner_low), done[0]))
        parts.append((near(crossed), parts_cot[1]))
        done.append(feed_forward(*parts[1]))
    rows_in, rows_cot = [jnp.concatenate([part[k] for part in parts], 0) for k in range(2)]
    act_low, d_pre = [jnp.concatenate([part[k] for part in done], 0) for k in range(2)]

    grad_outer = matmul_left(act_low, rows_cot).astype(BF16)
    grad_inner = matmul_left(rows_in, d_pre).astype(BF16)
    grad_inner = jnp.swapaxes(grad_inner.reshape(2 * chips, devices, shard, quarter), 0, 1)
    summed = jnp.concatenate(
        [grad_outer.reshape(devices, -1, features), grad_inner.reshape(devices, -1, features)], 1
    )

    def quarter_sum(values):
        total = core_sum(values[0])
        if chips == 2:
            total = total + flip(core_sum(values[1]).astype(BF16)).astype(F32)
        return total

    d_normed_two = core_sum(done[0][3])
    if chips == 2:
        crossed, summed = lax.optimization_barrier((flip(core_sum(done[1][3]).astype(BF16)), summed))
        d_normed_two = d_normed_two + crossed.astype(F32)
    d_from_two, grad_gain_two, grad_bias_two = norm_back(
        d_normed_two, unit_two, scale_two, gain_two
    )
    back_one = grad_one.astype(F32).reshape(own_rows, features) + d_from_two
    out_two = stream_b + quarter_sum([part[2] for part in done]) + full_outer_bias

    d_attended = near(back_one.astype(BF16))
    d_mixed = matmul_right(d_attended, full_output).astype(BF16)
    d_mixed = by_heads([d_mixed[:, p * width : (p + 1) * width] for p in range(chips)], at_call * HEAD_DIM)

    reduced = Held(lax.psum_scatter(summed, "seq", scatter_dimension=0, tiled=True)[0])

    grad_output = Scatter(matmul_left(mixed, d_attended), whole_core=False)
    output_steps = scatter_orders[0][:]

    def beside(value, count):
        for _ in range(count):
            grad_output.step(output_steps.pop(0))
        grad_output.held, value = lax.optimization_barrier((grad_output.held, value))
        return value

    d_mixed[0] = beside(d_mixed[0], len(chip_steps))
    quarter_bias_grad = jnp.sum(d_pre.astype(F32), 0).reshape(devices, -1)

    d_projected = []
    for call, (round_out, weights, placed, slot_spread) in enumerate(kept):
        all_dot = None
        if not mixing:
            inner = d_mixed[call].astype(F32) * round_out.astype(F32)
            inner = jnp.sum(inner.reshape(own_rounds, tokens, at_call, HEAD_DIM), -1)
            inner = group_sum(jnp.sum(weights[:, :, :at_call] * inner, 0), sharing)
            all_dot = jnp.pad(inner, ((0, 0), (0, 128 - at_call)))
        d_total = attention_backward(
            d_mixed[call], round_out, weights, all_dot, placed, slot_spread, places, key_bias
        )
        d_total = beside(d_total, 1)
        if not mixing:
            d_total = group_sum(d_total, sharing).astype(BF16)
        d_projected.append(beside(from_attention(d_total), len(mid_steps)))
    d_projected = join_heads(d_projected)

    chains = []
    for pair in range(chips):
        grad = matmul_left(hidden, d_projected[pair])
        chains.append(Scatter(grad.reshape(chips, 2, devices, shard, 2 * width)))
    orders = list(zip(*[scatter_orders[pair % 2] for pair in range(chips)]))
    for chain, step in zip(chains, orders[0]):
        chain.step(step)
    d_hidden = core_sum(
        functools.reduce(jnp.add, [matmul_right(d, w) for d, w in zip(d_projected, joined)])
    )
    d_from_one, grad_gain_one, grad_bias_one = norm_back(d_hidden, unit_one, scale_one, gain_one)
    back_two = cot_own.astype(F32) + d_from_one
    small_grads = jnp.stack(
        [grad_gain_one, grad_bias_one, grad_gain_two, grad_bias_two, jnp.sum(cot_own.astype(F32), 0)]
    )
    small_grads = jnp.swapaxes(small_grads.reshape(5, 2 * chips * devices, shard), 0, 1)
    small_grads = Halve(small_grads.reshape(-1, 5 * shard), F32)
    small_steps = chip_steps + [("core", 1)] + seq_steps
    while output_steps:
        grad_output.step(output_steps.pop(0))
    for k in range(max(len(orders) - 1, len(small_steps))):
        together(chains + [small_grads] + [grad_output, reduced] * (k == TIE))
        if k + 1 < len(orders):
            for chain, step in zip(chains, orders[k + 1]):
                chain.step(step)
        elif k + 1 == len(orders):
            grad_joined = jnp.stack([chain.held for chain in chains], 1)
            grad_joined = by_core(pick(grad_joined, core, 0), swap(pick(grad_joined, 1 - core, 0)))
        if small_steps[k][0] == "seq" and small_grads.held.shape[1] == 5 * shard:
            small_grads.held = jnp.concatenate([small_grads.held, quarter_bias_grad], 1)
        small_grads.step(small_steps[k])
    summed = reduced.held
    grad_outer = summed[: grad_rows].astype(F32)
    grad_inner = trade_quarters(summed[grad_rows:].reshape(chips, 2, shard, quarter))
    grad_inner = jnp.moveaxis(grad_inner, 2, 0).reshape(shard, hidden_units).astype(F32)
    small_grads, grad_inner_bias = (
        small_grads.held[0, : 5 * shard].reshape(5, shard), small_grads.held[0, 5 * shard :]
    )
    grad_joined = grad_joined.reshape(2, chips, shard, heads // at_call, 2, at_call * HEAD_DIM)
    grad_joined = jnp.transpose(grad_joined, (4, 2, 1, 0, 3, 5)).reshape(2, shard, features)
    out_shape = (batch, tok, features)
    return (
        out_one.reshape(out_shape),
        out_two.reshape(out_shape),
        back_one.reshape(out_shape),
        back_two.reshape(out_shape),
        small_grads[0],
        small_grads[1],
        grad_joined[0],
        grad_joined[1],
        grad_output.held,
        small_grads[2],
        small_grads[3],
        grad_inner,
        grad_inner_bias,
        grad_outer,
        small_grads[4],
    )


def solution(mesh):
    split = Mesh(
        mesh.devices.reshape(mesh.shape["dp"] // 2, 2, mesh.shape["seq"]), ("chip", "core", "seq")
    )
    dp = ("chip", "core")
    every = ("chip", "core", "seq")
    stream, meta, vector, matrix = (
        P(dp, "seq", None), P(dp, None, "seq"), P(every), P(every, None)
    )
    return jax.shard_map(
        local,
        mesh=split,
        in_specs=(
            stream, stream, meta, meta, stream, stream,
            vector, vector, matrix, matrix, matrix, vector, vector, matrix, vector, matrix, vector,
        ),
        out_specs=(
            stream, stream, stream, stream,
            vector, vector, matrix, matrix, matrix, vector, vector, matrix, vector, matrix, vector,
        ),
        check_vma=False,
    )
```

```python
import functools

import jax
import jax.numpy as jnp
from jax import lax
from jax.experimental import pallas as pl
from jax.experimental.pallas import tpu as pltpu
from jax.sharding import Mesh, PartitionSpec as P

HEADS = 8
HEAD_DIM = 128
SPAN = 64
PAIR = 2 * SPAN
WINDOW = PAIR + SPAN
FORWARD_PAIRS = 12
BACKWARD_PAIRS = 12
HEADS_AT_CALL = 2
TIE = 0
F32 = jnp.float32
BF16 = jnp.bfloat16
CORE_SWAP = [(0, 1), (1, 0)]


def matmul(left, right):
    return jnp.dot(left, right, preferred_element_type=F32)


def matmul_left(left, right):
    return lax.dot_general(left, right, (((0,), (0,)), ((), ())), preferred_element_type=F32)


def matmul_right(left, right):
    return lax.dot_general(left, right, (((1,), (1,)), ((), ())), preferred_element_type=F32)


def norm_parts(value, gain, bias):
    row_mean = jnp.mean(value, -1, keepdims=True)
    centred = value - row_mean
    inv_scale = lax.rsqrt(jnp.mean(centred * centred, -1, keepdims=True) + 1e-05)
    normal = centred * inv_scale
    return (normal * gain + bias, normal, inv_scale)


def norm_back(cotangent, normal, inv_scale, gain):
    d_normal = cotangent * gain
    d_input = inv_scale * (
        d_normal
        - jnp.mean(d_normal, -1, keepdims=True)
        - normal * jnp.mean(d_normal * normal, -1, keepdims=True)
    )
    return (d_input, jnp.sum(cotangent * normal, 0), jnp.sum(cotangent, 0))


def swap(block):
    return lax.ppermute(block, "core", CORE_SWAP)


def pick(block, position, axis):
    return lax.dynamic_index_in_dim(block, position, axis, keepdims=False)


def exchange(block, axis, bit):
    size = lax.axis_size(axis)
    return lax.ppermute(block, axis, [(i, i ^ bit) for i in range(size)])


def half_steps(axis):
    steps = []
    bit = lax.axis_size(axis) // 2
    while bit:
        steps.append((axis, bit))
        bit //= 2
    return steps


def side(axis, bit):
    return (lax.axis_index(axis) // bit) % 2


def ordered(own, other, axis, bit):
    upper = side(axis, bit) == 1
    return jnp.where(upper, jnp.stack([other, own]), jnp.stack([own, other]))


class Gather:
    def __init__(self, block):
        self.dims = half_steps("chip") + [None] + half_steps("seq")
        self.tail = list(block.shape[1:])
        self.sizes = [2 if dim is None else 1 for dim in self.dims] + self.tail
        self.starts = [0 if dim is None else side(*dim) for dim in self.dims] + [0] * len(self.tail)
        buffer = jnp.zeros([2] * len(self.dims) + self.tail, block.dtype)
        self.held = lax.dynamic_update_slice(buffer, block.reshape(self.sizes), self.starts)

    def step(self, step):
        dim = self.dims.index(step)
        piece = exchange(lax.dynamic_slice(self.held, self.starts, self.sizes), *step)
        opposite = list(self.starts)
        opposite[dim] = 1 - self.starts[dim]
        self.held = lax.dynamic_update_slice(self.held, piece, opposite)
        self.starts[dim], self.sizes[dim] = 0, 2


class Held:
    def __init__(self, held):
        self.held = held


class Scatter:
    def __init__(self, total, whole_core=True):
        self.dims = half_steps("chip") + [None] * whole_core + half_steps("seq")
        shape = total.shape[3:] if whole_core else (-1,) + total.shape[1:]
        self.held = total.reshape([2] * len(self.dims) + list(shape))

    def step(self, step):
        dim = self.dims.index(step)
        mine = side(*step)
        sent = exchange(pick(self.held, 1 - mine, dim).astype(BF16), *step)
        self.held = pick(self.held, mine, dim) + sent.astype(F32)
        self.dims.pop(dim)


class Halve:
    def __init__(self, total, sent_as):
        self.held, self.sent_as = total, sent_as

    def step(self, step):
        half = self.held.reshape((2, self.held.shape[0] // 2) + self.held.shape[1:])
        mine = side(*step)
        sent = exchange(pick(half, 1 - mine, 0).astype(self.sent_as), *step)
        self.held = pick(half, mine, 0) + sent.astype(F32)


def together(chains):
    for chain, held in zip(chains, lax.optimization_barrier([chain.held for chain in chains])):
        chain.held = held


def all_to_all(block):
    return lax.all_to_all(block, "seq", split_axis=0, concat_axis=0, tiled=True)


def group_routes(count):
    size = lax.axis_size("seq")
    return [
        [(i, i // count * count + (i % count + step) % count) for i in range(size)]
        for step in range(1, count)
    ]


def group_sum(value, count):
    total = value
    for route in group_routes(count):
        total = total + lax.ppermute(value, "seq", route)
    return total


def group_max(value, count):
    total = value
    for route in group_routes(count):
        total = jnp.maximum(total, lax.ppermute(value, "seq", route))
    return total


def own_bias():
    own = jnp.arange(WINDOW)[:, None] == jnp.arange(PAIR)[None, :] + SPAN
    return jnp.where(own, -1e5, 0.0).astype(F32)


def pair_rows():
    return (jnp.arange(HEAD_DIM)[:, None] == jnp.arange(PAIR)[None, :] // SPAN).astype(BF16)


def flipped(value):
    return jnp.transpose(value.astype(F32)).astype(BF16)


def split_three(value):
    high = value.astype(BF16).astype(F32)
    rest = value - high
    middle = rest.astype(BF16).astype(F32)
    return high, middle, rest - middle


def in_lanes(columns, rows):
    lane = lax.broadcasted_iota(jnp.int32, (rows, 128), 1)
    out = jnp.zeros((rows, 128), F32)
    for k, column in enumerate(columns):
        out = jnp.where(lane == k, column, out)
    return out


def stacked_rows(rows):
    blank = jnp.zeros((128 - len(rows), 128), F32)
    return jnp.transpose(jnp.concatenate(rows + [blank], 0))


def pack_three(value, count):
    high, middle, low = split_three(value)
    return (high + pltpu.roll(middle, count, 1) + pltpu.roll(low, 2 * count, 1)).astype(BF16)


def sum_three(packed, count):
    return packed + pltpu.roll(packed, 128 - count, 1) + pltpu.roll(packed, 128 - 2 * count, 1)


def one_hot_rows(place_row, base, rows, tokens):
    slot = lax.broadcasted_iota(jnp.int32, (rows, tokens), 0) + base
    return jnp.where(slot == place_row, 1.0, 0.0).astype(BF16)


def one_hot_columns(place_column, rows, slots):
    slot = lax.broadcasted_iota(jnp.int32, (rows, slots), 1)
    return jnp.where(slot == place_column, 1.0, 0.0).astype(BF16)


def tile_rows(tokens):
    if tokens <= 1024:
        return 3 * tokens // 4, tokens // 2
    return 3 * SPAN, 128


def at_once(pairs, most):
    return most if pairs % most == 0 else 1


def aligned(start, rows):
    return pl.ds(pl.multiple_of(start, SPAN), rows)


def forward_kernel(
    heads, mixing, qv_ref, row_ref, column_ref, key_bias_ref, own_bias_ref, pair_row_ref,
    out_ref, spread_ref, mixed_ref, placed_ref, slot_spread_ref, result_ref
):
    this_round, rounds = pl.program_id(0), out_ref.shape[0]
    tokens = qv_ref.shape[0]
    slots = placed_ref.shape[1] - SPAN
    width = heads * HEAD_DIM
    place_rows, token_rows = tile_rows(tokens)
    placed_ref[0, 0:SPAN] = jnp.zeros((SPAN, 3 * width), BF16)

    def place(step, carry):
        base = pl.multiple_of(step * place_rows, place_rows)
        hot = one_hot_rows(row_ref[0], base, place_rows, tokens)
        rows = matmul(hot, qv_ref[...])
        where = pl.ds(pl.multiple_of(base + SPAN, SPAN), place_rows)
        placed_ref[0, where, 0 : 2 * width] = rows.astype(BF16)
        for head in range(heads):
            query = rows[:, head * HEAD_DIM : (head + 1) * HEAD_DIM]
            scale = lax.rsqrt(jnp.mean(query * query, -1, keepdims=True) + 1e-06)
            first = 2 * width + head * HEAD_DIM
            placed_ref[0, where, first : first + HEAD_DIM] = (query * (scale * (1.0 / HEAD_DIM))).astype(BF16)
        return carry

    lax.fori_loop(0, slots // place_rows, place, 0, unroll=2)

    pairs = slots // PAIR
    batch = at_once(pairs, FORWARD_PAIRS)
    lanes_of = [slice(head * HEAD_DIM, (head + 1) * HEAD_DIM) for head in range(heads)]

    def attend(step, carry):
        chains = [(step * batch + part, head) for part in range(batch) for head in range(heads)]
        bias, pair_row = own_bias_ref[...], pair_row_ref[...]
        scores = []
        for pair, head in chains:
            query = placed_ref[0, aligned(pair * PAIR + SPAN, PAIR), lanes_of[head]]
            keys = placed_ref[0, aligned(pair * PAIR, WINDOW), 2 * width + head * HEAD_DIM : 2 * width + (head + 1) * HEAD_DIM]
            left = jnp.concatenate([keys, key_bias_ref[0, pair]], 1)
            right = jnp.concatenate([flipped(query), pair_row], 0)
            scores.append(matmul(left, right) + bias)
        tops = [jnp.max(score, 0, keepdims=True) for score in scores]
        exponents = [jnp.exp(score - top) for score, top in zip(scores, tops)]
        sums = [jnp.sum(exponent, 0, keepdims=True) for exponent in exponents]
        spreads = [top + jnp.log(total) for top, total in zip(tops, sums)]
        for (pair, head), exponent, total in zip(chains, exponents, sums):
            values = placed_ref[0, aligned(pair * PAIR, WINDOW), width + head * HEAD_DIM : width + (head + 1) * HEAD_DIM]
            probability = jnp.transpose(exponent * (1.0 / total)).astype(BF16)
            result_ref[aligned(pair * PAIR, PAIR), lanes_of[head]] = matmul(probability, values).astype(BF16)
        for part in range(batch):
            pair, rows = step * batch + part, spreads[part * heads : (part + 1) * heads]
            slot_spread_ref[0, pair] = jnp.concatenate(rows + [jnp.zeros((8 - heads, 128), F32)], 0)
            terms = [split_three(row) for row in rows]
            packed = stacked_rows([term[k] for k in range(3) for term in terms])
            result_ref[aligned(pair * PAIR, PAIR), width : width + 128] = packed.astype(BF16)
        return carry

    lax.fori_loop(0, pairs // batch, attend, 0)

    def read_back(step, carry):
        where = pl.ds(pl.multiple_of(step * token_rows, token_rows), token_rows)
        hot = one_hot_columns(column_ref[0, where, :], token_rows, slots)
        rows = matmul(hot, result_ref[...])
        out_ref[this_round, where, :] = rows[:, :width].astype(BF16)
        spread_ref[this_round, where, :] = sum_three(rows[:, width:], heads)
        return carry

    lax.fori_loop(0, tokens // token_rows, read_back, 0, unroll=2)

    if mixing:

        @pl.when(this_round == rounds - 1)
        def _():
            def mix(step, carry):
                where = pl.ds(pl.multiple_of(step * 128, 128), 128)
                spreads = [spread_ref[r, where, :] for r in range(rounds)]
                top = functools.reduce(jnp.maximum, spreads)
                weights = [jnp.exp(spread - top) for spread in spreads]
                share = 1.0 / functools.reduce(jnp.add, weights)
                weights = [weight * share for weight in weights]
                for r in range(rounds):
                    spread_ref[r, where, :] = weights[r]
                for head in range(heads):
                    lanes = slice(head * HEAD_DIM, (head + 1) * HEAD_DIM)
                    total = functools.reduce(
                        jnp.add,
                        [
                            weights[r][:, head : head + 1] * out_ref[r, where, lanes].astype(F32)
                            for r in range(rounds)
                        ],
                    )
                    mixed_ref[where, lanes] = total.astype(BF16)
                return carry

            lax.fori_loop(0, tokens // 128, mix, 0, unroll=4)


def backward_kernel(
    heads, mixing, d_mixed_ref, out_ref, weight_ref, dot_ref, placed_ref, slot_spread_ref, row_ref,
    column_ref, key_bias_ref, own_bias_ref, pair_row_ref, total_ref, d_spread_ref, token_grad_ref, slot_grad_ref,
    d_place_ref, sum_ref
):
    if not mixing:
        sum_ref = total_ref
    this_round, rounds = pl.program_id(0), out_ref.shape[0]
    tokens = d_mixed_ref.shape[0]
    slots = placed_ref.shape[1] - SPAN
    width = heads * HEAD_DIM
    place_rows, token_rows = tile_rows(tokens)
    head_lanes = [slice(head * HEAD_DIM, (head + 1) * HEAD_DIM) for head in range(heads)]

    @pl.when(this_round == 0)
    def _():
        sum_ref[...] = jnp.zeros(sum_ref.shape, F32)

        def dots(step, carry):
            where = pl.ds(pl.multiple_of(step * 128, 128), 128)
            inner = []
            for r in range(rounds):
                columns = [
                    jnp.sum(
                        d_mixed_ref[where, lanes].astype(F32) * out_ref[r, where, lanes].astype(F32),
                        -1,
                        keepdims=True,
                    )
                    for lanes in head_lanes
                ]
                inner.append(in_lanes(columns, 128))
            if mixing:
                every = functools.reduce(
                    jnp.add, [weight_ref[r, where, :] * inner[r] for r in range(rounds)]
                )
            else:
                every = dot_ref[where, :]
            for r in range(rounds):
                d_spread_ref[r, where, :] = weight_ref[r, where, :] * (inner[r] - every)
            return carry

        lax.fori_loop(0, tokens // 128, dots, 0, unroll=4)


    def weigh(step, carry):
        where = pl.ds(pl.multiple_of(step * 128, 128), 128)
        for head, lanes in enumerate(head_lanes):
            share = weight_ref[this_round, where, head : head + 1]
            token_grad_ref[where, lanes] = (share * d_mixed_ref[where, lanes].astype(F32)).astype(BF16)
        token_grad_ref[where, width : width + 128] = pack_three(
            d_spread_ref[this_round, where, :], heads
        )
        return carry

    lax.fori_loop(0, tokens // 128, weigh, 0, unroll=4)

    def place(step, carry):
        base = pl.multiple_of(step * place_rows, place_rows)
        hot = one_hot_rows(row_ref[0], base, place_rows, tokens)
        slot_grad_ref[pl.ds(base, place_rows), :] = matmul(
            hot, token_grad_ref[...]
        ).astype(BF16)
        return carry

    lax.fori_loop(0, slots // place_rows, place, 0, unroll=2)

    pairs = slots // PAIR
    batch = at_once(pairs, BACKWARD_PAIRS)

    def finish(start, rows, head, d_query, d_unit, d_value):
        here = aligned(start + SPAN, rows)
        query = placed_ref[0, here, head_lanes[head]].astype(F32)
        scale = lax.rsqrt(jnp.mean(query * query, -1, keepdims=True) + 1e-06)
        inner = jnp.mean(d_unit * query, -1, keepdims=True)
        factor = scale * (1.0 / HEAD_DIM)
        d_query = d_query + factor * d_unit - query * (factor * scale * scale * inner)
        d_place_ref[here, head_lanes[head]] = d_query.astype(BF16)
        d_place_ref[here, width + head * HEAD_DIM : width + (head + 1) * HEAD_DIM] = d_value.astype(BF16)

    def attend(step, carry):
        chains = [(step * batch + part, head) for part in range(batch) for head in range(heads)]
        bias, pair_row = own_bias_ref[...], pair_row_ref[...]
        d_spread_rows = []
        for part in range(batch):
            packed = slot_grad_ref[aligned((step * batch + part) * PAIR, PAIR), width : width + 128]
            rows = jnp.transpose(packed.astype(F32))
            d_spread_rows += [
                rows[head : head + 1]
                + rows[heads + head : heads + head + 1]
                + rows[2 * heads + head : 2 * heads + head + 1]
                for head in range(heads)
            ]
        scores, d_probs = [], []
        for pair, head in chains:
            query = placed_ref[0, aligned(pair * PAIR + SPAN, PAIR), head_lanes[head]]
            keys = placed_ref[0, aligned(pair * PAIR, WINDOW), 2 * width + head * HEAD_DIM : 2 * width + (head + 1) * HEAD_DIM]
            values = placed_ref[0, aligned(pair * PAIR, WINDOW), width + head * HEAD_DIM : width + (head + 1) * HEAD_DIM]
            left = jnp.concatenate([keys, key_bias_ref[0, pair]], 1)
            right = jnp.concatenate([flipped(query), pair_row], 0)
            scores.append(matmul(left, right) + bias)
            d_out = slot_grad_ref[aligned(pair * PAIR, PAIR), head_lanes[head]]
            d_probs.append(matmul(values, flipped(d_out)))
        probs = [
            jnp.exp(score - slot_spread_ref[0, pair, head : head + 1, :])
            for (pair, head), score in zip(chains, scores)
        ]
        dots = [jnp.sum(p * d, 0, keepdims=True) for p, d in zip(probs, d_probs)]
        d_scores = [
            p * (d + (row - dot)) for p, d, row, dot in zip(probs, d_probs, d_spread_rows, dots)
        ]
        last = list(carry)
        for (pair, head), p, d in zip(chains, probs, d_scores):
            query = placed_ref[0, aligned(pair * PAIR + SPAN, PAIR), head_lanes[head]]
            keys = placed_ref[0, aligned(pair * PAIR, WINDOW), 2 * width + head * HEAD_DIM : 2 * width + (head + 1) * HEAD_DIM]
            d_out = slot_grad_ref[aligned(pair * PAIR, PAIR), head_lanes[head]]
            d_query = matmul(jnp.transpose(d).astype(BF16), keys)
            d_keys = matmul(d.astype(BF16), query)
            d_values = matmul(p.astype(BF16), d_out)
            last_query, last_key, last_value = last[head]

            before = pair * PAIR - SPAN
            finish(before, SPAN, head, last_query, last_key + d_keys[:SPAN], last_value + d_values[:SPAN])
            finish(pair * PAIR, SPAN, head, d_query[:SPAN], d_keys[SPAN:PAIR], d_values[SPAN:PAIR])
            last[head] = (d_query[SPAN:], d_keys[PAIR:], d_values[PAIR:])
        return tuple(last)

    blank = jnp.zeros((SPAN, HEAD_DIM), F32)
    carry = lax.fori_loop(
        0, pairs // batch, attend, tuple((blank, blank, blank) for _ in range(heads))
    )
    for head in range(heads):
        finish(slots - SPAN, SPAN, head, *carry[head])

    def read_back(step, carry):
        where = pl.ds(pl.multiple_of(step * token_rows, token_rows), token_rows)
        hot = one_hot_columns(column_ref[0, where, :], token_rows, slots)
        sum_ref[where, :] += matmul(hot, d_place_ref[SPAN:, :])
        return carry

    lax.fori_loop(0, tokens // token_rows, read_back, 0, unroll=2)

    if mixing:

        @pl.when(this_round == rounds - 1)
        def _():
            total_ref[...] = sum_ref[...].astype(BF16)


def per_round(shape, buffers):
    rest = (0,) * (len(shape) - 1)
    return pl.BlockSpec((1,) + shape[1:], lambda r: (r,) + rest, pipeline_mode=pl.Buffered(buffers))


def whole(shape):
    return pl.BlockSpec(shape, lambda r: (0,) * len(shape), pipeline_mode=pl.Buffered(1))


def attention_forward(qv, places, key_bias, mixing):
    row, column = places
    rounds, _, tokens = row.shape
    slots = key_bias.shape[1] * PAIR
    width = qv.shape[1] // 2
    heads = width // HEAD_DIM
    buffers = min(2, rounds)
    bias, pair_row = own_bias(), pair_rows()
    kept = [
        jax.ShapeDtypeStruct((rounds, tokens, width), BF16),
        jax.ShapeDtypeStruct((rounds, tokens, 128), F32),
        jax.ShapeDtypeStruct((tokens if mixing else 8, width), BF16),
    ]
    outs = [
        jax.ShapeDtypeStruct((rounds, slots + SPAN, 3 * width), BF16),
        jax.ShapeDtypeStruct((rounds, slots // PAIR, 8, PAIR), F32),
    ]
    flops = rounds * slots * (2 * tokens * (3 * width + 128) + 4 * width * WINDOW)
    return pl.pallas_call(
        functools.partial(forward_kernel, heads, mixing),
        grid=(rounds,),
        in_specs=[whole(qv.shape)]
        + [per_round(x.shape, buffers) for x in (row, column, key_bias)]
        + [whole(bias.shape), whole(pair_row.shape)],
        out_specs=[whole(x.shape) for x in kept] + [per_round(x.shape, buffers) for x in outs],
        out_shape=kept + outs,
        scratch_shapes=[pltpu.VMEM((slots, width + 128), BF16)],
        compiler_params=pltpu.CompilerParams(vmem_limit_bytes=56 * 1024 * 1024),
        cost_estimate=pl.CostEstimate(flops=flops, bytes_accessed=20 << 20, transcendentals=0),
    )(qv, row, column, key_bias, bias, pair_row)


def attention_backward(d_mixed, round_out, weights, all_dot, placed, slot_spread, places, key_bias):
    row, column = places
    rounds, _, tokens = row.shape
    slots = placed.shape[1] - SPAN
    width = placed.shape[2] // 3
    heads = width // HEAD_DIM
    buffers = min(2, rounds)
    bias, pair_row = own_bias(), pair_rows()
    mixing = all_dot is None
    if mixing:
        all_dot = jnp.zeros((8, 128), F32)
    flops = rounds * slots * (2 * tokens * (3 * width + 128) + 10 * width * WINDOW)
    return pl.pallas_call(
        functools.partial(backward_kernel, heads, mixing),
        grid=(rounds,),
        in_specs=[whole(x.shape) for x in (d_mixed, round_out, weights, all_dot)]
        + [per_round(x.shape, buffers) for x in (placed, slot_spread, row, column, key_bias)]
        + [whole(bias.shape), whole(pair_row.shape)],
        out_specs=whole((tokens, 2 * width)),
        out_shape=jax.ShapeDtypeStruct((tokens, 2 * width), BF16 if mixing else F32),
        scratch_shapes=[
            pltpu.VMEM((rounds, tokens, 128), F32),
            pltpu.VMEM((tokens, width + 128), BF16),
            pltpu.VMEM((slots, width + 128), BF16),
            pltpu.VMEM((slots + SPAN, 2 * width), BF16),
            pltpu.VMEM((tokens if mixing else 8, 2 * width), F32),
        ],
        compiler_params=pltpu.CompilerParams(vmem_limit_bytes=60 * 1024 * 1024),
        cost_estimate=pl.CostEstimate(flops=flops, bytes_accessed=20 << 20, transcendentals=0),
    )(d_mixed, round_out, weights, all_dot, placed, slot_spread, row, column, key_bias, bias, pair_row)


def local(
    stream_one,
    stream_two,
    slot_place,
    bucket_ids,
    grad_one,
    grad_two,
    norm1_gain,
    norm1_bias,
    w_query_key,
    w_value,
    w_output,
    norm2_gain,
    norm2_bias,
    w_inner,
    inner_bias,
    w_outer,
    outer_bias,
):
    chips, devices = lax.axis_size("chip"), lax.axis_size("seq")
    batch, tok, features = stream_one.shape
    rounds = slot_place.shape[1]
    sequences = 2 * batch
    tokens = devices * tok
    slots = 3 * tokens // 2
    own_rows = batch * tok
    width = features // (2 * chips)
    heads = width // HEAD_DIM
    at_call = min(heads, HEADS_AT_CALL)
    hidden_units = w_inner.shape[1]
    quarter = hidden_units // (2 * chips)
    units = sequences * chips
    sharing = devices // units
    mixing = sharing == 1
    own_rounds = rounds // sharing
    shard = w_query_key.shape[0]
    core, chip = lax.axis_index("core"), lax.axis_index("chip")

    def by_core(own, other):
        return jnp.where(core == 0, jnp.stack([own, other]), jnp.stack([other, own]))

    def flip(block):
        return exchange(block, "chip", 1)

    def both_chips(block):
        return ordered(block, flip(block), "chip", 1) if chips == 2 else block[None]

    def trade_quarters(pieces):
        if chips == 2:
            kept, sent = pick(pieces, chip, 0), pick(pieces, 1 - chip, 0)
            pieces = ordered(kept, flip(sent), "chip", 1)
        return jnp.swapaxes(by_core(pick(pieces, core, 1), swap(pick(pieces, 1 - core, 1))), 0, 1)

    seq_steps, chip_steps = half_steps("seq"), half_steps("chip")
    mid_steps = seq_steps[1:-1]
    gather_orders = [
        seq_steps[:1] + seq_steps[-1:] + mid_steps + chip_steps,
        chip_steps + seq_steps[:1] + seq_steps[-1:] + mid_steps,
    ]
    scatter_orders = [
        chip_steps + seq_steps[-1:] + mid_steps + seq_steps[:1],
        seq_steps[-1:] + chip_steps + mid_steps + seq_steps[:1],
    ]

    base = 64
    meta = jnp.stack([slot_place // base, slot_place % base, bucket_ids + 1], 1).astype(BF16)
    vectors = jnp.stack([norm1_gain, norm1_bias, norm2_gain, norm2_bias, outer_bias])
    small_rows = [meta.reshape(-1, tok)] + [
        jnp.pad(part, ((0, 0), (0, tok - part.shape[1]))) for part in (vectors, inner_bias[None])
    ]
    taken = [part.shape[0] for part in small_rows]
    fold = 2 * width // tok
    extra = 8 * (-(-sum(taken) // (8 * fold)))
    small = jnp.concatenate(
        small_rows + [jnp.zeros((extra * fold - sum(taken), tok), BF16)], 0
    )
    small = jnp.concatenate([small[k * extra : (k + 1) * extra] for k in range(fold)], 1)

    key_split = w_query_key.reshape(shard, chips, 2, heads, HEAD_DIM)
    value_split = w_value.reshape(shard, chips, 2, heads, HEAD_DIM)

    def pair_blocks(which):
        keys, values = pick(key_split, which, 2), pick(value_split, which, 2)
        blocks = [
            jnp.concatenate(
                [
                    part[:, pair, head]
                    for first in range(0, heads, at_call)
                    for part in (keys, values)
                    for head in range(first, first + at_call)
                ],
                1,
            )
            for pair in range(chips)
        ]
        return [jnp.concatenate([blocks[0], small], 0)] + blocks[1:]

    sent = jnp.concatenate(pair_blocks(1 - core), 0)
    streams, got = lax.optimization_barrier((stream_two.reshape(own_rows, features), swap(sent)))
    got = [got[: shard + extra]] + [
        got[extra + pair * shard : extra + (pair + 1) * shard] for pair in range(1, chips)
    ]
    chains = [Gather(by_core(own, other)) for own, other in zip(pair_blocks(core), got)]
    for k in range(len(seq_steps) + len(chip_steps)):
        for pair, chain in enumerate(chains):
            chain.step(gather_orders[pair % 2][k])
        together(chains)
    small = chains[0].held.reshape(-1, shard + extra, 2 * width)[:, shard:]
    small = jnp.concatenate([small[:, :, k * tok : (k + 1) * tok] for k in range(fold)], 1)
    joined = [chains[0].held.reshape(-1, shard + extra, 2 * width)[:, :shard]]
    joined = [part.reshape(features, 2 * width) for part in joined + [c.held for c in chains[1:]]]
    cuts = [taken[0], taken[0] + taken[1]]
    vectors = jnp.moveaxis(small[:, cuts[0] : cuts[1], :shard], 1, 0).reshape(taken[1], features)
    vectors = vectors.astype(F32)
    gain_one, bias_one, gain_two, bias_two, full_outer_bias = [vectors[k] for k in range(5)]
    by_place = small.reshape(chips, 2, devices, -1, tok)
    quarter_bias = lax.dynamic_slice(
        by_place, (chip, core, 0, cuts[1], 0), (1, 1, devices, 1, inner_bias.shape[0])
    )
    quarter_bias = quarter_bias.reshape(-1).astype(F32)
    meta = pick(by_place, chip, 0)[:, :, : cuts[0]]
    meta = jnp.swapaxes(meta, 0, 1).reshape(devices, 2, batch, 3, rounds, tok)

    inner_pieces = jnp.moveaxis(w_inner.reshape(shard, chips, 2, quarter), 0, 2)
    inner_pieces = trade_quarters(inner_pieces).reshape(-1, features)
    output_pieces = both_chips(w_output).reshape(-1, features)
    bundle = jnp.concatenate([w_outer, inner_pieces, output_pieces], 0)
    bundle, *joined = lax.optimization_barrier([bundle] + joined)
    grad_rows = w_outer.shape[0]
    cuts = [grad_rows, grad_rows + inner_pieces.shape[0]]
    gathered = lax.all_gather(bundle, "seq", axis=0, tiled=False)
    full_outer = gathered[:, : cuts[0]].reshape(quarter, features)
    full_inner = gathered[:, cuts[0] : cuts[1]].reshape(devices, 2 * chips, shard, quarter)
    full_inner = jnp.swapaxes(full_inner, 0, 1).reshape(features, quarter)
    full_output = gathered[:, cuts[1] :].reshape(devices, chips, shard, features)
    full_output = jnp.swapaxes(full_output, 0, 1).reshape(chips * width, features)

    unit = lax.axis_index("seq") // sharing
    sequence = unit // chips
    owner = jnp.where(sequence < batch, core, 1 - core)
    meta = lax.dynamic_slice(
        meta,
        (0, owner, sequence % batch, 0, lax.axis_index("seq") % sharing * own_rounds, 0),
        (devices, 1, 1, 3, own_rounds, tok),
    )
    meta = jnp.moveaxis(meta.reshape(devices, 3, own_rounds, tok), 0, 2)
    meta = meta.reshape(3, own_rounds, tokens).astype(jnp.int32)
    token_place, token_tag = meta[0] * base + meta[1], meta[2]
    found = token_place[:, :, None] == jnp.arange(slots)[None, None, :]
    slot_tag = jnp.sum(jnp.where(found, token_tag[:, :, None], 0), 1)
    slot_tag = jnp.pad(slot_tag.reshape(own_rounds, slots // SPAN, SPAN), ((0, 0), (1, 0), (0, 0)))
    span_tag = jnp.max(slot_tag, 2, keepdims=True)
    first, second, third = slot_tag[:, :-2:2], slot_tag[:, 1:-1:2], slot_tag[:, 2::2]
    unmet = jnp.full(first.shape, False)
    met = jnp.stack(
        [
            jnp.concatenate([first == span_tag[:, 1:-1:2], second == span_tag[:, 1:-1:2], unmet], 2),
            jnp.concatenate([unmet, second == span_tag[:, 2::2], third == span_tag[:, 2::2]], 2),
        ],
        3,
    )
    key_bias = jnp.where(met, 0.0, -1e9).astype(BF16)
    key_bias = jnp.pad(key_bias, ((0, 0), (0, 0), (0, 0), (0, HEAD_DIM - 2)))
    places = (token_place[:, None, :], token_place[:, :, None])

    def near(value):
        return jnp.concatenate([value, swap(value)], 0)

    def far(value):
        return near(flip(value))

    def everywhere(value):
        return jnp.concatenate([near(value), far(value)], 0) if chips == 2 else near(value)

    stream_a = stream_one.astype(F32).reshape(own_rows, features)
    stream_b = streams.astype(F32)
    normed_one, unit_one, scale_one = norm_parts(near(streams).astype(F32), gain_one, bias_one)
    hidden = normed_one.astype(BF16)
    unit_one, scale_one = unit_one[:own_rows], scale_one[:own_rows]
    projected = [matmul(hidden, weight).astype(BF16) for weight in joined]

    def to_attention(pairs):
        value = jnp.stack([pair.reshape(sequences, tok, -1) for pair in pairs], 1)
        value = jnp.broadcast_to(value[:, :, None], value.shape[:2] + (sharing,) + value.shape[2:])
        return all_to_all(value.reshape(devices, tok, -1)).reshape(tokens, -1)

    def from_attention(value):
        value = all_to_all(value.reshape(devices, tok, -1))
        value = value.reshape(sequences, chips, sharing, tok, -1)
        return [value[:, pair, 0].reshape(sequences * tok, -1) for pair in range(chips)]

    def by_heads(pairs, size):
        arrived = []
        for call in range(heads // at_call):
            parts = [pair[:, call * size : (call + 1) * size] for pair in pairs]
            if arrived:
                parts, arrived[-1] = lax.optimization_barrier((parts, arrived[-1]))
            arrived.append(to_attention(parts))
        return arrived

    def join_heads(parts):
        return [jnp.concatenate([part[pair] for part in parts], 1) for pair in range(chips)]

    kept, mixed = [], []
    for qv in by_heads(projected, 2 * at_call * HEAD_DIM):
        round_out, weights, head_mixed, placed, slot_spread = attention_forward(
            qv, places, key_bias, mixing
        )
        if not mixing:
            top = group_max(jnp.max(weights, 0), sharing)
            weights = jnp.exp(weights - top)
            weights = weights / group_sum(jnp.sum(weights, 0), sharing)
            by_head = round_out.reshape(own_rounds, tokens, at_call, HEAD_DIM)
            head_mixed = group_sum(jnp.sum(weights[:, :, :at_call, None] * by_head, 0), sharing)
            head_mixed = head_mixed.reshape(tokens, -1).astype(BF16)
        kept.append((round_out, weights, placed, slot_spread))
        mixed.append(from_attention(head_mixed))
    mixed = jnp.concatenate(join_heads(mixed), 1)
    cot_own = grad_two.reshape(own_rows, features)
    parts_cot = [near(cot_own)] + ([far(cot_own)] if chips == 2 else [])
    mixed, parts_cot = lax.optimization_barrier((mixed, parts_cot))

    def core_sum(value):
        return value[:own_rows] + swap(value[own_rows:])

    out_one = stream_a + core_sum(matmul(mixed, full_output))
    normed_two, unit_two, scale_two = norm_parts(out_one, gain_two, bias_two)
    inner_low = normed_two.astype(BF16)

    def feed_forward(value, cotangent):
        pre_act = matmul(value, full_inner) + quarter_bias
        activated, gelu_pull = jax.vjp(jax.nn.gelu, pre_act)
        act_low = activated.astype(BF16)
        d_act = matmul_right(cotangent, full_outer)
        d_pre = gelu_pull(d_act)[0].astype(BF16)
        return act_low, d_pre, matmul(act_low, full_outer), matmul_right(d_pre, full_inner)

    parts = [(near(inner_low), parts_cot[0])]
    done = [feed_forward(*parts[0])]
    if chips == 2:
        crossed, done[0] = lax.optimization_barrier((flip(inner_low), done[0]))
        parts.append((near(crossed), parts_cot[1]))
        done.append(feed_forward(*parts[1]))
    rows_in, rows_cot = [jnp.concatenate([part[k] for part in parts], 0) for k in range(2)]
    act_low, d_pre = [jnp.concatenate([part[k] for part in done], 0) for k in range(2)]

    grad_outer = matmul_left(act_low, rows_cot).astype(BF16)
    grad_inner = matmul_left(rows_in, d_pre).astype(BF16)
    grad_inner = jnp.swapaxes(grad_inner.reshape(2 * chips, devices, shard, quarter), 0, 1)
    summed = jnp.concatenate(
        [grad_outer.reshape(devices, -1, features), grad_inner.reshape(devices, -1, features)], 1
    )

    def quarter_sum(values):
        total = core_sum(values[0])
        if chips == 2:
            total = total + flip(core_sum(values[1]).astype(BF16)).astype(F32)
        return total

    d_normed_two = core_sum(done[0][3])
    if chips == 2:
        crossed, summed = lax.optimization_barrier((flip(core_sum(done[1][3]).astype(BF16)), summed))
        d_normed_two = d_normed_two + crossed.astype(F32)
    d_from_two, grad_gain_two, grad_bias_two = norm_back(
        d_normed_two, unit_two, scale_two, gain_two
    )
    back_one = grad_one.astype(F32).reshape(own_rows, features) + d_from_two
    out_two = stream_b + quarter_sum([part[2] for part in done]) + full_outer_bias

    d_attended = near(back_one.astype(BF16))
    d_mixed = matmul_right(d_attended, full_output).astype(BF16)
    d_mixed = by_heads([d_mixed[:, p * width : (p + 1) * width] for p in range(chips)], at_call * HEAD_DIM)

    reduced = Held(lax.psum_scatter(summed, "seq", scatter_dimension=0, tiled=True)[0])

    grad_output = Scatter(matmul_left(mixed, d_attended), whole_core=False)
    output_steps = scatter_orders[0][:]

    def beside(value, count):
        for _ in range(count):
            grad_output.step(output_steps.pop(0))
        grad_output.held, value = lax.optimization_barrier((grad_output.held, value))
        return value

    d_mixed[0] = beside(d_mixed[0], len(chip_steps))
    quarter_bias_grad = jnp.sum(d_pre.astype(F32), 0).reshape(devices, -1)

    d_projected = []
    for call, (round_out, weights, placed, slot_spread) in enumerate(kept):
        all_dot = None
        if not mixing:
            inner = d_mixed[call].astype(F32) * round_out.astype(F32)
            inner = jnp.sum(inner.reshape(own_rounds, tokens, at_call, HEAD_DIM), -1)
            inner = group_sum(jnp.sum(weights[:, :, :at_call] * inner, 0), sharing)
            all_dot = jnp.pad(inner, ((0, 0), (0, 128 - at_call)))
        d_total = attention_backward(
            d_mixed[call], round_out, weights, all_dot, placed, slot_spread, places, key_bias
        )
        d_total = beside(d_total, 1)
        if not mixing:
            d_total = group_sum(d_total, sharing).astype(BF16)
        d_projected.append(beside(from_attention(d_total), len(mid_steps)))
    d_projected = join_heads(d_projected)

    chains = []
    for pair in range(chips):
        grad = matmul_left(hidden, d_projected[pair])
        chains.append(Scatter(grad.reshape(chips, 2, devices, shard, 2 * width)))
    orders = list(zip(*[scatter_orders[pair % 2] for pair in range(chips)]))
    for chain, step in zip(chains, orders[0]):
        chain.step(step)
    d_hidden = core_sum(
        functools.reduce(jnp.add, [matmul_right(d, w) for d, w in zip(d_projected, joined)])
    )
    d_from_one, grad_gain_one, grad_bias_one = norm_back(d_hidden, unit_one, scale_one, gain_one)
    back_two = cot_own.astype(F32) + d_from_one
    small_grads = jnp.stack(
        [grad_gain_one, grad_bias_one, grad_gain_two, grad_bias_two, jnp.sum(cot_own.astype(F32), 0)]
    )
    small_grads = jnp.swapaxes(small_grads.reshape(5, 2 * chips * devices, shard), 0, 1)
    small_grads = Halve(small_grads.reshape(-1, 5 * shard), F32)
    small_steps = chip_steps + [("core", 1)] + seq_steps
    while output_steps:
        grad_output.step(output_steps.pop(0))
    for k in range(max(len(orders) - 1, len(small_steps))):
        held = [Held(d_from_one), reduced, small_grads] if k == 1 else []
        together(chains + ([grad_output, reduced] if k == 0 else held))
        if k == 1:
            back_two = cot_own.astype(F32) + held[0].held
        if k + 1 < len(orders):
            for chain, step in zip(chains, orders[k + 1]):
                chain.step(step)
        elif k + 1 == len(orders):
            grad_joined = jnp.stack([chain.held for chain in chains], 1)
            grad_joined = by_core(pick(grad_joined, core, 0), swap(pick(grad_joined, 1 - core, 0)))
        if small_steps[k][0] == "seq" and small_grads.held.shape[1] == 5 * shard:
            small_grads.held = jnp.concatenate([small_grads.held, quarter_bias_grad], 1)
        small_grads.step(small_steps[k])
    summed = reduced.held
    grad_outer = summed[: grad_rows].astype(F32)
    grad_inner = trade_quarters(summed[grad_rows:].reshape(chips, 2, shard, quarter))
    grad_inner = jnp.moveaxis(grad_inner, 2, 0).reshape(shard, hidden_units).astype(F32)
    small_grads, grad_inner_bias = (
        small_grads.held[0, : 5 * shard].reshape(5, shard), small_grads.held[0, 5 * shard :]
    )
    grad_joined = grad_joined.reshape(2, chips, shard, heads // at_call, 2, at_call * HEAD_DIM)
    grad_joined = jnp.transpose(grad_joined, (4, 2, 1, 0, 3, 5)).reshape(2, shard, features)
    out_shape = (batch, tok, features)
    return (
        out_one.reshape(out_shape),
        out_two.reshape(out_shape),
        back_one.reshape(out_shape),
        back_two.reshape(out_shape),
        small_grads[0],
        small_grads[1],
        grad_joined[0],
        grad_joined[1],
        grad_output.held,
        small_grads[2],
        small_grads[3],
        grad_inner,
        grad_inner_bias,
        grad_outer,
        small_grads[4],
    )


def solution(mesh):
    split = Mesh(
        mesh.devices.reshape(mesh.shape["dp"] // 2, 2, mesh.shape["seq"]), ("chip", "core", "seq")
    )
    dp = ("chip", "core")
    every = ("chip", "core", "seq")
    stream, meta, vector, matrix = (
        P(dp, "seq", None), P(dp, None, "seq"), P(every), P(every, None)
    )
    return jax.shard_map(
        local,
        mesh=split,
        in_specs=(
            stream, stream, meta, meta, stream, stream,
            vector, vector, matrix, matrix, matrix, vector, vector, matrix, vector, matrix, vector,
        ),
        out_specs=(
            stream, stream, stream, stream,
            vector, vector, matrix, matrix, matrix, vector, vector, matrix, vector, matrix, vector,
        ),
        check_vma=False,
    )
```

```python
import functools

import jax
import jax.numpy as jnp
from jax import lax
from jax.experimental import pallas as pl
from jax.experimental.pallas import tpu as pltpu
from jax.sharding import Mesh, PartitionSpec as P

HEADS = 8
HEAD_DIM = 128
SPAN = 64
PAIR = 2 * SPAN
WINDOW = PAIR + SPAN
FORWARD_PAIRS = 12
BACKWARD_PAIRS = 12
HEADS_AT_CALL = 2
TIE = 0
F32 = jnp.float32
BF16 = jnp.bfloat16
CORE_SWAP = [(0, 1), (1, 0)]


def matmul(left, right):
    return jnp.dot(left, right, preferred_element_type=F32)


def matmul_left(left, right):
    return lax.dot_general(left, right, (((0,), (0,)), ((), ())), preferred_element_type=F32)


def matmul_right(left, right):
    return lax.dot_general(left, right, (((1,), (1,)), ((), ())), preferred_element_type=F32)


def norm_parts(value, gain, bias):
    row_mean = jnp.mean(value, -1, keepdims=True)
    centred = value - row_mean
    inv_scale = lax.rsqrt(jnp.mean(centred * centred, -1, keepdims=True) + 1e-05)
    normal = centred * inv_scale
    return (normal * gain + bias, normal, inv_scale)


def norm_back(cotangent, normal, inv_scale, gain):
    d_normal = cotangent * gain
    d_input = inv_scale * (
        d_normal
        - jnp.mean(d_normal, -1, keepdims=True)
        - normal * jnp.mean(d_normal * normal, -1, keepdims=True)
    )
    return (d_input, jnp.sum(cotangent * normal, 0), jnp.sum(cotangent, 0))


def swap(block):
    return lax.ppermute(block, "core", CORE_SWAP)


def pick(block, position, axis):
    return lax.dynamic_index_in_dim(block, position, axis, keepdims=False)


def exchange(block, axis, bit):
    size = lax.axis_size(axis)
    return lax.ppermute(block, axis, [(i, i ^ bit) for i in range(size)])


def half_steps(axis):
    steps = []
    bit = lax.axis_size(axis) // 2
    while bit:
        steps.append((axis, bit))
        bit //= 2
    return steps


def side(axis, bit):
    return (lax.axis_index(axis) // bit) % 2


def ordered(own, other, axis, bit):
    upper = side(axis, bit) == 1
    return jnp.where(upper, jnp.stack([other, own]), jnp.stack([own, other]))


class Gather:
    def __init__(self, block, whole_core=True):
        self.dims = half_steps("chip") + [None] * whole_core + half_steps("seq")
        self.tail = list(block.shape[1:] if whole_core else block.shape)
        self.sizes = [2 if dim is None else 1 for dim in self.dims] + self.tail
        self.starts = [0 if dim is None else side(*dim) for dim in self.dims] + [0] * len(self.tail)
        buffer = jnp.zeros([2] * len(self.dims) + self.tail, block.dtype)
        self.held = lax.dynamic_update_slice(buffer, block.reshape(self.sizes), self.starts)

    def step(self, step):
        dim = self.dims.index(step)
        piece = exchange(lax.dynamic_slice(self.held, self.starts, self.sizes), *step)
        opposite = list(self.starts)
        opposite[dim] = 1 - self.starts[dim]
        self.held = lax.dynamic_update_slice(self.held, piece, opposite)
        self.starts[dim], self.sizes[dim] = 0, 2


class Held:
    def __init__(self, held):
        self.held = held


class Scatter:
    def __init__(self, total, whole_core=True):
        self.dims = half_steps("chip") + [None] * whole_core + half_steps("seq")
        shape = total.shape[3:] if whole_core else (-1,) + total.shape[1:]
        self.held = total.reshape([2] * len(self.dims) + list(shape))

    def step(self, step):
        dim = self.dims.index(step)
        mine = side(*step)
        sent = exchange(pick(self.held, 1 - mine, dim).astype(BF16), *step)
        self.held = pick(self.held, mine, dim) + sent.astype(F32)
        self.dims.pop(dim)


class Halve:
    def __init__(self, total, sent_as):
        self.held, self.sent_as = total, sent_as

    def step(self, step):
        half = self.held.reshape((2, self.held.shape[0] // 2) + self.held.shape[1:])
        mine = side(*step)
        sent = exchange(pick(half, 1 - mine, 0).astype(self.sent_as), *step)
        self.held = pick(half, mine, 0) + sent.astype(F32)


def together(chains):
    for chain, held in zip(chains, lax.optimization_barrier([chain.held for chain in chains])):
        chain.held = held


def all_to_all(block):
    return lax.all_to_all(block, "seq", split_axis=0, concat_axis=0, tiled=True)


def group_routes(count):
    size = lax.axis_size("seq")
    return [
        [(i, i // count * count + (i % count + step) % count) for i in range(size)]
        for step in range(1, count)
    ]


def group_sum(value, count):
    total = value
    for route in group_routes(count):
        total = total + lax.ppermute(value, "seq", route)
    return total


def group_max(value, count):
    total = value
    for route in group_routes(count):
        total = jnp.maximum(total, lax.ppermute(value, "seq", route))
    return total


def own_bias():
    own = jnp.arange(WINDOW)[:, None] == jnp.arange(PAIR)[None, :] + SPAN
    return jnp.where(own, -1e5, 0.0).astype(F32)


def pair_rows():
    return (jnp.arange(HEAD_DIM)[:, None] == jnp.arange(PAIR)[None, :] // SPAN).astype(BF16)


def flipped(value):
    return jnp.transpose(value.astype(F32)).astype(BF16)


def split_three(value):
    high = value.astype(BF16).astype(F32)
    rest = value - high
    middle = rest.astype(BF16).astype(F32)
    return high, middle, rest - middle


def in_lanes(columns, rows):
    lane = lax.broadcasted_iota(jnp.int32, (rows, 128), 1)
    out = jnp.zeros((rows, 128), F32)
    for k, column in enumerate(columns):
        out = jnp.where(lane == k, column, out)
    return out


def stacked_rows(rows):
    blank = jnp.zeros((128 - len(rows), 128), F32)
    return jnp.transpose(jnp.concatenate(rows + [blank], 0))


def pack_three(value, count):
    high, middle, low = split_three(value)
    return (high + pltpu.roll(middle, count, 1) + pltpu.roll(low, 2 * count, 1)).astype(BF16)


def sum_three(packed, count):
    return packed + pltpu.roll(packed, 128 - count, 1) + pltpu.roll(packed, 128 - 2 * count, 1)


def one_hot_rows(place_row, base, rows, tokens):
    slot = lax.broadcasted_iota(jnp.int32, (rows, tokens), 0) + base
    return jnp.where(slot == place_row, 1.0, 0.0).astype(BF16)


def one_hot_columns(place_column, rows, slots):
    slot = lax.broadcasted_iota(jnp.int32, (rows, slots), 1)
    return jnp.where(slot == place_column, 1.0, 0.0).astype(BF16)


def tile_rows(tokens):
    if tokens <= 1024:
        return 3 * tokens // 4, tokens // 2
    return 3 * SPAN, 128


def at_once(pairs, most):
    return most if pairs % most == 0 else 1


def aligned(start, rows):
    return pl.ds(pl.multiple_of(start, SPAN), rows)


def forward_kernel(
    heads, mixing, qv_ref, row_ref, column_ref, key_bias_ref, own_bias_ref, pair_row_ref,
    out_ref, spread_ref, mixed_ref, placed_ref, slot_spread_ref, result_ref
):
    this_round, rounds = pl.program_id(0), out_ref.shape[0]
    tokens = qv_ref.shape[0]
    slots = placed_ref.shape[1] - SPAN
    width = heads * HEAD_DIM
    place_rows, token_rows = tile_rows(tokens)
    placed_ref[0, 0:SPAN] = jnp.zeros((SPAN, 3 * width), BF16)

    def place(step, carry):
        base = pl.multiple_of(step * place_rows, place_rows)
        hot = one_hot_rows(row_ref[0], base, place_rows, tokens)
        rows = matmul(hot, qv_ref[...])
        where = pl.ds(pl.multiple_of(base + SPAN, SPAN), place_rows)
        placed_ref[0, where, 0 : 2 * width] = rows.astype(BF16)
        for head in range(heads):
            query = rows[:, head * HEAD_DIM : (head + 1) * HEAD_DIM]
            scale = lax.rsqrt(jnp.mean(query * query, -1, keepdims=True) + 1e-06)
            first = 2 * width + head * HEAD_DIM
            placed_ref[0, where, first : first + HEAD_DIM] = (query * (scale * (1.0 / HEAD_DIM))).astype(BF16)
        return carry

    lax.fori_loop(0, slots // place_rows, place, 0, unroll=2)

    pairs = slots // PAIR
    batch = at_once(pairs, FORWARD_PAIRS)
    lanes_of = [slice(head * HEAD_DIM, (head + 1) * HEAD_DIM) for head in range(heads)]

    def attend(step, carry):
        chains = [(step * batch + part, head) for part in range(batch) for head in range(heads)]
        bias, pair_row = own_bias_ref[...], pair_row_ref[...]
        scores = []
        for pair, head in chains:
            query = placed_ref[0, aligned(pair * PAIR + SPAN, PAIR), lanes_of[head]]
            keys = placed_ref[0, aligned(pair * PAIR, WINDOW), 2 * width + head * HEAD_DIM : 2 * width + (head + 1) * HEAD_DIM]
            left = jnp.concatenate([keys, key_bias_ref[0, pair]], 1)
            right = jnp.concatenate([flipped(query), pair_row], 0)
            scores.append(matmul(left, right) + bias)
        tops = [jnp.max(score, 0, keepdims=True) for score in scores]
        exponents = [jnp.exp(score - top) for score, top in zip(scores, tops)]
        sums = [jnp.sum(exponent, 0, keepdims=True) for exponent in exponents]
        spreads = [top + jnp.log(total) for top, total in zip(tops, sums)]
        for (pair, head), exponent, total in zip(chains, exponents, sums):
            values = placed_ref[0, aligned(pair * PAIR, WINDOW), width + head * HEAD_DIM : width + (head + 1) * HEAD_DIM]
            probability = jnp.transpose(exponent * (1.0 / total)).astype(BF16)
            result_ref[aligned(pair * PAIR, PAIR), lanes_of[head]] = matmul(probability, values).astype(BF16)
        for part in range(batch):
            pair, rows = step * batch + part, spreads[part * heads : (part + 1) * heads]
            slot_spread_ref[0, pair] = jnp.concatenate(rows + [jnp.zeros((8 - heads, 128), F32)], 0)
            terms = [split_three(row) for row in rows]
            packed = stacked_rows([term[k] for k in range(3) for term in terms])
            result_ref[aligned(pair * PAIR, PAIR), width : width + 128] = packed.astype(BF16)
        return carry

    lax.fori_loop(0, pairs // batch, attend, 0)

    def read_back(step, carry):
        where = pl.ds(pl.multiple_of(step * token_rows, token_rows), token_rows)
        hot = one_hot_columns(column_ref[0, where, :], token_rows, slots)
        rows = matmul(hot, result_ref[...])
        out_ref[this_round, where, :] = rows[:, :width].astype(BF16)
        spread_ref[this_round, where, :] = sum_three(rows[:, width:], heads)
        return carry

    lax.fori_loop(0, tokens // token_rows, read_back, 0, unroll=2)

    if mixing:

        @pl.when(this_round == rounds - 1)
        def _():
            def mix(step, carry):
                where = pl.ds(pl.multiple_of(step * 128, 128), 128)
                spreads = [spread_ref[r, where, :] for r in range(rounds)]
                top = functools.reduce(jnp.maximum, spreads)
                weights = [jnp.exp(spread - top) for spread in spreads]
                share = 1.0 / functools.reduce(jnp.add, weights)
                weights = [weight * share for weight in weights]
                for r in range(rounds):
                    spread_ref[r, where, :] = weights[r]
                for head in range(heads):
                    lanes = slice(head * HEAD_DIM, (head + 1) * HEAD_DIM)
                    total = functools.reduce(
                        jnp.add,
                        [
                            weights[r][:, head : head + 1] * out_ref[r, where, lanes].astype(F32)
                            for r in range(rounds)
                        ],
                    )
                    mixed_ref[where, lanes] = total.astype(BF16)
                return carry

            lax.fori_loop(0, tokens // 128, mix, 0, unroll=4)


def backward_kernel(
    heads, mixing, d_mixed_ref, out_ref, weight_ref, dot_ref, placed_ref, slot_spread_ref, row_ref,
    column_ref, key_bias_ref, own_bias_ref, pair_row_ref, total_ref, d_spread_ref, token_grad_ref, slot_grad_ref,
    d_place_ref, sum_ref
):
    if not mixing:
        sum_ref = total_ref
    this_round, rounds = pl.program_id(0), out_ref.shape[0]
    tokens = d_mixed_ref.shape[0]
    slots = placed_ref.shape[1] - SPAN
    width = heads * HEAD_DIM
    place_rows, token_rows = tile_rows(tokens)
    head_lanes = [slice(head * HEAD_DIM, (head + 1) * HEAD_DIM) for head in range(heads)]

    @pl.when(this_round == 0)
    def _():
        sum_ref[...] = jnp.zeros(sum_ref.shape, F32)

        def dots(step, carry):
            where = pl.ds(pl.multiple_of(step * 128, 128), 128)
            inner = []
            for r in range(rounds):
                columns = [
                    jnp.sum(
                        d_mixed_ref[where, lanes].astype(F32) * out_ref[r, where, lanes].astype(F32),
                        -1,
                        keepdims=True,
                    )
                    for lanes in head_lanes
                ]
                inner.append(in_lanes(columns, 128))
            if mixing:
                every = functools.reduce(
                    jnp.add, [weight_ref[r, where, :] * inner[r] for r in range(rounds)]
                )
            else:
                every = dot_ref[where, :]
            for r in range(rounds):
                d_spread_ref[r, where, :] = weight_ref[r, where, :] * (inner[r] - every)
            return carry

        lax.fori_loop(0, tokens // 128, dots, 0, unroll=4)


    def weigh(step, carry):
        where = pl.ds(pl.multiple_of(step * 128, 128), 128)
        for head, lanes in enumerate(head_lanes):
            share = weight_ref[this_round, where, head : head + 1]
            token_grad_ref[where, lanes] = (share * d_mixed_ref[where, lanes].astype(F32)).astype(BF16)
        token_grad_ref[where, width : width + 128] = pack_three(
            d_spread_ref[this_round, where, :], heads
        )
        return carry

    lax.fori_loop(0, tokens // 128, weigh, 0, unroll=4)

    def place(step, carry):
        base = pl.multiple_of(step * place_rows, place_rows)
        hot = one_hot_rows(row_ref[0], base, place_rows, tokens)
        slot_grad_ref[pl.ds(base, place_rows), :] = matmul(
            hot, token_grad_ref[...]
        ).astype(BF16)
        return carry

    lax.fori_loop(0, slots // place_rows, place, 0, unroll=2)

    pairs = slots // PAIR
    batch = at_once(pairs, BACKWARD_PAIRS)

    def finish(start, rows, head, d_query, d_unit, d_value):
        here = aligned(start + SPAN, rows)
        query = placed_ref[0, here, head_lanes[head]].astype(F32)
        scale = lax.rsqrt(jnp.mean(query * query, -1, keepdims=True) + 1e-06)
        inner = jnp.mean(d_unit * query, -1, keepdims=True)
        factor = scale * (1.0 / HEAD_DIM)
        d_query = d_query + factor * d_unit - query * (factor * scale * scale * inner)
        d_place_ref[here, head_lanes[head]] = d_query.astype(BF16)
        d_place_ref[here, width + head * HEAD_DIM : width + (head + 1) * HEAD_DIM] = d_value.astype(BF16)

    def attend(step, carry):
        chains = [(step * batch + part, head) for part in range(batch) for head in range(heads)]
        bias, pair_row = own_bias_ref[...], pair_row_ref[...]
        d_spread_rows = []
        for part in range(batch):
            packed = slot_grad_ref[aligned((step * batch + part) * PAIR, PAIR), width : width + 128]
            rows = jnp.transpose(packed.astype(F32))
            d_spread_rows += [
                rows[head : head + 1]
                + rows[heads + head : heads + head + 1]
                + rows[2 * heads + head : 2 * heads + head + 1]
                for head in range(heads)
            ]
        scores, d_probs = [], []
        for pair, head in chains:
            query = placed_ref[0, aligned(pair * PAIR + SPAN, PAIR), head_lanes[head]]
            keys = placed_ref[0, aligned(pair * PAIR, WINDOW), 2 * width + head * HEAD_DIM : 2 * width + (head + 1) * HEAD_DIM]
            values = placed_ref[0, aligned(pair * PAIR, WINDOW), width + head * HEAD_DIM : width + (head + 1) * HEAD_DIM]
            left = jnp.concatenate([keys, key_bias_ref[0, pair]], 1)
            right = jnp.concatenate([flipped(query), pair_row], 0)
            scores.append(matmul(left, right) + bias)
            d_out = slot_grad_ref[aligned(pair * PAIR, PAIR), head_lanes[head]]
            d_probs.append(matmul(values, flipped(d_out)))
        probs = [
            jnp.exp(score - slot_spread_ref[0, pair, head : head + 1, :])
            for (pair, head), score in zip(chains, scores)
        ]
        dots = [jnp.sum(p * d, 0, keepdims=True) for p, d in zip(probs, d_probs)]
        d_scores = [
            p * (d + (row - dot)) for p, d, row, dot in zip(probs, d_probs, d_spread_rows, dots)
        ]
        last = list(carry)
        for (pair, head), p, d in zip(chains, probs, d_scores):
            query = placed_ref[0, aligned(pair * PAIR + SPAN, PAIR), head_lanes[head]]
            keys = placed_ref[0, aligned(pair * PAIR, WINDOW), 2 * width + head * HEAD_DIM : 2 * width + (head + 1) * HEAD_DIM]
            d_out = slot_grad_ref[aligned(pair * PAIR, PAIR), head_lanes[head]]
            d_query = matmul(jnp.transpose(d).astype(BF16), keys)
            d_keys = matmul(d.astype(BF16), query)
            d_values = matmul(p.astype(BF16), d_out)
            last_query, last_key, last_value = last[head]

            before = pair * PAIR - SPAN
            finish(before, SPAN, head, last_query, last_key + d_keys[:SPAN], last_value + d_values[:SPAN])
            finish(pair * PAIR, SPAN, head, d_query[:SPAN], d_keys[SPAN:PAIR], d_values[SPAN:PAIR])
            last[head] = (d_query[SPAN:], d_keys[PAIR:], d_values[PAIR:])
        return tuple(last)

    blank = jnp.zeros((SPAN, HEAD_DIM), F32)
    carry = lax.fori_loop(
        0, pairs // batch, attend, tuple((blank, blank, blank) for _ in range(heads))
    )
    for head in range(heads):
        finish(slots - SPAN, SPAN, head, *carry[head])

    def read_back(step, carry):
        where = pl.ds(pl.multiple_of(step * token_rows, token_rows), token_rows)
        hot = one_hot_columns(column_ref[0, where, :], token_rows, slots)
        sum_ref[where, :] += matmul(hot, d_place_ref[SPAN:, :])
        return carry

    lax.fori_loop(0, tokens // token_rows, read_back, 0, unroll=2)

    if mixing:

        @pl.when(this_round == rounds - 1)
        def _():
            total_ref[...] = sum_ref[...].astype(BF16)


def per_round(shape, buffers):
    rest = (0,) * (len(shape) - 1)
    return pl.BlockSpec((1,) + shape[1:], lambda r: (r,) + rest, pipeline_mode=pl.Buffered(buffers))


def whole(shape):
    return pl.BlockSpec(shape, lambda r: (0,) * len(shape), pipeline_mode=pl.Buffered(1))


def attention_forward(qv, places, key_bias, mixing):
    row, column = places
    rounds, _, tokens = row.shape
    slots = key_bias.shape[1] * PAIR
    width = qv.shape[1] // 2
    heads = width // HEAD_DIM
    buffers = min(2, rounds)
    bias, pair_row = own_bias(), pair_rows()
    kept = [
        jax.ShapeDtypeStruct((rounds, tokens, width), BF16),
        jax.ShapeDtypeStruct((rounds, tokens, 128), F32),
        jax.ShapeDtypeStruct((tokens if mixing else 8, width), BF16),
    ]
    outs = [
        jax.ShapeDtypeStruct((rounds, slots + SPAN, 3 * width), BF16),
        jax.ShapeDtypeStruct((rounds, slots // PAIR, 8, PAIR), F32),
    ]
    flops = rounds * slots * (2 * tokens * (3 * width + 128) + 4 * width * WINDOW)
    return pl.pallas_call(
        functools.partial(forward_kernel, heads, mixing),
        grid=(rounds,),
        in_specs=[whole(qv.shape)]
        + [per_round(x.shape, buffers) for x in (row, column, key_bias)]
        + [whole(bias.shape), whole(pair_row.shape)],
        out_specs=[whole(x.shape) for x in kept] + [per_round(x.shape, buffers) for x in outs],
        out_shape=kept + outs,
        scratch_shapes=[pltpu.VMEM((slots, width + 128), BF16)],
        compiler_params=pltpu.CompilerParams(vmem_limit_bytes=56 * 1024 * 1024),
        cost_estimate=pl.CostEstimate(flops=flops, bytes_accessed=20 << 20, transcendentals=0),
    )(qv, row, column, key_bias, bias, pair_row)


def attention_backward(d_mixed, round_out, weights, all_dot, placed, slot_spread, places, key_bias):
    row, column = places
    rounds, _, tokens = row.shape
    slots = placed.shape[1] - SPAN
    width = placed.shape[2] // 3
    heads = width // HEAD_DIM
    buffers = min(2, rounds)
    bias, pair_row = own_bias(), pair_rows()
    mixing = all_dot is None
    if mixing:
        all_dot = jnp.zeros((8, 128), F32)
    flops = rounds * slots * (2 * tokens * (3 * width + 128) + 10 * width * WINDOW)
    return pl.pallas_call(
        functools.partial(backward_kernel, heads, mixing),
        grid=(rounds,),
        in_specs=[whole(x.shape) for x in (d_mixed, round_out, weights, all_dot)]
        + [per_round(x.shape, buffers) for x in (placed, slot_spread, row, column, key_bias)]
        + [whole(bias.shape), whole(pair_row.shape)],
        out_specs=whole((tokens, 2 * width)),
        out_shape=jax.ShapeDtypeStruct((tokens, 2 * width), BF16 if mixing else F32),
        scratch_shapes=[
            pltpu.VMEM((rounds, tokens, 128), F32),
            pltpu.VMEM((tokens, width + 128), BF16),
            pltpu.VMEM((slots, width + 128), BF16),
            pltpu.VMEM((slots + SPAN, 2 * width), BF16),
            pltpu.VMEM((tokens if mixing else 8, 2 * width), F32),
        ],
        compiler_params=pltpu.CompilerParams(vmem_limit_bytes=60 * 1024 * 1024),
        cost_estimate=pl.CostEstimate(flops=flops, bytes_accessed=20 << 20, transcendentals=0),
    )(d_mixed, round_out, weights, all_dot, placed, slot_spread, row, column, key_bias, bias, pair_row)


def local(
    stream_one,
    stream_two,
    slot_place,
    bucket_ids,
    grad_one,
    grad_two,
    norm1_gain,
    norm1_bias,
    w_query_key,
    w_value,
    w_output,
    norm2_gain,
    norm2_bias,
    w_inner,
    inner_bias,
    w_outer,
    outer_bias,
):
    chips, devices = lax.axis_size("chip"), lax.axis_size("seq")
    batch, tok, features = stream_one.shape
    rounds = slot_place.shape[1]
    sequences = 2 * batch
    tokens = devices * tok
    slots = 3 * tokens // 2
    own_rows = batch * tok
    width = features // (2 * chips)
    heads = width // HEAD_DIM
    at_call = min(heads, HEADS_AT_CALL)
    hidden_units = w_inner.shape[1]
    quarter = hidden_units // (2 * chips)
    units = sequences * chips
    sharing = devices // units
    mixing = sharing == 1
    own_rounds = rounds // sharing
    shard = w_query_key.shape[0]
    core, chip = lax.axis_index("core"), lax.axis_index("chip")

    def by_core(own, other):
        return jnp.where(core == 0, jnp.stack([own, other]), jnp.stack([other, own]))

    def flip(block):
        return exchange(block, "chip", 1)

    def both_chips(block):
        return ordered(block, flip(block), "chip", 1) if chips == 2 else block[None]

    def trade_quarters(pieces):
        if chips == 2:
            kept, sent = pick(pieces, chip, 0), pick(pieces, 1 - chip, 0)
            pieces = ordered(kept, flip(sent), "chip", 1)
        return jnp.swapaxes(by_core(pick(pieces, core, 1), swap(pick(pieces, 1 - core, 1))), 0, 1)

    seq_steps, chip_steps = half_steps("seq"), half_steps("chip")
    mid_steps = seq_steps[1:-1]
    gather_orders = [
        seq_steps[:1] + seq_steps[-1:] + mid_steps + chip_steps,
        chip_steps + seq_steps[:1] + seq_steps[-1:] + mid_steps,
    ]
    scatter_orders = [
        chip_steps + seq_steps[-1:] + mid_steps + seq_steps[:1],
        seq_steps[-1:] + chip_steps + mid_steps + seq_steps[:1],
    ]

    base = 64
    meta = jnp.stack([slot_place // base, slot_place % base, bucket_ids + 1], 1).astype(BF16)
    vectors = jnp.stack([norm1_gain, norm1_bias, norm2_gain, norm2_bias, outer_bias])
    small_rows = [meta.reshape(-1, tok)] + [
        jnp.pad(part, ((0, 0), (0, tok - part.shape[1]))) for part in (vectors, inner_bias[None])
    ]
    taken = [part.shape[0] for part in small_rows]
    fold = 2 * width // tok
    extra = 8 * (-(-sum(taken) // (8 * fold)))
    small = jnp.concatenate(
        small_rows + [jnp.zeros((extra * fold - sum(taken), tok), BF16)], 0
    )
    small = jnp.concatenate([small[k * extra : (k + 1) * extra] for k in range(fold)], 1)

    key_split = w_query_key.reshape(shard, chips, 2, heads, HEAD_DIM)
    value_split = w_value.reshape(shard, chips, 2, heads, HEAD_DIM)

    def pair_blocks(which):
        keys, values = pick(key_split, which, 2), pick(value_split, which, 2)
        blocks = [
            jnp.concatenate(
                [
                    part[:, pair, head]
                    for first in range(0, heads, at_call)
                    for part in (keys, values)
                    for head in range(first, first + at_call)
                ],
                1,
            )
            for pair in range(chips)
        ]
        return [jnp.concatenate([blocks[0], small], 0)] + blocks[1:]

    sent = jnp.concatenate(pair_blocks(1 - core), 0)
    streams, got = lax.optimization_barrier((stream_two.reshape(own_rows, features), swap(sent)))
    got = [got[: shard + extra]] + [
        got[extra + pair * shard : extra + (pair + 1) * shard] for pair in range(1, chips)
    ]
    chains = [Gather(by_core(own, other)) for own, other in zip(pair_blocks(core), got)]
    for k in range(len(seq_steps) + len(chip_steps)):
        for pair, chain in enumerate(chains):
            chain.step(gather_orders[pair % 2][k])
        later = [Held(w_inner)] if k == 0 else []
        together(chains + later)
        if later:
            w_inner = later[0].held
    small = chains[0].held.reshape(-1, shard + extra, 2 * width)[:, shard:]
    small = jnp.concatenate([small[:, :, k * tok : (k + 1) * tok] for k in range(fold)], 1)
    joined = [chains[0].held.reshape(-1, shard + extra, 2 * width)[:, :shard]]
    joined = [part.reshape(features, 2 * width) for part in joined + [c.held for c in chains[1:]]]
    cuts = [taken[0], taken[0] + taken[1]]
    vectors = jnp.moveaxis(small[:, cuts[0] : cuts[1], :shard], 1, 0).reshape(taken[1], features)
    vectors = vectors.astype(F32)
    gain_one, bias_one, gain_two, bias_two, full_outer_bias = [vectors[k] for k in range(5)]
    by_place = small.reshape(chips, 2, devices, -1, tok)
    quarter_bias = lax.dynamic_slice(
        by_place, (chip, core, 0, cuts[1], 0), (1, 1, devices, 1, inner_bias.shape[0])
    )
    quarter_bias = quarter_bias.reshape(-1).astype(F32)
    meta = pick(by_place, chip, 0)[:, :, : cuts[0]]
    meta = jnp.swapaxes(meta, 0, 1).reshape(devices, 2, batch, 3, rounds, tok)

    inner_pieces = jnp.moveaxis(w_inner.reshape(shard, chips, 2, quarter), 0, 2)
    inner_pieces = trade_quarters(inner_pieces).reshape(-1, features)
    bundle = jnp.concatenate([w_outer, inner_pieces], 0)
    bundle, *joined = lax.optimization_barrier([bundle] + joined)
    grad_rows = w_outer.shape[0]
    cuts = [grad_rows, grad_rows + inner_pieces.shape[0]]
    gathered = lax.all_gather(bundle, "seq", axis=0, tiled=False)
    full_outer = gathered[:, : cuts[0]].reshape(quarter, features)
    full_inner = gathered[:, cuts[0] : cuts[1]].reshape(devices, 2 * chips, shard, quarter)
    full_inner = jnp.swapaxes(full_inner, 0, 1).reshape(features, quarter)

    unit = lax.axis_index("seq") // sharing
    sequence = unit // chips
    owner = jnp.where(sequence < batch, core, 1 - core)
    meta = lax.dynamic_slice(
        meta,
        (0, owner, sequence % batch, 0, lax.axis_index("seq") % sharing * own_rounds, 0),
        (devices, 1, 1, 3, own_rounds, tok),
    )
    meta = jnp.moveaxis(meta.reshape(devices, 3, own_rounds, tok), 0, 2)
    meta = meta.reshape(3, own_rounds, tokens).astype(jnp.int32)
    token_place, token_tag = meta[0] * base + meta[1], meta[2]
    found = token_place[:, :, None] == jnp.arange(slots)[None, None, :]
    slot_tag = jnp.sum(jnp.where(found, token_tag[:, :, None], 0), 1)
    slot_tag = jnp.pad(slot_tag.reshape(own_rounds, slots // SPAN, SPAN), ((0, 0), (1, 0), (0, 0)))
    span_tag = jnp.max(slot_tag, 2, keepdims=True)
    first, second, third = slot_tag[:, :-2:2], slot_tag[:, 1:-1:2], slot_tag[:, 2::2]
    unmet = jnp.full(first.shape, False)
    met = jnp.stack(
        [
            jnp.concatenate([first == span_tag[:, 1:-1:2], second == span_tag[:, 1:-1:2], unmet], 2),
            jnp.concatenate([unmet, second == span_tag[:, 2::2], third == span_tag[:, 2::2]], 2),
        ],
        3,
    )
    key_bias = jnp.where(met, 0.0, -1e9).astype(BF16)
    key_bias = jnp.pad(key_bias, ((0, 0), (0, 0), (0, 0), (0, HEAD_DIM - 2)))
    places = (token_place[:, None, :], token_place[:, :, None])

    def near(value):
        return jnp.concatenate([value, swap(value)], 0)

    def far(value):
        return near(flip(value))

    def everywhere(value):
        return jnp.concatenate([near(value), far(value)], 0) if chips == 2 else near(value)

    stream_a = stream_one.astype(F32).reshape(own_rows, features)
    stream_b = streams.astype(F32)
    normed_one, unit_one, scale_one = norm_parts(near(streams).astype(F32), gain_one, bias_one)
    hidden = normed_one.astype(BF16)
    unit_one, scale_one = unit_one[:own_rows], scale_one[:own_rows]
    projected = [matmul(hidden, weight).astype(BF16) for weight in joined]

    def to_attention(pairs):
        value = jnp.stack([pair.reshape(sequences, tok, -1) for pair in pairs], 1)
        value = jnp.broadcast_to(value[:, :, None], value.shape[:2] + (sharing,) + value.shape[2:])
        return all_to_all(value.reshape(devices, tok, -1)).reshape(tokens, -1)

    def from_attention(value):
        value = all_to_all(value.reshape(devices, tok, -1))
        value = value.reshape(sequences, chips, sharing, tok, -1)
        return [value[:, pair, 0].reshape(sequences * tok, -1) for pair in range(chips)]

    def by_heads(pairs, size):
        arrived = []
        for call in range(heads // at_call):
            parts = [pair[:, call * size : (call + 1) * size] for pair in pairs]
            if arrived:
                parts, arrived[-1] = lax.optimization_barrier((parts, arrived[-1]))
            arrived.append(to_attention(parts))
        return arrived

    def join_heads(parts):
        return [jnp.concatenate([part[pair] for part in parts], 1) for pair in range(chips)]

    late_output, *projected = lax.optimization_barrier([w_output] + projected)
    output_weights = Gather(late_output, whole_core=False)
    arrived = by_heads(projected, 2 * at_call * HEAD_DIM)
    for step in seq_steps[:1] + seq_steps[-1:] + mid_steps:
        output_weights.step(step)
    output_weights.held, arrived[0] = lax.optimization_barrier((output_weights.held, arrived[0]))
    for step in chip_steps:
        output_weights.step(step)
    full_output = output_weights.held.reshape(chips * width, features)
    kept, mixed = [], []
    for qv in arrived:
        round_out, weights, head_mixed, placed, slot_spread = attention_forward(
            qv, places, key_bias, mixing
        )
        if not mixing:
            top = group_max(jnp.max(weights, 0), sharing)
            weights = jnp.exp(weights - top)
            weights = weights / group_sum(jnp.sum(weights, 0), sharing)
            by_head = round_out.reshape(own_rounds, tokens, at_call, HEAD_DIM)
            head_mixed = group_sum(jnp.sum(weights[:, :, :at_call, None] * by_head, 0), sharing)
            head_mixed = head_mixed.reshape(tokens, -1).astype(BF16)
        kept.append((round_out, weights, placed, slot_spread))
        mixed.append(from_attention(head_mixed))
    mixed = jnp.concatenate(join_heads(mixed), 1)
    cot_own = grad_two.reshape(own_rows, features)
    parts_cot = [near(cot_own)] + ([far(cot_own)] if chips == 2 else [])
    mixed, parts_cot, full_inner, full_outer = lax.optimization_barrier(
        (mixed, parts_cot, full_inner, full_outer)
    )

    def core_sum(value):
        return value[:own_rows] + swap(value[own_rows:])

    out_one = stream_a + core_sum(matmul(mixed, full_output))
    normed_two, unit_two, scale_two = norm_parts(out_one, gain_two, bias_two)
    inner_low = normed_two.astype(BF16)

    def feed_forward(value, cotangent):
        pre_act = matmul(value, full_inner) + quarter_bias
        activated, gelu_pull = jax.vjp(jax.nn.gelu, pre_act)
        act_low = activated.astype(BF16)
        d_act = matmul_right(cotangent, full_outer)
        d_pre = gelu_pull(d_act)[0].astype(BF16)
        return act_low, d_pre, matmul(act_low, full_outer), matmul_right(d_pre, full_inner)

    parts = [(near(inner_low), parts_cot[0])]
    done = [feed_forward(*parts[0])]
    if chips == 2:
        crossed, done[0] = lax.optimization_barrier((flip(inner_low), done[0]))
        parts.append((near(crossed), parts_cot[1]))
        done.append(feed_forward(*parts[1]))
    rows_in, rows_cot = [jnp.concatenate([part[k] for part in parts], 0) for k in range(2)]
    act_low, d_pre = [jnp.concatenate([part[k] for part in done], 0) for k in range(2)]

    grad_outer = matmul_left(act_low, rows_cot).astype(BF16)
    grad_inner = matmul_left(rows_in, d_pre).astype(BF16)
    grad_inner = jnp.swapaxes(grad_inner.reshape(2 * chips, devices, shard, quarter), 0, 1)
    summed = jnp.concatenate(
        [grad_outer.reshape(devices, -1, features), grad_inner.reshape(devices, -1, features)], 1
    )

    def quarter_sum(values):
        total = core_sum(values[0])
        if chips == 2:
            total = total + flip(core_sum(values[1]).astype(BF16)).astype(F32)
        return total

    d_normed_two = core_sum(done[0][3])
    if chips == 2:
        crossed, summed = lax.optimization_barrier((flip(core_sum(done[1][3]).astype(BF16)), summed))
        d_normed_two = d_normed_two + crossed.astype(F32)
    d_from_two, grad_gain_two, grad_bias_two = norm_back(
        d_normed_two, unit_two, scale_two, gain_two
    )
    back_one = grad_one.astype(F32).reshape(own_rows, features) + d_from_two
    out_two = stream_b + quarter_sum([part[2] for part in done]) + full_outer_bias

    d_attended = near(back_one.astype(BF16))
    d_mixed = matmul_right(d_attended, full_output).astype(BF16)
    d_mixed = by_heads([d_mixed[:, p * width : (p + 1) * width] for p in range(chips)], at_call * HEAD_DIM)

    reduced = Held(lax.psum_scatter(summed, "seq", scatter_dimension=0, tiled=True)[0])

    grad_output = Scatter(matmul_left(mixed, d_attended), whole_core=False)
    output_steps = scatter_orders[0][:]

    def beside(value, count):
        for _ in range(count):
            grad_output.step(output_steps.pop(0))
        grad_output.held, value = lax.optimization_barrier((grad_output.held, value))
        return value

    d_mixed[0] = beside(d_mixed[0], len(chip_steps))
    quarter_bias_grad = jnp.sum(d_pre.astype(F32), 0).reshape(devices, -1)

    d_projected = []
    for call, (round_out, weights, placed, slot_spread) in enumerate(kept):
        all_dot = None
        if not mixing:
            inner = d_mixed[call].astype(F32) * round_out.astype(F32)
            inner = jnp.sum(inner.reshape(own_rounds, tokens, at_call, HEAD_DIM), -1)
            inner = group_sum(jnp.sum(weights[:, :, :at_call] * inner, 0), sharing)
            all_dot = jnp.pad(inner, ((0, 0), (0, 128 - at_call)))
        d_total = attention_backward(
            d_mixed[call], round_out, weights, all_dot, placed, slot_spread, places, key_bias
        )
        d_total = beside(d_total, 1)
        if not mixing:
            d_total = group_sum(d_total, sharing).astype(BF16)
        d_projected.append(beside(from_attention(d_total), len(mid_steps)))
    d_projected = join_heads(d_projected)

    chains = []
    for pair in range(chips):
        grad = matmul_left(hidden, d_projected[pair])
        chains.append(Scatter(grad.reshape(chips, 2, devices, shard, 2 * width)))
    orders = list(zip(*[scatter_orders[pair % 2] for pair in range(chips)]))
    for chain, step in zip(chains, orders[0]):
        chain.step(step)
    d_hidden = core_sum(
        functools.reduce(jnp.add, [matmul_right(d, w) for d, w in zip(d_projected, joined)])
    )
    d_from_one, grad_gain_one, grad_bias_one = norm_back(d_hidden, unit_one, scale_one, gain_one)
    back_two = cot_own.astype(F32) + d_from_one
    small_grads = jnp.stack(
        [grad_gain_one, grad_bias_one, grad_gain_two, grad_bias_two, jnp.sum(cot_own.astype(F32), 0)]
    )
    small_grads = jnp.swapaxes(small_grads.reshape(5, 2 * chips * devices, shard), 0, 1)
    small_grads = Halve(small_grads.reshape(-1, 5 * shard), F32)
    small_steps = chip_steps + [("core", 1)] + seq_steps
    while output_steps:
        grad_output.step(output_steps.pop(0))
    for k in range(max(len(orders) - 1, len(small_steps))):
        held = [Held(d_from_one), reduced, small_grads] if k == 1 else []
        together(chains + ([grad_output, reduced] if k == 0 else held))
        if k == 1:
            back_two = cot_own.astype(F32) + held[0].held
        if k + 1 < len(orders):
            for chain, step in zip(chains, orders[k + 1]):
                chain.step(step)
        elif k + 1 == len(orders):
            grad_joined = jnp.stack([chain.held for chain in chains], 1)
            grad_joined = by_core(pick(grad_joined, core, 0), swap(pick(grad_joined, 1 - core, 0)))
        if small_steps[k][0] == "seq" and small_grads.held.shape[1] == 5 * shard:
            small_grads.held = jnp.concatenate([small_grads.held, quarter_bias_grad], 1)
        small_grads.step(small_steps[k])
    summed = reduced.held
    grad_outer = summed[: grad_rows].astype(F32)
    grad_inner = trade_quarters(summed[grad_rows:].reshape(chips, 2, shard, quarter))
    grad_inner = jnp.moveaxis(grad_inner, 2, 0).reshape(shard, hidden_units).astype(F32)
    small_grads, grad_inner_bias = (
        small_grads.held[0, : 5 * shard].reshape(5, shard), small_grads.held[0, 5 * shard :]
    )
    grad_joined = grad_joined.reshape(2, chips, shard, heads // at_call, 2, at_call * HEAD_DIM)
    grad_joined = jnp.transpose(grad_joined, (4, 2, 1, 0, 3, 5)).reshape(2, shard, features)
    out_shape = (batch, tok, features)
    return (
        out_one.reshape(out_shape),
        out_two.reshape(out_shape),
        back_one.reshape(out_shape),
        back_two.reshape(out_shape),
        small_grads[0],
        small_grads[1],
        grad_joined[0],
        grad_joined[1],
        grad_output.held,
        small_grads[2],
        small_grads[3],
        grad_inner,
        grad_inner_bias,
        grad_outer,
        small_grads[4],
    )


def solution(mesh):
    split = Mesh(
        mesh.devices.reshape(mesh.shape["dp"] // 2, 2, mesh.shape["seq"]), ("chip", "core", "seq")
    )
    dp = ("chip", "core")
    every = ("chip", "core", "seq")
    stream, meta, vector, matrix = (
        P(dp, "seq", None), P(dp, None, "seq"), P(every), P(every, None)
    )
    return jax.shard_map(
        local,
        mesh=split,
        in_specs=(
            stream, stream, meta, meta, stream, stream,
            vector, vector, matrix, matrix, matrix, vector, vector, matrix, vector, matrix, vector,
        ),
        out_specs=(
            stream, stream, stream, stream,
            vector, vector, matrix, matrix, matrix, vector, vector, matrix, vector, matrix, vector,
        ),
        check_vma=False,
    )
```

```python
import functools

import jax
import jax.numpy as jnp
from jax import lax
from jax.experimental import pallas as pl
from jax.experimental.pallas import tpu as pltpu
from jax.sharding import Mesh, PartitionSpec as P

HEADS = 8
HEAD_DIM = 128
SPAN = 64
PAIR = 2 * SPAN
WINDOW = PAIR + SPAN
FORWARD_PAIRS = 12
BACKWARD_PAIRS = 12
HEADS_AT_CALL = 2
TIE = 0
F32 = jnp.float32
BF16 = jnp.bfloat16
CORE_SWAP = [(0, 1), (1, 0)]


def matmul(left, right):
    return jnp.dot(left, right, preferred_element_type=F32)


def matmul_left(left, right):
    return lax.dot_general(left, right, (((0,), (0,)), ((), ())), preferred_element_type=F32)


def matmul_right(left, right):
    return lax.dot_general(left, right, (((1,), (1,)), ((), ())), preferred_element_type=F32)


def norm_parts(value, gain, bias):
    row_mean = jnp.mean(value, -1, keepdims=True)
    centred = value - row_mean
    inv_scale = lax.rsqrt(jnp.mean(centred * centred, -1, keepdims=True) + 1e-05)
    normal = centred * inv_scale
    return (normal * gain + bias, normal, inv_scale)


def norm_back(cotangent, normal, inv_scale, gain):
    d_normal = cotangent * gain
    d_input = inv_scale * (
        d_normal
        - jnp.mean(d_normal, -1, keepdims=True)
        - normal * jnp.mean(d_normal * normal, -1, keepdims=True)
    )
    return (d_input, jnp.sum(cotangent * normal, 0), jnp.sum(cotangent, 0))


def swap(block):
    return lax.ppermute(block, "core", CORE_SWAP)


def pick(block, position, axis):
    return lax.dynamic_index_in_dim(block, position, axis, keepdims=False)


def exchange(block, axis, bit):
    size = lax.axis_size(axis)
    return lax.ppermute(block, axis, [(i, i ^ bit) for i in range(size)])


def half_steps(axis):
    steps = []
    bit = lax.axis_size(axis) // 2
    while bit:
        steps.append((axis, bit))
        bit //= 2
    return steps


def side(axis, bit):
    return (lax.axis_index(axis) // bit) % 2


def ordered(own, other, axis, bit):
    upper = side(axis, bit) == 1
    return jnp.where(upper, jnp.stack([other, own]), jnp.stack([own, other]))


class Gather:
    def __init__(self, block, whole_core=True):
        self.dims = half_steps("chip") + [None] * whole_core + half_steps("seq")
        self.tail = list(block.shape[1:] if whole_core else block.shape)
        self.sizes = [2 if dim is None else 1 for dim in self.dims] + self.tail
        self.starts = [0 if dim is None else side(*dim) for dim in self.dims] + [0] * len(self.tail)
        buffer = jnp.zeros([2] * len(self.dims) + self.tail, block.dtype)
        self.held = lax.dynamic_update_slice(buffer, block.reshape(self.sizes), self.starts)

    def step(self, step):
        dim = self.dims.index(step)
        piece = exchange(lax.dynamic_slice(self.held, self.starts, self.sizes), *step)
        opposite = list(self.starts)
        opposite[dim] = 1 - self.starts[dim]
        self.held = lax.dynamic_update_slice(self.held, piece, opposite)
        self.starts[dim], self.sizes[dim] = 0, 2


class Held:
    def __init__(self, held):
        self.held = held


class Scatter:
    def __init__(self, total, whole_core=True):
        self.dims = half_steps("chip") + [None] * whole_core + half_steps("seq")
        shape = total.shape[3:] if whole_core else (-1,) + total.shape[1:]
        self.held = total.reshape([2] * len(self.dims) + list(shape))

    def step(self, step):
        dim = self.dims.index(step)
        mine = side(*step)
        sent = exchange(pick(self.held, 1 - mine, dim).astype(BF16), *step)
        self.held = pick(self.held, mine, dim) + sent.astype(F32)
        self.dims.pop(dim)


class Halve:
    def __init__(self, total, sent_as):
        self.held, self.sent_as = total, sent_as

    def step(self, step):
        half = self.held.reshape((2, self.held.shape[0] // 2) + self.held.shape[1:])
        mine = side(*step)
        sent = exchange(pick(half, 1 - mine, 0).astype(self.sent_as), *step)
        self.held = pick(half, mine, 0) + sent.astype(F32)


def together(chains):
    for chain, held in zip(chains, lax.optimization_barrier([chain.held for chain in chains])):
        chain.held = held


def all_to_all(block):
    return lax.all_to_all(block, "seq", split_axis=0, concat_axis=0, tiled=True)


def group_routes(count):
    size = lax.axis_size("seq")
    return [
        [(i, i // count * count + (i % count + step) % count) for i in range(size)]
        for step in range(1, count)
    ]


def group_sum(value, count):
    total = value
    for route in group_routes(count):
        total = total + lax.ppermute(value, "seq", route)
    return total


def group_max(value, count):
    total = value
    for route in group_routes(count):
        total = jnp.maximum(total, lax.ppermute(value, "seq", route))
    return total


def own_bias():
    own = jnp.arange(WINDOW)[:, None] == jnp.arange(PAIR)[None, :] + SPAN
    return jnp.where(own, -1e5, 0.0).astype(F32)


def pair_rows():
    return (jnp.arange(HEAD_DIM)[:, None] == jnp.arange(PAIR)[None, :] // SPAN).astype(BF16)


def flipped(value):
    return jnp.transpose(value.astype(F32)).astype(BF16)


def split_three(value):
    high = value.astype(BF16).astype(F32)
    rest = value - high
    middle = rest.astype(BF16).astype(F32)
    return high, middle, rest - middle


def in_lanes(columns, rows):
    lane = lax.broadcasted_iota(jnp.int32, (rows, 128), 1)
    out = jnp.zeros((rows, 128), F32)
    for k, column in enumerate(columns):
        out = jnp.where(lane == k, column, out)
    return out


def stacked_rows(rows):
    blank = jnp.zeros((128 - len(rows), 128), F32)
    return jnp.transpose(jnp.concatenate(rows + [blank], 0))


def pack_three(value, count):
    high, middle, low = split_three(value)
    return (high + pltpu.roll(middle, count, 1) + pltpu.roll(low, 2 * count, 1)).astype(BF16)


def sum_three(packed, count):
    return packed + pltpu.roll(packed, 128 - count, 1) + pltpu.roll(packed, 128 - 2 * count, 1)


def one_hot_rows(place_row, base, rows, tokens):
    slot = lax.broadcasted_iota(jnp.int32, (rows, tokens), 0) + base
    return jnp.where(slot == place_row, 1.0, 0.0).astype(BF16)


def one_hot_columns(place_column, rows, slots):
    slot = lax.broadcasted_iota(jnp.int32, (rows, slots), 1)
    return jnp.where(slot == place_column, 1.0, 0.0).astype(BF16)


def tile_rows(tokens):
    if tokens <= 1024:
        return 3 * tokens // 4, tokens // 2
    return 3 * SPAN, 128


def at_once(pairs, most):
    return most if pairs % most == 0 else 1


def aligned(start, rows):
    return pl.ds(pl.multiple_of(start, SPAN), rows)


def forward_kernel(
    heads, mixing, qv_ref, row_ref, column_ref, key_bias_ref, own_bias_ref, pair_row_ref,
    out_ref, spread_ref, mixed_ref, placed_ref, slot_spread_ref, result_ref
):
    this_round, rounds = pl.program_id(0), out_ref.shape[0]
    tokens = qv_ref.shape[0]
    slots = placed_ref.shape[1] - SPAN
    width = heads * HEAD_DIM
    place_rows, token_rows = tile_rows(tokens)
    placed_ref[0, 0:SPAN] = jnp.zeros((SPAN, 3 * width), BF16)

    def place(step, carry):
        base = pl.multiple_of(step * place_rows, place_rows)
        hot = one_hot_rows(row_ref[0], base, place_rows, tokens)
        rows = matmul(hot, qv_ref[...])
        where = pl.ds(pl.multiple_of(base + SPAN, SPAN), place_rows)
        placed_ref[0, where, 0 : 2 * width] = rows.astype(BF16)
        for head in range(heads):
            query = rows[:, head * HEAD_DIM : (head + 1) * HEAD_DIM]
            scale = lax.rsqrt(jnp.mean(query * query, -1, keepdims=True) + 1e-06)
            first = 2 * width + head * HEAD_DIM
            placed_ref[0, where, first : first + HEAD_DIM] = (query * (scale * (1.0 / HEAD_DIM))).astype(BF16)
        return carry

    lax.fori_loop(0, slots // place_rows, place, 0, unroll=2)

    pairs = slots // PAIR
    batch = at_once(pairs, FORWARD_PAIRS)
    lanes_of = [slice(head * HEAD_DIM, (head + 1) * HEAD_DIM) for head in range(heads)]

    def attend(step, carry):
        chains = [(step * batch + part, head) for part in range(batch) for head in range(heads)]
        bias, pair_row = own_bias_ref[...], pair_row_ref[...]
        scores = []
        for pair, head in chains:
            query = placed_ref[0, aligned(pair * PAIR + SPAN, PAIR), lanes_of[head]]
            keys = placed_ref[0, aligned(pair * PAIR, WINDOW), 2 * width + head * HEAD_DIM : 2 * width + (head + 1) * HEAD_DIM]
            left = jnp.concatenate([keys, key_bias_ref[0, pair]], 1)
            right = jnp.concatenate([flipped(query), pair_row], 0)
            scores.append(matmul(left, right) + bias)
        tops = [jnp.max(score, 0, keepdims=True) for score in scores]
        exponents = [jnp.exp(score - top) for score, top in zip(scores, tops)]
        sums = [jnp.sum(exponent, 0, keepdims=True) for exponent in exponents]
        spreads = [top + jnp.log(total) for top, total in zip(tops, sums)]
        for (pair, head), exponent, total in zip(chains, exponents, sums):
            values = placed_ref[0, aligned(pair * PAIR, WINDOW), width + head * HEAD_DIM : width + (head + 1) * HEAD_DIM]
            probability = jnp.transpose(exponent * (1.0 / total)).astype(BF16)
            result_ref[aligned(pair * PAIR, PAIR), lanes_of[head]] = matmul(probability, values).astype(BF16)
        for part in range(batch):
            pair, rows = step * batch + part, spreads[part * heads : (part + 1) * heads]
            slot_spread_ref[0, pair] = jnp.concatenate(rows + [jnp.zeros((8 - heads, 128), F32)], 0)
            terms = [split_three(row) for row in rows]
            packed = stacked_rows([term[k] for k in range(3) for term in terms])
            result_ref[aligned(pair * PAIR, PAIR), width : width + 128] = packed.astype(BF16)
        return carry

    lax.fori_loop(0, pairs // batch, attend, 0)

    def read_back(step, carry):
        where = pl.ds(pl.multiple_of(step * token_rows, token_rows), token_rows)
        hot = one_hot_columns(column_ref[0, where, :], token_rows, slots)
        rows = matmul(hot, result_ref[...])
        out_ref[this_round, where, :] = rows[:, :width].astype(BF16)
        spread_ref[this_round, where, :] = sum_three(rows[:, width:], heads)
        return carry

    lax.fori_loop(0, tokens // token_rows, read_back, 0, unroll=2)

    if mixing:

        @pl.when(this_round == rounds - 1)
        def _():
            def mix(step, carry):
                where = pl.ds(pl.multiple_of(step * 128, 128), 128)
                spreads = [spread_ref[r, where, :] for r in range(rounds)]
                top = functools.reduce(jnp.maximum, spreads)
                weights = [jnp.exp(spread - top) for spread in spreads]
                share = 1.0 / functools.reduce(jnp.add, weights)
                weights = [weight * share for weight in weights]
                for r in range(rounds):
                    spread_ref[r, where, :] = weights[r]
                for head in range(heads):
                    lanes = slice(head * HEAD_DIM, (head + 1) * HEAD_DIM)
                    total = functools.reduce(
                        jnp.add,
                        [
                            weights[r][:, head : head + 1] * out_ref[r, where, lanes].astype(F32)
                            for r in range(rounds)
                        ],
                    )
                    mixed_ref[where, lanes] = total.astype(BF16)
                return carry

            lax.fori_loop(0, tokens // 128, mix, 0, unroll=4)


def backward_kernel(
    heads, mixing, d_mixed_ref, out_ref, weight_ref, dot_ref, placed_ref, slot_spread_ref, row_ref,
    column_ref, key_bias_ref, own_bias_ref, pair_row_ref, total_ref, d_spread_ref, token_grad_ref, slot_grad_ref,
    d_place_ref, sum_ref
):
    if not mixing:
        sum_ref = total_ref
    this_round, rounds = pl.program_id(0), out_ref.shape[0]
    tokens = d_mixed_ref.shape[0]
    slots = placed_ref.shape[1] - SPAN
    width = heads * HEAD_DIM
    place_rows, token_rows = tile_rows(tokens)
    head_lanes = [slice(head * HEAD_DIM, (head + 1) * HEAD_DIM) for head in range(heads)]

    @pl.when(this_round == 0)
    def _():
        sum_ref[...] = jnp.zeros(sum_ref.shape, F32)

        def dots(step, carry):
            where = pl.ds(pl.multiple_of(step * 128, 128), 128)
            inner = []
            for r in range(rounds):
                columns = [
                    jnp.sum(
                        d_mixed_ref[where, lanes].astype(F32) * out_ref[r, where, lanes].astype(F32),
                        -1,
                        keepdims=True,
                    )
                    for lanes in head_lanes
                ]
                inner.append(in_lanes(columns, 128))
            if mixing:
                every = functools.reduce(
                    jnp.add, [weight_ref[r, where, :] * inner[r] for r in range(rounds)]
                )
            else:
                every = dot_ref[where, :]
            for r in range(rounds):
                d_spread_ref[r, where, :] = weight_ref[r, where, :] * (inner[r] - every)
            return carry

        lax.fori_loop(0, tokens // 128, dots, 0, unroll=4)


    def weigh(step, carry):
        where = pl.ds(pl.multiple_of(step * 128, 128), 128)
        for head, lanes in enumerate(head_lanes):
            share = weight_ref[this_round, where, head : head + 1]
            token_grad_ref[where, lanes] = (share * d_mixed_ref[where, lanes].astype(F32)).astype(BF16)
        token_grad_ref[where, width : width + 128] = pack_three(
            d_spread_ref[this_round, where, :], heads
        )
        return carry

    lax.fori_loop(0, tokens // 128, weigh, 0, unroll=4)

    def place(step, carry):
        base = pl.multiple_of(step * place_rows, place_rows)
        hot = one_hot_rows(row_ref[0], base, place_rows, tokens)
        slot_grad_ref[pl.ds(base, place_rows), :] = matmul(
            hot, token_grad_ref[...]
        ).astype(BF16)
        return carry

    lax.fori_loop(0, slots // place_rows, place, 0, unroll=2)

    pairs = slots // PAIR
    batch = at_once(pairs, BACKWARD_PAIRS)

    def finish(start, rows, head, d_query, d_unit, d_value):
        here = aligned(start + SPAN, rows)
        query = placed_ref[0, here, head_lanes[head]].astype(F32)
        scale = lax.rsqrt(jnp.mean(query * query, -1, keepdims=True) + 1e-06)
        inner = jnp.mean(d_unit * query, -1, keepdims=True)
        factor = scale * (1.0 / HEAD_DIM)
        d_query = d_query + factor * d_unit - query * (factor * scale * scale * inner)
        d_place_ref[here, head_lanes[head]] = d_query.astype(BF16)
        d_place_ref[here, width + head * HEAD_DIM : width + (head + 1) * HEAD_DIM] = d_value.astype(BF16)

    def attend(step, carry):
        chains = [(step * batch + part, head) for part in range(batch) for head in range(heads)]
        bias, pair_row = own_bias_ref[...], pair_row_ref[...]
        d_spread_rows = []
        for part in range(batch):
            packed = slot_grad_ref[aligned((step * batch + part) * PAIR, PAIR), width : width + 128]
            rows = jnp.transpose(packed.astype(F32))
            d_spread_rows += [
                rows[head : head + 1]
                + rows[heads + head : heads + head + 1]
                + rows[2 * heads + head : 2 * heads + head + 1]
                for head in range(heads)
            ]
        scores, d_probs = [], []
        for pair, head in chains:
            query = placed_ref[0, aligned(pair * PAIR + SPAN, PAIR), head_lanes[head]]
            keys = placed_ref[0, aligned(pair * PAIR, WINDOW), 2 * width + head * HEAD_DIM : 2 * width + (head + 1) * HEAD_DIM]
            values = placed_ref[0, aligned(pair * PAIR, WINDOW), width + head * HEAD_DIM : width + (head + 1) * HEAD_DIM]
            left = jnp.concatenate([keys, key_bias_ref[0, pair]], 1)
            right = jnp.concatenate([flipped(query), pair_row], 0)
            scores.append(matmul(left, right) + bias)
            d_out = slot_grad_ref[aligned(pair * PAIR, PAIR), head_lanes[head]]
            d_probs.append(matmul(values, flipped(d_out)))
        probs = [
            jnp.exp(score - slot_spread_ref[0, pair, head : head + 1, :])
            for (pair, head), score in zip(chains, scores)
        ]
        dots = [jnp.sum(p * d, 0, keepdims=True) for p, d in zip(probs, d_probs)]
        d_scores = [
            p * (d + (row - dot)) for p, d, row, dot in zip(probs, d_probs, d_spread_rows, dots)
        ]
        last = list(carry)
        for (pair, head), p, d in zip(chains, probs, d_scores):
            query = placed_ref[0, aligned(pair * PAIR + SPAN, PAIR), head_lanes[head]]
            keys = placed_ref[0, aligned(pair * PAIR, WINDOW), 2 * width + head * HEAD_DIM : 2 * width + (head + 1) * HEAD_DIM]
            d_out = slot_grad_ref[aligned(pair * PAIR, PAIR), head_lanes[head]]
            d_query = matmul(jnp.transpose(d).astype(BF16), keys)
            d_keys = matmul(d.astype(BF16), query)
            d_values = matmul(p.astype(BF16), d_out)
            last_query, last_key, last_value = last[head]

            before = pair * PAIR - SPAN
            finish(before, SPAN, head, last_query, last_key + d_keys[:SPAN], last_value + d_values[:SPAN])
            finish(pair * PAIR, SPAN, head, d_query[:SPAN], d_keys[SPAN:PAIR], d_values[SPAN:PAIR])
            last[head] = (d_query[SPAN:], d_keys[PAIR:], d_values[PAIR:])
        return tuple(last)

    blank = jnp.zeros((SPAN, HEAD_DIM), F32)
    carry = lax.fori_loop(
        0, pairs // batch, attend, tuple((blank, blank, blank) for _ in range(heads))
    )
    for head in range(heads):
        finish(slots - SPAN, SPAN, head, *carry[head])

    def read_back(step, carry):
        where = pl.ds(pl.multiple_of(step * token_rows, token_rows), token_rows)
        hot = one_hot_columns(column_ref[0, where, :], token_rows, slots)
        sum_ref[where, :] += matmul(hot, d_place_ref[SPAN:, :])
        return carry

    lax.fori_loop(0, tokens // token_rows, read_back, 0, unroll=2)

    if mixing:

        @pl.when(this_round == rounds - 1)
        def _():
            total_ref[...] = sum_ref[...].astype(BF16)


def per_round(shape, buffers):
    rest = (0,) * (len(shape) - 1)
    return pl.BlockSpec((1,) + shape[1:], lambda r: (r,) + rest, pipeline_mode=pl.Buffered(buffers))


def whole(shape):
    return pl.BlockSpec(shape, lambda r: (0,) * len(shape), pipeline_mode=pl.Buffered(1))


def attention_forward(qv, places, key_bias, mixing):
    row, column = places
    rounds, _, tokens = row.shape
    slots = key_bias.shape[1] * PAIR
    width = qv.shape[1] // 2
    heads = width // HEAD_DIM
    buffers = min(2, rounds)
    bias, pair_row = own_bias(), pair_rows()
    kept = [
        jax.ShapeDtypeStruct((rounds, tokens, width), BF16),
        jax.ShapeDtypeStruct((rounds, tokens, 128), F32),
        jax.ShapeDtypeStruct((tokens if mixing else 8, width), BF16),
    ]
    outs = [
        jax.ShapeDtypeStruct((rounds, slots + SPAN, 3 * width), BF16),
        jax.ShapeDtypeStruct((rounds, slots // PAIR, 8, PAIR), F32),
    ]
    flops = rounds * slots * (2 * tokens * (3 * width + 128) + 4 * width * WINDOW)
    return pl.pallas_call(
        functools.partial(forward_kernel, heads, mixing),
        grid=(rounds,),
        in_specs=[whole(qv.shape)]
        + [per_round(x.shape, buffers) for x in (row, column, key_bias)]
        + [whole(bias.shape), whole(pair_row.shape)],
        out_specs=[whole(x.shape) for x in kept] + [per_round(x.shape, buffers) for x in outs],
        out_shape=kept + outs,
        scratch_shapes=[pltpu.VMEM((slots, width + 128), BF16)],
        compiler_params=pltpu.CompilerParams(vmem_limit_bytes=56 * 1024 * 1024),
        cost_estimate=pl.CostEstimate(flops=flops, bytes_accessed=20 << 20, transcendentals=0),
    )(qv, row, column, key_bias, bias, pair_row)


def attention_backward(d_mixed, round_out, weights, all_dot, placed, slot_spread, places, key_bias):
    row, column = places
    rounds, _, tokens = row.shape
    slots = placed.shape[1] - SPAN
    width = placed.shape[2] // 3
    heads = width // HEAD_DIM
    buffers = min(2, rounds)
    bias, pair_row = own_bias(), pair_rows()
    mixing = all_dot is None
    if mixing:
        all_dot = jnp.zeros((8, 128), F32)
    flops = rounds * slots * (2 * tokens * (3 * width + 128) + 10 * width * WINDOW)
    return pl.pallas_call(
        functools.partial(backward_kernel, heads, mixing),
        grid=(rounds,),
        in_specs=[whole(x.shape) for x in (d_mixed, round_out, weights, all_dot)]
        + [per_round(x.shape, buffers) for x in (placed, slot_spread, row, column, key_bias)]
        + [whole(bias.shape), whole(pair_row.shape)],
        out_specs=whole((tokens, 2 * width)),
        out_shape=jax.ShapeDtypeStruct((tokens, 2 * width), BF16 if mixing else F32),
        scratch_shapes=[
            pltpu.VMEM((rounds, tokens, 128), F32),
            pltpu.VMEM((tokens, width + 128), BF16),
            pltpu.VMEM((slots, width + 128), BF16),
            pltpu.VMEM((slots + SPAN, 2 * width), BF16),
            pltpu.VMEM((tokens if mixing else 8, 2 * width), F32),
        ],
        compiler_params=pltpu.CompilerParams(vmem_limit_bytes=60 * 1024 * 1024),
        cost_estimate=pl.CostEstimate(flops=flops, bytes_accessed=20 << 20, transcendentals=0),
    )(d_mixed, round_out, weights, all_dot, placed, slot_spread, row, column, key_bias, bias, pair_row)


def local(
    stream_one,
    stream_two,
    slot_place,
    bucket_ids,
    grad_one,
    grad_two,
    norm1_gain,
    norm1_bias,
    w_query_key,
    w_value,
    w_output,
    norm2_gain,
    norm2_bias,
    w_inner,
    inner_bias,
    w_outer,
    outer_bias,
):
    chips, devices = lax.axis_size("chip"), lax.axis_size("seq")
    batch, tok, features = stream_one.shape
    rounds = slot_place.shape[1]
    sequences = 2 * batch
    tokens = devices * tok
    slots = 3 * tokens // 2
    own_rows = batch * tok
    width = features // (2 * chips)
    heads = width // HEAD_DIM
    at_call = min(heads, HEADS_AT_CALL)
    hidden_units = w_inner.shape[1]
    quarter = hidden_units // (2 * chips)
    units = sequences * chips
    sharing = devices // units
    mixing = sharing == 1
    own_rounds = rounds // sharing
    shard = w_query_key.shape[0]
    core, chip = lax.axis_index("core"), lax.axis_index("chip")

    def by_core(own, other):
        return jnp.where(core == 0, jnp.stack([own, other]), jnp.stack([other, own]))

    def flip(block):
        return exchange(block, "chip", 1)

    def both_chips(block):
        return ordered(block, flip(block), "chip", 1) if chips == 2 else block[None]

    def trade_quarters(pieces):
        if chips == 2:
            kept, sent = pick(pieces, chip, 0), pick(pieces, 1 - chip, 0)
            pieces = ordered(kept, flip(sent), "chip", 1)
        return jnp.swapaxes(by_core(pick(pieces, core, 1), swap(pick(pieces, 1 - core, 1))), 0, 1)

    seq_steps, chip_steps = half_steps("seq"), half_steps("chip")
    mid_steps = seq_steps[1:-1]
    gather_orders = [
        seq_steps[:1] + seq_steps[-1:] + mid_steps + chip_steps,
        chip_steps + seq_steps[:1] + seq_steps[-1:] + mid_steps,
    ]
    scatter_orders = [
        chip_steps + seq_steps[-1:] + mid_steps + seq_steps[:1],
        seq_steps[-1:] + chip_steps + mid_steps + seq_steps[:1],
    ]

    base = 64
    meta = jnp.stack([slot_place // base, slot_place % base, bucket_ids + 1], 1).astype(BF16)
    vectors = jnp.stack([norm1_gain, norm1_bias, norm2_gain, norm2_bias, outer_bias])
    small_rows = [meta.reshape(-1, tok)] + [
        jnp.pad(part, ((0, 0), (0, tok - part.shape[1]))) for part in (vectors, inner_bias[None])
    ]
    taken = [part.shape[0] for part in small_rows]
    fold = 2 * width // tok
    extra = 8 * (-(-sum(taken) // (8 * fold)))
    small = jnp.concatenate(
        small_rows + [jnp.zeros((extra * fold - sum(taken), tok), BF16)], 0
    )
    small = jnp.concatenate([small[k * extra : (k + 1) * extra] for k in range(fold)], 1)

    key_split = w_query_key.reshape(shard, chips, 2, heads, HEAD_DIM)
    value_split = w_value.reshape(shard, chips, 2, heads, HEAD_DIM)

    def pair_blocks(which):
        keys, values = pick(key_split, which, 2), pick(value_split, which, 2)
        blocks = [
            jnp.concatenate(
                [
                    part[:, pair, head]
                    for first in range(0, heads, at_call)
                    for part in (keys, values)
                    for head in range(first, first + at_call)
                ],
                1,
            )
            for pair in range(chips)
        ]
        return [jnp.concatenate([blocks[0], small], 0)] + blocks[1:]

    sent = jnp.concatenate(pair_blocks(1 - core), 0)
    streams, got = lax.optimization_barrier((stream_two.reshape(own_rows, features), swap(sent)))
    got = [got[: shard + extra]] + [
        got[extra + pair * shard : extra + (pair + 1) * shard] for pair in range(1, chips)
    ]
    chains = [Gather(by_core(own, other)) for own, other in zip(pair_blocks(core), got)]
    for k in range(len(seq_steps) + len(chip_steps)):
        for pair, chain in enumerate(chains):
            chain.step(gather_orders[pair % 2][k])
        together(chains)
    small = chains[0].held.reshape(-1, shard + extra, 2 * width)[:, shard:]
    small = jnp.concatenate([small[:, :, k * tok : (k + 1) * tok] for k in range(fold)], 1)
    joined = [chains[0].held.reshape(-1, shard + extra, 2 * width)[:, :shard]]
    joined = [part.reshape(features, 2 * width) for part in joined + [c.held for c in chains[1:]]]
    cuts = [taken[0], taken[0] + taken[1]]
    vectors = jnp.moveaxis(small[:, cuts[0] : cuts[1], :shard], 1, 0).reshape(taken[1], features)
    vectors = vectors.astype(F32)
    gain_one, bias_one, gain_two, bias_two, full_outer_bias = [vectors[k] for k in range(5)]
    by_place = small.reshape(chips, 2, devices, -1, tok)
    quarter_bias = lax.dynamic_slice(
        by_place, (chip, core, 0, cuts[1], 0), (1, 1, devices, 1, inner_bias.shape[0])
    )
    quarter_bias = quarter_bias.reshape(-1).astype(F32)
    meta = pick(by_place, chip, 0)[:, :, : cuts[0]]
    meta = jnp.swapaxes(meta, 0, 1).reshape(devices, 2, batch, 3, rounds, tok)

    inner_pieces = jnp.moveaxis(w_inner.reshape(shard, chips, 2, quarter), 0, 2)
    inner_pieces = trade_quarters(inner_pieces).reshape(-1, features)
    bundle = jnp.concatenate([w_outer, inner_pieces], 0)
    bundle, *joined = lax.optimization_barrier([bundle] + joined)
    grad_rows = w_outer.shape[0]
    cuts = [grad_rows, grad_rows + inner_pieces.shape[0]]
    gathered = lax.all_gather(bundle, "seq", axis=0, tiled=False)
    full_outer = gathered[:, : cuts[0]].reshape(quarter, features)
    full_inner = gathered[:, cuts[0] : cuts[1]].reshape(devices, 2 * chips, shard, quarter)
    full_inner = jnp.swapaxes(full_inner, 0, 1).reshape(features, quarter)

    unit = lax.axis_index("seq") // sharing
    sequence = unit // chips
    owner = jnp.where(sequence < batch, core, 1 - core)
    meta = lax.dynamic_slice(
        meta,
        (0, owner, sequence % batch, 0, lax.axis_index("seq") % sharing * own_rounds, 0),
        (devices, 1, 1, 3, own_rounds, tok),
    )
    meta = jnp.moveaxis(meta.reshape(devices, 3, own_rounds, tok), 0, 2)
    meta = meta.reshape(3, own_rounds, tokens).astype(jnp.int32)
    token_place, token_tag = meta[0] * base + meta[1], meta[2]
    found = token_place[:, :, None] == jnp.arange(slots)[None, None, :]
    slot_tag = jnp.sum(jnp.where(found, token_tag[:, :, None], 0), 1)
    slot_tag = jnp.pad(slot_tag.reshape(own_rounds, slots // SPAN, SPAN), ((0, 0), (1, 0), (0, 0)))
    span_tag = jnp.max(slot_tag, 2, keepdims=True)
    first, second, third = slot_tag[:, :-2:2], slot_tag[:, 1:-1:2], slot_tag[:, 2::2]
    unmet = jnp.full(first.shape, False)
    met = jnp.stack(
        [
            jnp.concatenate([first == span_tag[:, 1:-1:2], second == span_tag[:, 1:-1:2], unmet], 2),
            jnp.concatenate([unmet, second == span_tag[:, 2::2], third == span_tag[:, 2::2]], 2),
        ],
        3,
    )
    key_bias = jnp.where(met, 0.0, -1e9).astype(BF16)
    key_bias = jnp.pad(key_bias, ((0, 0), (0, 0), (0, 0), (0, HEAD_DIM - 2)))
    places = (token_place[:, None, :], token_place[:, :, None])

    def near(value):
        return jnp.concatenate([value, swap(value)], 0)

    def far(value):
        return near(flip(value))

    def everywhere(value):
        return jnp.concatenate([near(value), far(value)], 0) if chips == 2 else near(value)

    stream_a = stream_one.astype(F32).reshape(own_rows, features)
    stream_b = streams.astype(F32)
    normed_one, unit_one, scale_one = norm_parts(near(streams).astype(F32), gain_one, bias_one)
    hidden = normed_one.astype(BF16)
    unit_one, scale_one = unit_one[:own_rows], scale_one[:own_rows]
    projected = [matmul(hidden, weight).astype(BF16) for weight in joined]

    def to_attention(pairs):
        value = jnp.stack([pair.reshape(sequences, tok, -1) for pair in pairs], 1)
        value = jnp.broadcast_to(value[:, :, None], value.shape[:2] + (sharing,) + value.shape[2:])
        return all_to_all(value.reshape(devices, tok, -1)).reshape(tokens, -1)

    def from_attention(value):
        value = all_to_all(value.reshape(devices, tok, -1))
        value = value.reshape(sequences, chips, sharing, tok, -1)
        return [value[:, pair, 0].reshape(sequences * tok, -1) for pair in range(chips)]

    def by_heads(pairs, size):
        arrived = []
        for call in range(heads // at_call):
            parts = [pair[:, call * size : (call + 1) * size] for pair in pairs]
            if arrived:
                parts, arrived[-1] = lax.optimization_barrier((parts, arrived[-1]))
            arrived.append(to_attention(parts))
        return arrived

    def join_heads(parts):
        return [jnp.concatenate([part[pair] for part in parts], 1) for pair in range(chips)]

    late_output, *projected = lax.optimization_barrier([w_output] + projected)
    output_weights = Gather(late_output, whole_core=False)
    arrived = by_heads(projected, 2 * at_call * HEAD_DIM)
    for step in seq_steps[:1] + seq_steps[-1:] + mid_steps:
        output_weights.step(step)
    output_weights.held, arrived[0] = lax.optimization_barrier((output_weights.held, arrived[0]))
    for step in chip_steps:
        output_weights.step(step)
    full_output = output_weights.held.reshape(chips * width, features)
    kept, mixed = [], []
    for qv in arrived:
        round_out, weights, head_mixed, placed, slot_spread = attention_forward(
            qv, places, key_bias, mixing
        )
        if not mixing:
            top = group_max(jnp.max(weights, 0), sharing)
            weights = jnp.exp(weights - top)
            weights = weights / group_sum(jnp.sum(weights, 0), sharing)
            by_head = round_out.reshape(own_rounds, tokens, at_call, HEAD_DIM)
            head_mixed = group_sum(jnp.sum(weights[:, :, :at_call, None] * by_head, 0), sharing)
            head_mixed = head_mixed.reshape(tokens, -1).astype(BF16)
        kept.append((round_out, weights, placed, slot_spread))
        mixed.append(from_attention(head_mixed))
    mixed = jnp.concatenate(join_heads(mixed), 1)
    cot_own = grad_two.reshape(own_rows, features)
    parts_cot = [near(cot_own)] + ([far(cot_own)] if chips == 2 else [])
    mixed, parts_cot, full_inner, full_outer = lax.optimization_barrier(
        (mixed, parts_cot, full_inner, full_outer)
    )

    def core_sum(value):
        return value[:own_rows] + swap(value[own_rows:])

    out_one = stream_a + core_sum(matmul(mixed, full_output))
    normed_two, unit_two, scale_two = norm_parts(out_one, gain_two, bias_two)
    inner_low = normed_two.astype(BF16)

    def feed_forward(value, cotangent):
        pre_act = matmul(value, full_inner) + quarter_bias
        activated, gelu_pull = jax.vjp(jax.nn.gelu, pre_act)
        act_low = activated.astype(BF16)
        d_act = matmul_right(cotangent, full_outer)
        d_pre = gelu_pull(d_act)[0].astype(BF16)
        return act_low, d_pre, matmul(act_low, full_outer), matmul_right(d_pre, full_inner)

    parts = [(near(inner_low), parts_cot[0])]
    done = [feed_forward(*parts[0])]
    if chips == 2:
        crossed, done[0] = lax.optimization_barrier((flip(inner_low), done[0]))
        parts.append((near(crossed), parts_cot[1]))
        done.append(feed_forward(*parts[1]))
    rows_in, rows_cot = [jnp.concatenate([part[k] for part in parts], 0) for k in range(2)]
    act_low, d_pre = [jnp.concatenate([part[k] for part in done], 0) for k in range(2)]

    grad_outer = matmul_left(act_low, rows_cot).astype(BF16)
    grad_inner = matmul_left(rows_in, d_pre).astype(BF16)
    grad_inner = jnp.swapaxes(grad_inner.reshape(2 * chips, devices, shard, quarter), 0, 1)
    summed = jnp.concatenate(
        [grad_outer.reshape(devices, -1, features), grad_inner.reshape(devices, -1, features)], 1
    )

    def quarter_sum(values):
        total = core_sum(values[0])
        if chips == 2:
            total = total + flip(core_sum(values[1]).astype(BF16)).astype(F32)
        return total

    d_normed_two = core_sum(done[0][3])
    if chips == 2:
        crossed, summed = lax.optimization_barrier((flip(core_sum(done[1][3]).astype(BF16)), summed))
        d_normed_two = d_normed_two + crossed.astype(F32)
    d_from_two, grad_gain_two, grad_bias_two = norm_back(
        d_normed_two, unit_two, scale_two, gain_two
    )
    back_one = grad_one.astype(F32).reshape(own_rows, features) + d_from_two
    out_two = stream_b + quarter_sum([part[2] for part in done]) + full_outer_bias

    d_attended = near(back_one.astype(BF16))
    d_mixed = matmul_right(d_attended, full_output).astype(BF16)
    d_mixed = by_heads([d_mixed[:, p * width : (p + 1) * width] for p in range(chips)], at_call * HEAD_DIM)

    reduced = Held(lax.psum_scatter(summed, "seq", scatter_dimension=0, tiled=True)[0])

    grad_output = Scatter(matmul_left(mixed, d_attended), whole_core=False)
    output_steps = scatter_orders[0][:]

    def beside(value, count):
        for _ in range(count):
            grad_output.step(output_steps.pop(0))
        grad_output.held, value = lax.optimization_barrier((grad_output.held, value))
        return value

    d_mixed[0] = beside(d_mixed[0], len(chip_steps))
    quarter_bias_grad = jnp.sum(d_pre.astype(F32), 0).reshape(devices, -1)

    d_projected = []
    for call, (round_out, weights, placed, slot_spread) in enumerate(kept):
        all_dot = None
        if not mixing:
            inner = d_mixed[call].astype(F32) * round_out.astype(F32)
            inner = jnp.sum(inner.reshape(own_rounds, tokens, at_call, HEAD_DIM), -1)
            inner = group_sum(jnp.sum(weights[:, :, :at_call] * inner, 0), sharing)
            all_dot = jnp.pad(inner, ((0, 0), (0, 128 - at_call)))
        d_total = attention_backward(
            d_mixed[call], round_out, weights, all_dot, placed, slot_spread, places, key_bias
        )
        d_total = beside(d_total, 1)
        if not mixing:
            d_total = group_sum(d_total, sharing).astype(BF16)
        d_projected.append(beside(from_attention(d_total), len(mid_steps)))
    d_projected = join_heads(d_projected)

    chains = []
    for pair in range(chips):
        grad = matmul_left(hidden, d_projected[pair])
        chains.append(Scatter(grad.reshape(chips, 2, devices, shard, 2 * width)))
    orders = list(zip(*[scatter_orders[pair % 2] for pair in range(chips)]))
    for chain, step in zip(chains, orders[0]):
        chain.step(step)
    d_hidden = core_sum(
        functools.reduce(jnp.add, [matmul_right(d, w) for d, w in zip(d_projected, joined)])
    )
    d_from_one, grad_gain_one, grad_bias_one = norm_back(d_hidden, unit_one, scale_one, gain_one)
    back_two = cot_own.astype(F32) + d_from_one
    small_grads = jnp.stack(
        [grad_gain_one, grad_bias_one, grad_gain_two, grad_bias_two, jnp.sum(cot_own.astype(F32), 0)]
    )
    small_grads = jnp.swapaxes(small_grads.reshape(5, 2 * chips * devices, shard), 0, 1)
    small_grads = Halve(small_grads.reshape(-1, 5 * shard), F32)
    small_steps = chip_steps + [("core", 1)] + seq_steps
    while output_steps:
        grad_output.step(output_steps.pop(0))
    for k in range(max(len(orders) - 1, len(small_steps))):
        held = [Held(d_from_one), reduced, small_grads] if k == 1 else []
        together(chains + ([grad_output, reduced] if k == 0 else held))
        if k == 1:
            back_two = cot_own.astype(F32) + held[0].held
        if k + 1 < len(orders):
            for chain, step in zip(chains, orders[k + 1]):
                chain.step(step)
        elif k + 1 == len(orders):
            grad_joined = jnp.stack([chain.held for chain in chains], 1)
            grad_joined = by_core(pick(grad_joined, core, 0), swap(pick(grad_joined, 1 - core, 0)))
        if small_steps[k][0] == "seq" and small_grads.held.shape[1] == 5 * shard:
            small_grads.held = jnp.concatenate([small_grads.held, quarter_bias_grad], 1)
        small_grads.step(small_steps[k])
    summed = reduced.held
    grad_outer = summed[: grad_rows].astype(F32)
    grad_inner = trade_quarters(summed[grad_rows:].reshape(chips, 2, shard, quarter))
    grad_inner = jnp.moveaxis(grad_inner, 2, 0).reshape(shard, hidden_units).astype(F32)
    small_grads, grad_inner_bias = (
        small_grads.held[0, : 5 * shard].reshape(5, shard), small_grads.held[0, 5 * shard :]
    )
    grad_joined = grad_joined.reshape(2, chips, shard, heads // at_call, 2, at_call * HEAD_DIM)
    grad_joined = jnp.transpose(grad_joined, (4, 2, 1, 0, 3, 5)).reshape(2, shard, features)
    out_shape = (batch, tok, features)
    return (
        out_one.reshape(out_shape),
        out_two.reshape(out_shape),
        back_one.reshape(out_shape),
        back_two.reshape(out_shape),
        small_grads[0],
        small_grads[1],
        grad_joined[0],
        grad_joined[1],
        grad_output.held,
        small_grads[2],
        small_grads[3],
        grad_inner,
        grad_inner_bias,
        grad_outer,
        small_grads[4],
    )


def solution(mesh):
    split = Mesh(
        mesh.devices.reshape(mesh.shape["dp"] // 2, 2, mesh.shape["seq"]), ("chip", "core", "seq")
    )
    dp = ("chip", "core")
    every = ("chip", "core", "seq")
    stream, meta, vector, matrix = (
        P(dp, "seq", None), P(dp, None, "seq"), P(every), P(every, None)
    )
    return jax.shard_map(
        local,
        mesh=split,
        in_specs=(
            stream, stream, meta, meta, stream, stream,
            vector, vector, matrix, matrix, matrix, vector, vector, matrix, vector, matrix, vector,
        ),
        out_specs=(
            stream, stream, stream, stream,
            vector, vector, matrix, matrix, matrix, vector, vector, matrix, vector, matrix, vector,
        ),
        check_vma=False,
    )
```
